32 devices in a mesh: seq: 2 (over y), rep: 4 (over z), tensor: 4 (over x, core).
Axes of the slice: x: 2, y: 2, z: 4, core: 2. Of those that a mesh axis runs over, the one named last changes fastest.
Arguments:
- key_value_rows: bfloat16 [4, 3072, 8, 256], P('rep', ('seq', 'tensor')), may hold values from -32 to 32
- queries: bfloat16 [4, 64, 64, 128], P('rep', None, 'tensor'), may hold values from -136 to 136
- w_comp: bfloat16 [2048, 512], replicated, may hold values from -0.125 to 0.125
- latent_gain: bfloat16 [512], replicated, may hold values from 0.099609375 to 1.8984375
- w_up: bfloat16 [8, 512, 256], P('tensor'), may hold values from -0.25 to 0.25
- w_out: bfloat16 [8192, 8192], P('tensor', 'seq'), may hold values from -0.0625 to 0.0625
- replica_order: int32 [4], replicated, may hold values from 0 to 3, each once
Outputs:
- decoded: bfloat16 [4, 64, 8192], P('rep', None, 'seq')
The draws below stay inside these ranges and needn't reach their ends.
Inputs may be any that keep to these rules, and one draw needn't show every extreme that they name: replica_order is a permutation of the prompts.
All inputs are finite; a program needn't handle non-finite values.
Results may differ from the reference program's by a relative error of at most 0.01.
Values may be sent and summed in bfloat16 or wider, within the bound.
No kernel may reach another device: no remote copies, remote signals or barrier semaphores. Data moves between devices by JAX's collectives and lax.ppermute only.
A program may use at most 64 MiB of HBM per device.

```python
import math
import jax
import jax.numpy as jnp
from jax import lax

D = 8192
HEADS = 64
GROUPS = 8
HD = 128
LAT = 512
NEW = 64
PROMPTS = 4
TOKENS = 3072


def scaled_rows(key, base):
    k_row, k_col = jax.random.split(key, 2)
    shape = base.shape
    row_scale = jnp.exp(jax.random.uniform(k_row, shape[:3] + (1,), jnp.float32, 0.0, math.log(10.0)))
    col_scale = jnp.exp(jax.random.uniform(k_col, (1, 1) + shape[2:], jnp.float32, 0.0, math.log(10.0)))
    return jnp.clip(base * row_scale * col_scale / 10.0, -32.0, 32.0)


def draw_key_value_rows(key, part):
    key = jax.random.fold_in(key, 11)
    k_base = jax.random.fold_in(key, 0)
    k_scale = jax.random.fold_in(key, 2)
    shape = (PROMPTS, TOKENS, GROUPS, 2 * HD)
    base = jax.random.normal(k_base, shape, jnp.float32)
    return scaled_rows(k_scale, base).astype(jnp.bfloat16)


def draw_queries(key, part):
    key = jax.random.fold_in(key, 23)
    k_base = jax.random.fold_in(key, 0)
    shape = (PROMPTS, NEW, HEADS, HD)
    base = jax.random.normal(k_base, shape, jnp.float32)
    return base.astype(jnp.bfloat16)


def shard_levels(rng, shape, cuts, least, top_value):
    loudness = 1.0
    for dim, parts in cuts:
        draws = jax.random.uniform(jax.random.fold_in(jax.random.fold_in(rng, 6), dim), (parts,), jnp.float32, least / len(cuts), top_value / len(cuts))
        loudness = loudness * jnp.repeat(jnp.exp(draws), shape[dim] // parts).reshape((-1,) + (1,) * (len(shape) - 1 - dim))
    return loudness


def scatter_about(key, extent, width, most, cuts=(), held_as=jnp.bfloat16):
    values = jax.random.normal(key, extent, jnp.float32) * width
    if len(cuts) > 0:
        values = shard_levels(key, extent, cuts, -0.22, 0.18) * values
    return jnp.clip(values, min=-most, max=most).astype(held_as)


def setup_inputs(seed: int = 0) -> dict:
    seeds = jax.random.split(jax.random.key(seed), 8)
    return {
        "key_value_rows": draw_key_value_rows(jax.random.fold_in(seeds[7], 71), 0),
        "queries": draw_queries(jax.random.fold_in(seeds[7], 71), 0),
        "w_comp": scatter_about(seeds[2], (GROUPS * 2 * HD, LAT), (GROUPS * 2 * HD) ** -0.5, 0.125),
        "latent_gain": jnp.clip(1.0 + 0.18 * jax.random.normal(seeds[3], (LAT,), jnp.float32), 0.099609375, 1.8984375).astype(jnp.bfloat16),
        "w_up": scatter_about(seeds[4], (GROUPS, LAT, 2 * HD), LAT ** -0.5, 0.25, ((0, 4),)),
        "w_out": scatter_about(seeds[5], (HEADS * HD, D), (HEADS * HD) ** -0.5, 0.0625, ((0, 4), (1, 2))),
        "replica_order": jax.random.permutation(seeds[6], PROMPTS).astype(jnp.int32),
    }


def compress(rows, weight, gain):
    projected = jnp.dot(rows, weight, preferred_element_type=jnp.float32)
    scale = lax.rsqrt(lax.optimization_barrier(jnp.mean(projected * projected, axis=-1, keepdims=True)) + 1e-06)
    return (projected * scale * gain.astype(jnp.float32)).astype(jnp.bfloat16)

def attend_group(latent_state, operands):
    query, lift = operands
    lifted = jnp.dot(latent_state, lift, preferred_element_type=jnp.float32).astype(jnp.bfloat16)
    head_size = query.shape[-1]
    keys = lifted[:, :head_size]
    values = lifted[:, head_size:]
    scores = jnp.einsum('nhd,td->nht', query.astype(jnp.float32), keys.astype(jnp.float32)) * head_size ** (-0.5)
    top = lax.optimization_barrier(jnp.max(scores, axis=-1, keepdims=True))
    expo = jnp.exp(scores - top)
    total = lax.optimization_barrier(jnp.sum(expo, axis=-1))
    weights = lax.optimization_barrier(expo.astype(jnp.bfloat16))
    summed = jnp.einsum('nht,td->nhd', weights.astype(jnp.float32), values.astype(jnp.float32))
    return (summed / total[..., None]).astype(jnp.bfloat16)

def reference(key_value_rows, queries, w_comp, latent_gain, w_up, w_out, replica_order):
    groups = w_up.shape[0]
    new_count = queries.shape[1]
    heads = queries.shape[2]
    head_size = queries.shape[3]
    outputs = []
    for replica in range(queries.shape[0]):
        prompt = replica_order[replica]
        rows = key_value_rows[prompt]
        rows = rows.reshape(rows.shape[0], -1)
        latent_state = compress(rows, w_comp, latent_gain)
        query = queries[replica].reshape(new_count, groups, heads // groups, head_size)
        query = jnp.moveaxis(query, 1, 0)
        attended_values = lax.map(partial_group(latent_state), (query, w_up))
        attended_values = jnp.moveaxis(attended_values, 0, 1).reshape(new_count, heads * head_size)
        outputs.append(jnp.dot(attended_values, w_out, preferred_element_type=jnp.float32).astype(jnp.bfloat16))
    return jnp.stack(outputs)

def partial_group(latent_state):

    def inner(operands):
        return attend_group(latent_state, operands)
    return inner
```

```python
import itertools
import math

import jax
import jax.numpy as jnp
from jax import lax
from jax.experimental import pallas as pl
from jax.experimental.pallas import tpu as pltpu
from jax.sharding import PartitionSpec as P

BF16, F32 = jnp.bfloat16, jnp.float32
VMEM_BYTES = 48 * 1024 * 1024
IN_VMEM = pl.BlockSpec(memory_space=pltpu.VMEM)
IN_SMEM = pl.BlockSpec(memory_space=pltpu.SMEM)


def params():
    return pltpu.CompilerParams(vmem_limit_bytes=VMEM_BYTES)


def compress(rows, weight, gain):
    projected = jnp.dot(rows, weight, preferred_element_type=F32)
    scale = lax.rsqrt(jnp.mean(projected * projected, axis=-1, keepdims=True) + 1e-06)
    return (projected * scale * gain.astype(F32)[None]).astype(BF16)


def order_index(replica_order, orders):
    table = jnp.array(orders, jnp.int32)
    match = jnp.all(table == replica_order[None], axis=1)
    return jnp.sum(jnp.where(match, lax.iota(jnp.int32, len(orders)), 0))


def route(value, index, orders, back):
    def branch(order):
        pairs = [(p, r) if back else (r, p) for r, p in enumerate(order)]
        return lambda v: lax.ppermute(v, "rep", pairs)

    return lax.switch(index, [branch(o) for o in orders], value)


def swap(value, axis, bit):
    pairs = [(i, i ^ bit) for i in range(lax.axis_size(axis))]
    return lax.ppermute(value, axis, pairs)


def attend(latents, lift, query):
    head_size = query.shape[-1]
    coef = head_size ** (-0.5) * math.log2(math.e)
    scores, values = [], []
    for latent in latents:
        lifted = jnp.dot(latent, lift, preferred_element_type=F32).astype(BF16)
        scores.append(
            lax.dot_general(
                lifted[:, :head_size], query, (((1,), (1,)), ((), ())), preferred_element_type=F32
            )
        )
        values.append(lifted[:, head_size:])
    top = jnp.max(scores[0], axis=0, keepdims=True)
    for score in scores[1:]:
        top = jnp.maximum(top, jnp.max(score, axis=0, keepdims=True))
    total, summed = 0.0, 0.0
    for score, value in zip(scores, values):
        expo = jnp.exp2((score - top) * coef)
        total = total + jnp.sum(expo, axis=0, keepdims=True)
        summed = summed + lax.dot_general(
            value, expo.astype(BF16), (((0,), (0,)), ((), ())), preferred_element_type=F32
        )
    return summed, top, total


def merge(one, two, head_size):
    coef = head_size ** (-0.5) * math.log2(math.e)
    top = jnp.maximum(one[1], two[1])
    scale_one = jnp.exp2((one[1] - top) * coef)
    scale_two = jnp.exp2((two[1] - top) * coef)
    return (
        one[0] * scale_one + two[0] * scale_two,
        top,
        one[2] * scale_one + two[2] * scale_two,
    )


def unpack(state, head_size):
    return state[:head_size], state[head_size : head_size + 1], state[head_size + 4 : head_size + 5]


def store(ref, state, head_size):
    columns = state[0].shape[1]
    ref[:head_size, :] = state[0]
    ref[head_size : head_size + 4, :] = jnp.broadcast_to(state[1], (4, columns))
    ref[head_size + 4 :, :] = jnp.broadcast_to(state[2], (4, columns))


def first_kernel(place_ref, lat_a, lat_b, lift_ref, query_ref, out_ref):
    head_size = query_ref.shape[-1]
    mine = place_ref[0]
    for slot, group in enumerate((1 - mine, mine)):
        state = attend((lat_a[...], lat_b[...]), lift_ref[group], query_ref[group])
        store(out_ref.at[slot], state, head_size)


def later_kernel(slot, place_ref, lat_a, lat_b, lift_ref, query_ref, before_ref, out_ref):
    head_size = query_ref.shape[-1]
    mine = place_ref[0]
    group = mine if slot else 1 - mine
    state = attend((lat_a[...], lat_b[...]), lift_ref[group], query_ref[group])
    store(out_ref, merge(unpack(before_ref[slot], head_size), state, head_size), head_size)


def finish_kernel(new_count, mine_ref, other_ref, out_ref):
    head_size = mine_ref.shape[0] - 8
    summed, _, total = merge(
        unpack(mine_ref[...], head_size), unpack(other_ref[...], head_size), head_size
    )
    rows = (summed / total).T.astype(out_ref.dtype)
    for head in range(rows.shape[0] // new_count):
        out_ref[:, head * head_size : (head + 1) * head_size] = rows[
            head * new_count : (head + 1) * new_count
        ]


def project_kernel(place_ref, rows_ref, weight_ref, out_ref):
    out_ref[...] = jnp.dot(rows_ref[...], weight_ref[...], preferred_element_type=F32)


def project_more_kernel(place_ref, rows_ref, weight_ref, before_ref, out_ref):
    out_ref[...] = before_ref[...] + jnp.dot(
        rows_ref[...], weight_ref[...], preferred_element_type=F32
    )


def project(place, rows, weight, tile=512):
    new_count, depth = rows.shape
    columns = weight.shape[1]
    return pl.pallas_call(
        project_kernel,
        out_shape=jax.ShapeDtypeStruct((new_count, columns), F32),
        grid_spec=pltpu.PrefetchScalarGridSpec(
            num_scalar_prefetch=1,
            grid=(columns // tile,),
            in_specs=[
                pl.BlockSpec((new_count, depth), lambda j, p: (0, 0)),
                pl.BlockSpec((depth, tile), lambda j, p: (p[0], j)),
            ],
            out_specs=pl.BlockSpec((new_count, tile), lambda j, p: (0, j)),
        ),
        compiler_params=params(),
        cost_estimate=pl.CostEstimate(
            flops=2 * new_count * depth * columns, bytes_accessed=2 * depth * columns, transcendentals=0
        ),
        name="project",
    )(place, rows, weight)


def project_more(place, rows, weight, before, own, tile=512):
    new_count, depth = rows.shape
    columns = weight.shape[1] // 2
    tiles = columns // tile

    def half(p):
        return p[1] if own else 1 - p[1]

    return pl.pallas_call(
        project_more_kernel,
        out_shape=jax.ShapeDtypeStruct((new_count, columns), F32),
        grid_spec=pltpu.PrefetchScalarGridSpec(
            num_scalar_prefetch=1,
            grid=(tiles,),
            in_specs=[
                pl.BlockSpec((new_count, depth), lambda j, p: (0, 0)),
                pl.BlockSpec((depth, tile), lambda j, p: (1 - p[0], half(p) * tiles + j)),
                pl.BlockSpec((new_count, tile), lambda j, p: (0, half(p) * tiles + j)),
            ],
            out_specs=pl.BlockSpec((new_count, tile), lambda j, p: (0, j)),
        ),
        compiler_params=params(),
        cost_estimate=pl.CostEstimate(
            flops=2 * new_count * depth * columns, bytes_accessed=2 * depth * columns, transcendentals=0
        ),
        name="project_own" if own else "project_sent",
    )(place, rows, weight, before)


def attend_cost(tokens, groups, lift, rows, head_size):
    flops = 2 * tokens * groups * (lift[0] * lift[1] + 2 * rows * head_size)
    return pl.CostEstimate(
        flops=flops, bytes_accessed=2 * tokens * lift[0], transcendentals=tokens * groups * rows
    )


def pair_shards(key_value_rows, queries, w_comp, latent_gain, w_up, w_out, replica_order):
    orders = list(itertools.permutations(range(lax.axis_size("rep"))))
    index = order_index(replica_order, orders)
    seq_at, tensor_at = lax.axis_index("seq"), lax.axis_index("tensor")
    core_at, chip_at = tensor_at % 2, tensor_at // 2
    place = jnp.stack([seq_at, core_at, chip_at]).astype(jnp.int32)
    _, new_count, heads, head_size = queries.shape
    groups = w_up.shape[0]
    rows = heads // groups * new_count

    query = jnp.swapaxes(queries[0], 0, 1).reshape(groups, rows, head_size)
    query = route(query, index, orders, False)

    tokens = key_value_rows.shape[1]
    latent = compress(key_value_rows[0].reshape(tokens, -1), w_comp, latent_gain)
    beside = swap(latent, "tensor", 1)
    across = swap(latent, "tensor", 2)
    across_beside = swap(across, "tensor", 1)

    state_shape = (head_size + 8, rows)
    first = pl.pallas_call(
        first_kernel,
        out_shape=jax.ShapeDtypeStruct((groups, *state_shape), F32),
        in_specs=[IN_SMEM] + [IN_VMEM] * 4,
        out_specs=IN_VMEM,
        compiler_params=params(),
        cost_estimate=attend_cost(2 * tokens, groups, w_up.shape[1:], rows, head_size),
        name="attend_chip",
    )(place, latent, beside, w_up, query)

    def later(slot):
        return pl.pallas_call(
            lambda *refs: later_kernel(slot, *refs),
            out_shape=jax.ShapeDtypeStruct(state_shape, F32),
            in_specs=[IN_SMEM] + [IN_VMEM] * 5,
            out_specs=IN_VMEM,
            compiler_params=params(),
            cost_estimate=attend_cost(2 * tokens, 1, w_up.shape[1:], rows, head_size),
            name="attend_own" if slot else "attend_sent",
        )(place, across, across_beside, w_up, query, first)

    other = swap(later(0), "seq", 1)
    mine = later(1)
    attended = pl.pallas_call(
        lambda *refs: finish_kernel(new_count, *refs),
        out_shape=jax.ShapeDtypeStruct((new_count, rows // new_count * head_size), BF16),
        in_specs=[IN_VMEM] * 2,
        out_specs=IN_VMEM,
        compiler_params=params(),
        name="finish",
    )(mine, other)

    attended = route(attended, index, orders, True)
    attended_other = swap(attended, "seq", 1)
    partial = project(place, attended, w_out)
    sent = swap(project_more(place, attended_other, w_out, partial, False), "tensor", 1)
    half = project_more(place, attended_other, w_out, partial, True) + sent
    quarter = half.shape[1] // 2
    low, high = half[:, :quarter], half[:, quarter:]
    upper = chip_at == 1
    arrived = swap(jnp.where(upper, low, high), "tensor", 2)
    summed = (jnp.where(upper, high, low) + arrived).astype(BF16)
    summed_across = swap(summed, "tensor", 2)
    half = jnp.where(
        upper,
        jnp.concatenate([summed_across, summed], axis=1),
        jnp.concatenate([summed, summed_across], axis=1),
    )
    half_beside = swap(half, "tensor", 1)
    whole = jnp.where(
        core_at == 1,
        jnp.concatenate([half_beside, half], axis=1),
        jnp.concatenate([half, half_beside], axis=1),
    )
    return whole[None]


def shards(key_value_rows, queries, w_comp, latent_gain, w_up, w_out, replica_order):
    orders = list(itertools.permutations(range(lax.axis_size("rep"))))
    index = order_index(replica_order, orders)
    query = route(queries[0], index, orders, False)
    rows = key_value_rows[0]
    latent = compress(rows.reshape(rows.shape[0], -1), w_comp, latent_gain)
    latent = lax.all_gather(latent, "tensor", axis=0, tiled=True)
    groups = w_up.shape[0]
    lifted = jnp.einsum("tf,gfy->tgy", latent, w_up, preferred_element_type=F32).astype(BF16)
    head_size = query.shape[-1]
    new_count = query.shape[0]
    keys = lifted[..., :head_size]
    values = lifted[..., head_size:]
    grouped_heads = query.reshape(new_count, groups, -1, head_size)
    scores = jnp.einsum(
        "nghd,tgd->nght", grouped_heads, keys, preferred_element_type=F32
    ) * head_size ** (-0.5)
    top = lax.pmax(jnp.max(scores, axis=-1), "seq")
    expo = jnp.exp(scores - top[..., None])
    total = jnp.sum(expo, axis=-1)
    summed = jnp.einsum("nght,tgd->nghd", expo.astype(BF16), values, preferred_element_type=F32)
    summed, total = lax.psum((summed, total), "seq")
    attended = (summed / total[..., None]).astype(BF16).reshape(new_count, -1)
    attended = route(attended, index, orders, True)
    partial = jnp.dot(attended, w_out, preferred_element_type=F32)
    return lax.psum(partial, "tensor").astype(BF16)[None]


def solution(mesh):
    placed = (
        P("rep", ("seq", "tensor"), None, None),
        P("rep", None, "tensor", None),
        P(),
        P(),
        P("tensor", None, None),
        P("tensor", "seq"),
        P(),
    )
    paired = mesh.shape["seq"] == 2 and mesh.shape["tensor"] == 4
    return jax.shard_map(
        pair_shards if paired else shards,
        mesh=mesh,
        in_specs=placed,
        out_specs=P("rep", None, "seq"),
        check_vma=False,
    )
```

```python
import itertools
import math

import jax
import jax.numpy as jnp
from jax import lax
from jax.experimental import pallas as pl
from jax.experimental.pallas import tpu as pltpu
from jax.sharding import PartitionSpec as P

BF16, F32 = jnp.bfloat16, jnp.float32
MIB = 1024 * 1024
IN_VMEM = pl.BlockSpec(memory_space=pltpu.VMEM)
IN_SMEM = pl.BlockSpec(memory_space=pltpu.SMEM)
ANYWHERE = pl.BlockSpec(memory_space=pl.ANY)
COPIES = 8


def shape(dims, dtype):
    return jax.ShapeDtypeStruct(dims, dtype)


def call(body, name, outs, operands, vmem, scratch=(), smem_in=0, smem_out=False, any_in=0, cost=None):
    specs = [IN_SMEM] * smem_in + [IN_VMEM] * (len(operands) - smem_in - any_in) + [ANYWHERE] * any_in
    out_specs = [IN_VMEM] * len(outs)
    if smem_out:
        out_specs[-1] = IN_SMEM
    return pl.pallas_call(
        body,
        out_shape=outs,
        in_specs=specs,
        out_specs=out_specs,
        scratch_shapes=list(scratch),
        compiler_params=pltpu.CompilerParams(vmem_limit_bytes=vmem * MIB),
        cost_estimate=cost,
        name=name,
    )(*operands)


def cost(flops, moved, exps=0):
    return pl.CostEstimate(flops=int(flops), bytes_accessed=int(moved), transcendentals=int(exps))


def dot(a, b):
    return jnp.dot(a, b, preferred_element_type=F32)


def compress(rows, weight, gain):
    projected = dot(rows, weight)
    scale = lax.rsqrt(jnp.mean(projected * projected, axis=-1, keepdims=True) + 1e-06)
    return (projected * scale * gain.astype(F32)[None]).astype(BF16)


def order_index(replica_order, orders):
    table = jnp.array(orders, jnp.int32)
    match = jnp.all(table == replica_order[None], axis=1)
    return jnp.sum(jnp.where(match, lax.iota(jnp.int32, len(orders)), 0))


def route_pairs(order, back):
    return [(p, r) if back else (r, p) for r, p in enumerate(order)]


def route(value, index, orders, back):
    def branch(order):
        return lambda v: lax.ppermute(v, "rep", route_pairs(order, back))

    return lax.switch(index, [branch(o) for o in orders], value)


def swap(value, axis, bit):
    pairs = [(i, i ^ bit) for i in range(lax.axis_size(axis))]
    return lax.ppermute(value, axis, pairs)


def cross(value, seq_core):
    pairs = [(i, i ^ (4 if i % 2 == seq_core else 2)) for i in range(8)]
    return lax.ppermute(value, ("seq", "tensor"), pairs)


def compress_kernel(order_ref, rows_ref, weight_ref, gain_ref, query_ref, latent_ref, half_ref, index_ref, wide):
    tokens, groups, width = rows_ref.shape
    lanes = wide.shape[2]
    for part in range(wide.shape[0]):
        values = rows_ref[:, :, part * lanes : (part + 1) * lanes].astype(F32)
        wide[part] = values.reshape(tokens * groups, lanes)
    projected = jnp.zeros((tokens, weight_ref.shape[1]), F32)
    for group in range(groups):
        picked = [
            wide[part, pl.ds(group, tokens, stride=groups), :] for part in range(wide.shape[0])
        ]
        picked = jnp.concatenate(picked, axis=1).astype(BF16)
        projected += dot(picked, weight_ref[group * width : (group + 1) * width, :])
    scale = lax.rsqrt(jnp.mean(projected * projected, axis=-1, keepdims=True) + 1e-06)
    latent_ref[...] = (projected * scale * gain_ref[...].astype(F32)).astype(BF16)

    new_count, heads, head_size = query_ref.shape
    query = query_ref[...].astype(F32)
    upper = lax.axis_index("seq") == 1
    query = jnp.where(upper, query[:, heads // 2 :], query[:, : heads // 2])
    half_ref[...] = query.reshape(half_ref.shape).astype(BF16)

    count = order_ref.shape[0]
    index = 0
    for i in range(count):
        smaller = 0
        for j in range(i + 1, count):
            smaller = smaller + (order_ref[j] < order_ref[i]).astype(jnp.int32)
        index = index + smaller * math.factorial(count - 1 - i)
    index_ref[0] = index


def score_kernel(parts, *refs):
    latent_refs, (lift_ref, query_ref), (score_ref, value_ref, top_ref) = (
        refs[:parts],
        refs[parts : parts + 2],
        refs[parts + 2 :],
    )
    head_size = query_ref.shape[-1]
    lift = lift_ref[lax.axis_index("seq")]
    query = query_ref[...]
    top = None
    for part, latent_ref in enumerate(latent_refs):
        tokens = latent_ref.shape[0]
        at = slice(part * tokens, (part + 1) * tokens)
        lifted = dot(latent_ref[...], lift).astype(BF16)
        score = lax.dot_general(
            lifted[:, :head_size], query, (((1,), (1,)), ((), ())), preferred_element_type=F32
        )
        score_ref[at] = score
        value_ref[at] = lifted[:, head_size:]
        part_top = jnp.max(score, axis=0, keepdims=True)
        top = part_top if top is None else jnp.maximum(top, part_top)
    top_ref[...] = jnp.broadcast_to(top, top_ref.shape)


def score_and_fetch_kernel(parts, *refs):
    *refs, held_ref, sems = refs
    weight_ref = refs.pop(parts + 2)
    rows = weight_ref.shape[0] // COPIES
    copies = []
    for i in range(COPIES):
        at = pl.ds(i * rows, rows)
        copies.append(pltpu.make_async_copy(weight_ref.at[at], held_ref.at[at], sems.at[i]))
    for copy in copies:
        copy.start()
    score_kernel(parts, *refs)
    for copy in copies:
        copy.wait()


def score_call(name, latents, lift, query, weight=None):
    tokens = sum(latent.shape[0] for latent in latents)
    rows, head_size = query.shape
    flops = 2 * tokens * (lift.shape[1] * lift.shape[2] + rows * head_size)
    outs = [shape((tokens, rows), F32), shape((tokens, head_size), BF16), shape((8, rows), F32)]
    operands = [*latents, lift, query]
    estimate = cost(flops, 6 * tokens * rows)
    if weight is None:
        body = lambda *refs: score_kernel(len(latents), *refs)
        return call(body, name, outs, operands, 16, cost=estimate)
    return call(
        lambda *refs: score_and_fetch_kernel(len(latents), *refs),
        name,
        [*outs, pltpu.VMEM(weight.shape, weight.dtype)],
        [*operands, weight],
        12,
        scratch=[pltpu.SemaphoreType.DMA((COPIES,))],
        any_in=1,
        cost=cost(flops, 2 * weight.shape[0] * weight.shape[1]),
    )


def attend_kernel(new_count, block, *refs):
    (*score_refs, out_ref, turned) = refs
    triples = [score_refs[i : i + 3] for i in range(0, len(score_refs), 3)]
    head_size = triples[0][1].shape[-1]
    coef = head_size ** (-0.5) * math.log2(math.e)
    top = triples[0][2][:1]
    for triple in triples[1:]:
        top = jnp.maximum(top, triple[2][:1])
    total = jnp.zeros_like(top)
    summed = jnp.zeros((head_size, top.shape[1]), F32)
    for score_ref, value_ref, _ in triples:
        for start in range(0, score_ref.shape[0], block):
            at = slice(start, start + block)
            expo = jnp.exp2((score_ref[at] - top) * coef)
            total += jnp.sum(expo, axis=0, keepdims=True)
            summed += lax.dot_general(
                value_ref[at], expo.astype(BF16), (((0,), (0,)), ((), ())), preferred_element_type=F32
            )
    turned[...] = (summed / total).T
    heads = turned.shape[0] // new_count
    for head in range(heads):
        out_ref[:, head * head_size : (head + 1) * head_size] = turned[
            pl.ds(head, new_count, stride=heads), :
        ].astype(BF16)


def project_kernel(tile, rows_ref, weight_ref, out_ref):
    depth = rows_ref.shape[1]
    start = pl.multiple_of(lax.axis_index("seq") * depth, depth)
    rows = rows_ref[...]
    width = out_ref.shape[2]
    for part in range(out_ref.shape[0]):
        for column in range(0, width, tile):
            at = part * width + column
            out_ref[part, :, column : column + tile] = dot(
                rows, weight_ref[pl.ds(start, depth), at : at + tile]
            )


def project_more_kernel(tile, own, rows_ref, weight_ref, before_ref, *refs):
    out_ref = refs[-1]
    depth = rows_ref.shape[1]
    start = pl.multiple_of((1 - lax.axis_index("seq")) * depth, depth)
    core = lax.axis_index("tensor") % 2
    part = core if own else 1 - core
    rows = rows_ref[...]
    width = out_ref.shape[1]
    for column in range(0, width, tile):
        at = pl.multiple_of(part * width + column, tile)
        value = before_ref[part, :, column : column + tile] + dot(
            rows, weight_ref[pl.ds(start, depth), pl.ds(at, tile)]
        )
        out_ref[:, column : column + tile] = value


def square_shards(key_value_rows, queries, w_comp, latent_gain, w_up, w_out, replica_order):
    orders = list(itertools.permutations(range(lax.axis_size("rep"))))
    tensor_at = lax.axis_index("tensor")
    core_at, chip_at = tensor_at % 2, tensor_at // 2
    _, new_count, heads, head_size = queries.shape
    _, tokens, all_groups, width = key_value_rows.shape
    latent_width = w_comp.shape[1]
    rows = heads // 2 * new_count

    latent, query, index = call(
        compress_kernel,
        "compress",
        [shape((tokens, latent_width), BF16), shape((rows, head_size), BF16), shape((1,), jnp.int32)],
        [replica_order, key_value_rows[0], w_comp, latent_gain[None], queries[0]],
        16,
        scratch=[pltpu.VMEM((width // 128, tokens * all_groups, 128), F32)],
        smem_in=1,
        smem_out=True,
        cost=cost(2 * tokens * all_groups * width * latent_width, 2 * tokens * all_groups * width),
    )

    def branch(order):
        def run(latent, query):
            return (
                cross(latent, 0),
                cross(latent, 1),
                swap(latent, "tensor", 1),
                lax.ppermute(query, "rep", route_pairs(order, False)),
            )

        return run

    near, far, beside, query = lax.switch(index[0], [branch(o) for o in orders], latent, query)
    corner = cross(near, 1)
    near_beside = swap(near, "tensor", 1)
    far_beside = swap(far, "tensor", 1)
    corner_beside = swap(corner, "tensor", 1)
    *first, held = score_call("score_chip", [latent, beside], w_up, query, w_out)
    second = score_call("score_next", [near, near_beside, far, far_beside], w_up, query)
    third = score_call("score_corner", [corner, corner_beside], w_up, query)
    depth = rows // new_count * head_size
    (attended,) = call(
        lambda *refs: attend_kernel(new_count, tokens, *refs),
        "attend",
        [shape((new_count, depth), BF16)],
        [*first, *second, *third],
        16,
        scratch=[pltpu.VMEM((rows, head_size), F32)],
        cost=cost(2 * 8 * tokens * rows * head_size, 8 * tokens * rows * 4, 8 * tokens * rows),
    )

    attended = route(attended, index[0], orders, True)
    attended_other = swap(attended, "seq", 1)
    columns = w_out.shape[1]
    tile = min(512, columns // 2)
    (partial,) = call(
        lambda *refs: project_kernel(tile, *refs),
        "project",
        [shape((2, new_count, columns // 2), F32)],
        [attended, held],
        12,
        cost=cost(2 * new_count * depth * columns, 2 * depth * columns),
    )

    def project_more(own, name):
        return call(
            lambda *refs: project_more_kernel(tile, own, *refs),
            name,
            [shape((new_count, columns // 2), F32)],
            [attended_other, held, partial],
            12,
            cost=cost(new_count * depth * columns, depth * columns),
        )[0]

    sent = swap(project_more(False, "project_sent"), "tensor", 1)
    half = project_more(True, "project_own") + sent
    quarter = half.shape[1] // 2
    low, high = half[:, :quarter], half[:, quarter:]
    upper = chip_at == 1
    arrived = swap(jnp.where(upper, low, high), "tensor", 2)
    summed = (jnp.where(upper, high, low) + arrived).astype(BF16)
    summed_across = swap(summed, "tensor", 2)
    half = jnp.where(
        upper,
        jnp.concatenate([summed_across, summed], axis=1),
        jnp.concatenate([summed, summed_across], axis=1),
    )
    half_beside = swap(half, "tensor", 1)
    whole = jnp.where(
        core_at == 1,
        jnp.concatenate([half_beside, half], axis=1),
        jnp.concatenate([half, half_beside], axis=1),
    )
    return whole[None]


def shards(key_value_rows, queries, w_comp, latent_gain, w_up, w_out, replica_order):
    orders = list(itertools.permutations(range(lax.axis_size("rep"))))
    index = order_index(replica_order, orders)
    query = route(queries[0], index, orders, False)
    rows = key_value_rows[0]
    latent = compress(rows.reshape(rows.shape[0], -1), w_comp, latent_gain)
    latent = lax.all_gather(latent, "tensor", axis=0, tiled=True)
    groups = w_up.shape[0]
    lifted = jnp.einsum("tf,gfy->tgy", latent, w_up, preferred_element_type=F32).astype(BF16)
    head_size = query.shape[-1]
    new_count = query.shape[0]
    keys = lifted[..., :head_size]
    values = lifted[..., head_size:]
    grouped_heads = query.reshape(new_count, groups, -1, head_size)
    scores = jnp.einsum(
        "nghd,tgd->nght", grouped_heads, keys, preferred_element_type=F32
    ) * head_size ** (-0.5)
    top = lax.pmax(jnp.max(scores, axis=-1), "seq")
    expo = jnp.exp(scores - top[..., None])
    total = jnp.sum(expo, axis=-1)
    summed = jnp.einsum("nght,tgd->nghd", expo.astype(BF16), values, preferred_element_type=F32)
    summed, total = lax.psum((summed, total), "seq")
    attended = (summed / total[..., None]).astype(BF16).reshape(new_count, -1)
    attended = route(attended, index, orders, True)
    return lax.psum(dot(attended, w_out), "tensor").astype(BF16)[None]


def solution(mesh):
    placed = (
        P("rep", ("seq", "tensor"), None, None),
        P("rep", None, "tensor", None),
        P(),
        P(),
        P("tensor", None, None),
        P("tensor", "seq"),
        P(),
    )
    square = mesh.shape["seq"] == 2 and mesh.shape["tensor"] == 4
    return jax.shard_map(
        square_shards if square else shards,
        mesh=mesh,
        in_specs=placed,
        out_specs=P("rep", None, "seq"),
        check_vma=False,
    )
```

```python
import itertools
import math

import jax
import jax.numpy as jnp
from jax import lax
from jax.experimental import pallas as pl
from jax.experimental.pallas import tpu as pltpu
from jax.sharding import PartitionSpec as P

BF16, F32 = jnp.bfloat16, jnp.float32
MIB = 1024 * 1024
IN_VMEM = pl.BlockSpec(memory_space=pltpu.VMEM)
IN_SMEM = pl.BlockSpec(memory_space=pltpu.SMEM)
IN_HBM = pl.BlockSpec(memory_space=pltpu.HBM)
COPIES = 8


def shape(dims, dtype):
    return jax.ShapeDtypeStruct(dims, dtype)


def call(body, name, outs, operands, vmem, scratch=(), smem_out=False, hbm_in=0, cost=None):
    kept = len(operands) - hbm_in
    specs = [IN_VMEM] * kept + [IN_HBM] * hbm_in
    operands = [
        *operands[:kept],
        *(pltpu.with_memory_space_constraint(operand, pltpu.HBM) for operand in operands[kept:]),
    ]
    out_specs = [IN_VMEM] * len(outs)
    if smem_out:
        out_specs[-1] = IN_SMEM
    return pl.pallas_call(
        body,
        out_shape=outs,
        in_specs=specs,
        out_specs=out_specs,
        scratch_shapes=list(scratch),
        compiler_params=pltpu.CompilerParams(vmem_limit_bytes=vmem * MIB),
        cost_estimate=cost,
        name=name,
    )(*operands)


def cost(flops, moved, exps=0):
    return pl.CostEstimate(flops=int(flops), bytes_accessed=int(moved), transcendentals=int(exps))


def dot(a, b):
    return jnp.dot(a, b, preferred_element_type=F32)


def compress(rows, weight, gain):
    projected = dot(rows, weight)
    scale = lax.rsqrt(jnp.mean(projected * projected, axis=-1, keepdims=True) + 1e-06)
    return (projected * scale * gain.astype(F32)[None]).astype(BF16)


def order_index(replica_order, orders):
    table = jnp.array(orders, jnp.int32)
    match = jnp.all(table == replica_order[None], axis=1)
    return jnp.sum(jnp.where(match, lax.iota(jnp.int32, len(orders)), 0))


def route_pairs(order, back):
    return [(p, r) if back else (r, p) for r, p in enumerate(order)]


def route(value, index, orders, back):
    def branch(order):
        return lambda v: lax.ppermute(v, "rep", route_pairs(order, back))

    return lax.switch(index, [branch(o) for o in orders], value)


def swap(value, axis, bit):
    pairs = [(i, i ^ bit) for i in range(lax.axis_size(axis))]
    return lax.ppermute(value, axis, pairs)


def cross(value, seq_core):
    pairs = [(i, i ^ (4 if i % 2 == seq_core else 2)) for i in range(8)]
    return lax.ppermute(value, ("seq", "tensor"), pairs)


def compress_kernel(chunks, *refs):
    (order_hbm, rows_hbm, weight_hbm, gain_hbm, query_hbm, latent_ref, half_ref, index_ref) = refs[:8]
    (order_ref, rows_ref, weight_ref, gain_ref, query_ref, wide, sems) = refs[8:]
    tokens, groups, width = rows_ref.shape
    chunk = tokens // chunks
    copies = [pltpu.make_async_copy(order_hbm, order_ref, sems.at[0])]
    for i in range(chunks):
        at = pl.ds(i * chunk, chunk)
        copies.append(pltpu.make_async_copy(rows_hbm.at[0, at], rows_ref.at[at], sems.at[1 + i]))
    for group in range(groups):
        at = pl.ds(group * width, width)
        copies.append(
            pltpu.make_async_copy(weight_hbm.at[at], weight_ref.at[at], sems.at[1 + chunks + group])
        )
    copies.append(pltpu.make_async_copy(gain_hbm, gain_ref, sems.at[1 + chunks + groups]))
    copies.append(pltpu.make_async_copy(query_hbm.at[0], query_ref, sems.at[2 + chunks + groups]))
    for copy in copies:
        copy.start()

    copies[0].wait()
    count = order_ref.shape[0]
    index = 0
    for i in range(count):
        smaller = 0
        for j in range(i + 1, count):
            smaller = smaller + (order_ref[j] < order_ref[i]).astype(jnp.int32)
        index = index + smaller * math.factorial(count - 1 - i)
    index_ref[0] = index

    lanes = wide.shape[2]
    for i in range(chunks):
        copies[1 + i].wait()
        for part in range(wide.shape[0]):
            values = rows_ref[i * chunk : (i + 1) * chunk, :, part * lanes : (part + 1) * lanes]
            wide[part, i * chunk * groups : (i + 1) * chunk * groups] = values.astype(F32).reshape(
                chunk * groups, lanes
            )
    projected = jnp.zeros((tokens, weight_ref.shape[1]), F32)
    for group in range(groups):
        picked = [
            wide[part, pl.ds(group, tokens, stride=groups), :] for part in range(wide.shape[0])
        ]
        picked = jnp.concatenate(picked, axis=1).astype(BF16)
        copies[1 + chunks + group].wait()
        projected += dot(picked, weight_ref[group * width : (group + 1) * width, :])
    copies[1 + chunks + groups].wait()
    scale = lax.rsqrt(jnp.mean(projected * projected, axis=-1, keepdims=True) + 1e-06)
    latent_ref[...] = (projected * scale * gain_ref[...].astype(F32)[None]).astype(BF16)

    copies[2 + chunks + groups].wait()
    new_count, heads, head_size = query_ref.shape
    query = query_ref[...].astype(F32)
    upper = lax.axis_index("seq") == 1
    query = jnp.where(upper, query[:, heads // 2 :], query[:, : heads // 2])
    half_ref[...] = query.reshape(half_ref.shape).astype(BF16)


def score_kernel(parts, *refs):
    latent_refs, (lift_ref, query_ref), (score_ref, value_ref, top_ref) = (
        refs[:parts],
        refs[parts : parts + 2],
        refs[parts + 2 :],
    )
    head_size = query_ref.shape[-1]
    lift = lift_ref[lax.axis_index("seq")]
    query = query_ref[...]
    top = None
    for part, latent_ref in enumerate(latent_refs):
        tokens = latent_ref.shape[0]
        at = slice(part * tokens, (part + 1) * tokens)
        lifted = dot(latent_ref[...], lift).astype(BF16)
        score = lax.dot_general(
            lifted[:, :head_size], query, (((1,), (1,)), ((), ())), preferred_element_type=F32
        )
        score_ref[at] = score
        value_ref[at] = lifted[:, head_size:]
        part_top = jnp.max(score, axis=0, keepdims=True)
        top = part_top if top is None else jnp.maximum(top, part_top)
    top_ref[...] = jnp.broadcast_to(top, top_ref.shape)


def score_and_fetch_kernel(parts, *refs):
    *refs, held_ref, sems = refs
    weight_ref = refs.pop(parts + 2)
    rows = weight_ref.shape[0] // COPIES
    copies = []
    for i in range(COPIES):
        at = pl.ds(i * rows, rows)
        copies.append(pltpu.make_async_copy(weight_ref.at[at], held_ref.at[at], sems.at[i]))
    for copy in copies:
        copy.start()
    score_kernel(parts, *refs)
    for copy in copies:
        copy.wait()


def score_call(name, latents, lift, query, weight=None):
    tokens = sum(latent.shape[0] for latent in latents)
    rows, head_size = query.shape
    flops = 2 * tokens * (lift.shape[1] * lift.shape[2] + rows * head_size)
    outs = [shape((tokens, rows), F32), shape((tokens, head_size), BF16), shape((8, rows), F32)]
    operands = [*latents, lift, query]
    estimate = cost(flops, 6 * tokens * rows)
    if weight is None:
        body = lambda *refs: score_kernel(len(latents), *refs)
        return call(body, name, outs, operands, 16, cost=estimate)
    return call(
        lambda *refs: score_and_fetch_kernel(len(latents), *refs),
        name,
        [*outs, pltpu.VMEM(weight.shape, weight.dtype)],
        [*operands, weight],
        12,
        scratch=[pltpu.SemaphoreType.DMA((COPIES,))],
        hbm_in=1,
        cost=cost(flops, 2 * weight.shape[0] * weight.shape[1]),
    )


def attend_kernel(new_count, block, *refs):
    (*score_refs, out_ref, turned) = refs
    triples = [score_refs[i : i + 3] for i in range(0, len(score_refs), 3)]
    head_size = triples[0][1].shape[-1]
    coef = head_size ** (-0.5) * math.log2(math.e)
    top = triples[0][2][:1]
    for triple in triples[1:]:
        top = jnp.maximum(top, triple[2][:1])
    total = jnp.zeros_like(top)
    summed = jnp.zeros((head_size, top.shape[1]), F32)
    for score_ref, value_ref, _ in triples:
        for start in range(0, score_ref.shape[0], block):
            at = slice(start, start + block)
            expo = jnp.exp2((score_ref[at] - top) * coef)
            total += jnp.sum(expo, axis=0, keepdims=True)
            summed += lax.dot_general(
                value_ref[at], expo.astype(BF16), (((0,), (0,)), ((), ())), preferred_element_type=F32
            )
    turned[...] = (summed / total).T
    heads = turned.shape[0] // new_count
    for head in range(heads):
        out_ref[:, head * head_size : (head + 1) * head_size] = turned[
            pl.ds(head, new_count, stride=heads), :
        ].astype(BF16)


def project_kernel(tile, rows_ref, weight_ref, out_ref):
    depth = rows_ref.shape[1]
    start = pl.multiple_of(lax.axis_index("seq") * depth, depth)
    rows = rows_ref[...]
    width = out_ref.shape[2]
    for part in range(out_ref.shape[0]):
        for column in range(0, width, tile):
            at = part * width + column
            out_ref[part, :, column : column + tile] = dot(
                rows, weight_ref[pl.ds(start, depth), at : at + tile]
            )


def project_more_kernel(tile, own, rows_ref, weight_ref, before_ref, *refs):
    out_ref = refs[-1]
    depth = rows_ref.shape[1]
    start = pl.multiple_of((1 - lax.axis_index("seq")) * depth, depth)
    core = lax.axis_index("tensor") % 2
    part = core if own else 1 - core
    rows = rows_ref[...]
    width = out_ref.shape[1]
    for column in range(0, width, tile):
        at = pl.multiple_of(part * width + column, tile)
        value = before_ref[part, :, column : column + tile] + dot(
            rows, weight_ref[pl.ds(start, depth), pl.ds(at, tile)]
        )
        out_ref[:, column : column + tile] = value


def square_shards(key_value_rows, queries, w_comp, latent_gain, w_up, w_out, replica_order):
    orders = list(itertools.permutations(range(lax.axis_size("rep"))))
    tensor_at = lax.axis_index("tensor")
    core_at, chip_at = tensor_at % 2, tensor_at // 2
    _, new_count, heads, head_size = queries.shape
    _, tokens, all_groups, width = key_value_rows.shape
    latent_width = w_comp.shape[1]
    rows = heads // 2 * new_count

    chunks = 3 if tokens % 48 == 0 else 1
    latent, query, index = call(
        lambda *refs: compress_kernel(chunks, *refs),
        "compress",
        [shape((tokens, latent_width), BF16), shape((rows, head_size), BF16), shape((1,), jnp.int32)],
        [replica_order, key_value_rows, w_comp, latent_gain, queries],
        16,
        scratch=[
            pltpu.SMEM(replica_order.shape, jnp.int32),
            pltpu.VMEM(key_value_rows.shape[1:], BF16),
            pltpu.VMEM(w_comp.shape, BF16),
            pltpu.VMEM(latent_gain.shape, BF16),
            pltpu.VMEM(queries.shape[1:], BF16),
            pltpu.VMEM((width // 128, tokens * all_groups, 128), F32),
            pltpu.SemaphoreType.DMA((3 + chunks + all_groups,)),
        ],
        hbm_in=5,
        smem_out=True,
        cost=cost(2 * tokens * all_groups * width * latent_width, 2 * tokens * all_groups * width),
    )

    def branch(order):
        def run(latent, query):
            return (
                cross(latent, 0),
                cross(latent, 1),
                swap(latent, "tensor", 1),
                lax.ppermute(query, "rep", route_pairs(order, False)),
            )

        return run

    near, far, beside, query = lax.switch(index[0], [branch(o) for o in orders], latent, query)
    corner = cross(near, 1)
    near_beside = swap(near, "tensor", 1)
    far_beside = swap(far, "tensor", 1)
    corner_beside = swap(corner, "tensor", 1)
    *first, held = score_call("score_chip", [latent, beside], w_up, query, w_out)
    held = pltpu.with_memory_space_constraint(held, pltpu.VMEM)
    second = score_call("score_next", [near, near_beside, far, far_beside], w_up, query)
    third = score_call("score_corner", [corner, corner_beside], w_up, query)
    depth = rows // new_count * head_size
    (attended,) = call(
        lambda *refs: attend_kernel(new_count, tokens, *refs),
        "attend",
        [shape((new_count, depth), BF16)],
        [*first, *second, *third],
        16,
        scratch=[pltpu.VMEM((rows, head_size), F32)],
        cost=cost(2 * 8 * tokens * rows * head_size, 8 * tokens * rows * 4, 8 * tokens * rows),
    )

    attended = route(attended, index[0], orders, True)
    attended_other = swap(attended, "seq", 1)
    columns = w_out.shape[1]
    tile = min(512, columns // 2)
    (partial,) = call(
        lambda *refs: project_kernel(tile, *refs),
        "project",
        [shape((2, new_count, columns // 2), F32)],
        [attended, held],
        12,
        cost=cost(2 * new_count * depth * columns, 2 * depth * columns),
    )

    def project_more(own, name):
        return call(
            lambda *refs: project_more_kernel(tile, own, *refs),
            name,
            [shape((new_count, columns // 2), F32)],
            [attended_other, held, partial],
            12,
            cost=cost(new_count * depth * columns, depth * columns),
        )[0]

    sent = swap(project_more(False, "project_sent"), "tensor", 1)
    half = project_more(True, "project_own") + sent
    quarter = half.shape[1] // 2
    low, high = half[:, :quarter], half[:, quarter:]
    upper = chip_at == 1
    arrived = swap(jnp.where(upper, low, high), "tensor", 2)
    summed = (jnp.where(upper, high, low) + arrived).astype(BF16)
    summed_across = swap(summed, "tensor", 2)
    half = jnp.where(
        upper,
        jnp.concatenate([summed_across, summed], axis=1),
        jnp.concatenate([summed, summed_across], axis=1),
    )
    half_beside = swap(half, "tensor", 1)
    whole = jnp.where(
        core_at == 1,
        jnp.concatenate([half_beside, half], axis=1),
        jnp.concatenate([half, half_beside], axis=1),
    )
    return whole[None]


def shards(key_value_rows, queries, w_comp, latent_gain, w_up, w_out, replica_order):
    orders = list(itertools.permutations(range(lax.axis_size("rep"))))
    index = order_index(replica_order, orders)
    query = route(queries[0], index, orders, False)
    rows = key_value_rows[0]
    latent = compress(rows.reshape(rows.shape[0], -1), w_comp, latent_gain)
    latent = lax.all_gather(latent, "tensor", axis=0, tiled=True)
    groups = w_up.shape[0]
    lifted = jnp.einsum("tf,gfy->tgy", latent, w_up, preferred_element_type=F32).astype(BF16)
    head_size = query.shape[-1]
    new_count = query.shape[0]
    keys = lifted[..., :head_size]
    values = lifted[..., head_size:]
    grouped_heads = query.reshape(new_count, groups, -1, head_size)
    scores = jnp.einsum(
        "nghd,tgd->nght", grouped_heads, keys, preferred_element_type=F32
    ) * head_size ** (-0.5)
    top = lax.pmax(jnp.max(scores, axis=-1), "seq")
    expo = jnp.exp(scores - top[..., None])
    total = jnp.sum(expo, axis=-1)
    summed = jnp.einsum("nght,tgd->nghd", expo.astype(BF16), values, preferred_element_type=F32)
    summed, total = lax.psum((summed, total), "seq")
    attended = (summed / total[..., None]).astype(BF16).reshape(new_count, -1)
    attended = route(attended, index, orders, True)
    return lax.psum(dot(attended, w_out), "tensor").astype(BF16)[None]


def solution(mesh):
    placed = (
        P("rep", ("seq", "tensor"), None, None),
        P("rep", None, "tensor", None),
        P(),
        P(),
        P("tensor", None, None),
        P("tensor", "seq"),
        P(),
    )
    square = mesh.shape["seq"] == 2 and mesh.shape["tensor"] == 4
    return jax.shard_map(
        square_shards if square else shards,
        mesh=mesh,
        in_specs=placed,
        out_specs=P("rep", None, "seq"),
        check_vma=False,
    )
```

```python
import itertools
import math

import jax
import jax.numpy as jnp
from jax import lax
from jax.experimental import pallas as pl
from jax.experimental.pallas import tpu as pltpu
from jax.sharding import PartitionSpec as P

BF16, F32 = jnp.bfloat16, jnp.float32
MIB = 1024 * 1024
IN_VMEM = pl.BlockSpec(memory_space=pltpu.VMEM)
IN_SMEM = pl.BlockSpec(memory_space=pltpu.SMEM)
IN_HBM = pl.BlockSpec(memory_space=pltpu.HBM)
COPIES = 8


def shape(dims, dtype):
    return jax.ShapeDtypeStruct(dims, dtype)


def call(body, name, outs, operands, vmem, scratch=(), smem_out=False, hbm_in=0, cost=None):
    kept = len(operands) - hbm_in
    specs = [IN_VMEM] * kept + [IN_HBM] * hbm_in
    operands = [
        *operands[:kept],
        *(pltpu.with_memory_space_constraint(operand, pltpu.HBM) for operand in operands[kept:]),
    ]
    out_specs = [IN_VMEM] * len(outs)
    if smem_out:
        out_specs[-1] = IN_SMEM
    return pl.pallas_call(
        body,
        out_shape=outs,
        in_specs=specs,
        out_specs=out_specs,
        scratch_shapes=list(scratch),
        compiler_params=pltpu.CompilerParams(vmem_limit_bytes=vmem * MIB),
        cost_estimate=cost,
        name=name,
    )(*operands)


def cost(flops, moved, exps=0):
    return pl.CostEstimate(flops=int(flops), bytes_accessed=int(moved), transcendentals=int(exps))


def dot(a, b):
    return jnp.dot(a, b, preferred_element_type=F32)


def compress(rows, weight, gain):
    projected = dot(rows, weight)
    scale = lax.rsqrt(jnp.mean(projected * projected, axis=-1, keepdims=True) + 1e-06)
    return (projected * scale * gain.astype(F32)[None]).astype(BF16)


def order_index(replica_order, orders):
    table = jnp.array(orders, jnp.int32)
    match = jnp.all(table == replica_order[None], axis=1)
    return jnp.sum(jnp.where(match, lax.iota(jnp.int32, len(orders)), 0))


def route_pairs(order, back):
    return [(p, r) if back else (r, p) for r, p in enumerate(order)]


def route(value, index, orders, back):
    def branch(order):
        return lambda v: lax.ppermute(v, "rep", route_pairs(order, back))

    return lax.switch(index, [branch(o) for o in orders], value)


def swap(value, axis, bit):
    pairs = [(i, i ^ bit) for i in range(lax.axis_size(axis))]
    return lax.ppermute(value, axis, pairs)


def cross(value, seq_core):
    pairs = [(i, i ^ (4 if i % 2 == seq_core else 2)) for i in range(8)]
    return lax.ppermute(value, ("seq", "tensor"), pairs)


def compress_kernel(chunks, *refs):
    (order_hbm, rows_hbm, weight_hbm, gain_hbm, query_hbm, latent_ref, half_ref, index_ref) = refs[:8]
    (order_ref, rows_ref, weight_ref, gain_ref, query_ref, wide, packed, sems) = refs[8:]
    tokens, groups, width = rows_ref.shape
    chunk = tokens // chunks
    copies = [pltpu.make_async_copy(order_hbm, order_ref, sems.at[0])]
    for i in range(chunks):
        at = pl.ds(i * chunk, chunk)
        copies.append(pltpu.make_async_copy(rows_hbm.at[0, at], rows_ref.at[at], sems.at[1 + i]))
    for group in range(groups):
        at = pl.ds(group * width, width)
        copies.append(
            pltpu.make_async_copy(weight_hbm.at[at], weight_ref.at[at], sems.at[1 + chunks + group])
        )
    copies.append(pltpu.make_async_copy(gain_hbm, gain_ref, sems.at[1 + chunks + groups]))
    copies.append(pltpu.make_async_copy(query_hbm.at[0], query_ref, sems.at[2 + chunks + groups]))
    for copy in copies:
        copy.start()

    copies[0].wait()
    count = order_ref.shape[0]
    index = 0
    for i in range(count):
        smaller = 0
        for j in range(i + 1, count):
            smaller = smaller + (order_ref[j] < order_ref[i]).astype(jnp.int32)
        index = index + smaller * math.factorial(count - 1 - i)
    index_ref[0] = index

    lanes = wide.shape[2]
    for i in range(chunks):
        copies[1 + i].wait()
        at = slice(i * chunk * groups, (i + 1) * chunk * groups)
        for part in range(wide.shape[0]):
            values = rows_ref[i * chunk : (i + 1) * chunk, :, part * lanes : (part + 1) * lanes]
            wide[part, at] = values.astype(F32).reshape(chunk * groups, lanes)
        for group in range(groups):
            for part in range(wide.shape[0]):
                start = group * width + part * lanes
                picked = wide[part, pl.ds(at.start + group, chunk, stride=groups), :]
                packed[i * chunk : (i + 1) * chunk, start : start + lanes] = picked.astype(BF16)
    for group in range(groups):
        copies[1 + chunks + group].wait()
    copies[1 + chunks + groups].wait()
    gain = gain_ref[...].astype(F32)[None]
    for i in range(chunks):
        at = slice(i * chunk, (i + 1) * chunk)
        projected = dot(packed[at], weight_ref[...])
        scale = lax.rsqrt(jnp.mean(projected * projected, axis=-1, keepdims=True) + 1e-06)
        latent_ref[at] = (projected * scale * gain).astype(BF16)

    copies[2 + chunks + groups].wait()
    new_count, heads, head_size = query_ref.shape
    query = query_ref[...].astype(F32)
    upper = lax.axis_index("seq") == 1
    query = jnp.where(upper, query[:, heads // 2 :], query[:, : heads // 2])
    half_ref[...] = query.reshape(half_ref.shape).astype(BF16)


def score_kernel(parts, *refs):
    latent_refs, (lift_ref, query_ref), (score_ref, value_ref, top_ref) = (
        refs[:parts],
        refs[parts : parts + 2],
        refs[parts + 2 :],
    )
    head_size = query_ref.shape[-1]
    lift = lift_ref[lax.axis_index("seq")]
    query = query_ref[...]
    top = None
    for part, latent_ref in enumerate(latent_refs):
        tokens = latent_ref.shape[0]
        at = slice(part * tokens, (part + 1) * tokens)
        lifted = dot(latent_ref[...], lift).astype(BF16)
        score = lax.dot_general(
            lifted[:, :head_size], query, (((1,), (1,)), ((), ())), preferred_element_type=F32
        )
        score_ref[at] = score
        value_ref[at] = lifted[:, head_size:]
        part_top = jnp.max(score, axis=0, keepdims=True)
        top = part_top if top is None else jnp.maximum(top, part_top)
    top_ref[...] = jnp.broadcast_to(top, top_ref.shape)


def score_and_fetch_kernel(parts, own, *refs):
    *refs, held_ref, sems = refs
    weight_ref = refs.pop(parts + 2)
    rows = held_ref.shape[0] // COPIES
    half = lax.axis_index("seq") if own else 1 - lax.axis_index("seq")
    start = half * held_ref.shape[0]
    copies = []
    for i in range(COPIES):
        source = weight_ref.at[pl.ds(pl.multiple_of(start + i * rows, rows), rows)]
        copies.append(
            pltpu.make_async_copy(source, held_ref.at[pl.ds(i * rows, rows)], sems.at[i])
        )
    for copy in copies:
        copy.start()
    score_kernel(parts, *refs)
    for copy in copies:
        copy.wait()


def score_call(name, latents, lift, query, weight=None, own=False):
    tokens = sum(latent.shape[0] for latent in latents)
    rows, head_size = query.shape
    flops = 2 * tokens * (lift.shape[1] * lift.shape[2] + rows * head_size)
    outs = [shape((tokens, rows), F32), shape((tokens, head_size), BF16), shape((8, rows), F32)]
    operands = [*latents, lift, query]
    estimate = cost(flops, 6 * tokens * rows)
    if weight is None:
        body = lambda *refs: score_kernel(len(latents), *refs)
        return call(body, name, outs, operands, 16, cost=estimate)
    held = (weight.shape[0] // 2, weight.shape[1])
    return call(
        lambda *refs: score_and_fetch_kernel(len(latents), own, *refs),
        name,
        [*outs, pltpu.VMEM(held, weight.dtype)],
        [*operands, weight],
        12,
        scratch=[pltpu.SemaphoreType.DMA((COPIES,))],
        hbm_in=1,
        cost=cost(flops, 2 * held[0] * held[1]),
    )


def attend_kernel(new_count, block, *refs):
    (*score_refs, out_ref, turned) = refs
    triples = [score_refs[i : i + 3] for i in range(0, len(score_refs), 3)]
    head_size = triples[0][1].shape[-1]
    coef = head_size ** (-0.5) * math.log2(math.e)
    top = triples[0][2][:1]
    for triple in triples[1:]:
        top = jnp.maximum(top, triple[2][:1])
    total = jnp.zeros_like(top)
    summed = jnp.zeros((head_size, top.shape[1]), F32)
    for score_ref, value_ref, _ in triples:
        for start in range(0, score_ref.shape[0], block):
            at = slice(start, start + block)
            expo = jnp.exp2((score_ref[at] - top) * coef)
            total += jnp.sum(expo, axis=0, keepdims=True)
            summed += lax.dot_general(
                value_ref[at], expo.astype(BF16), (((0,), (0,)), ((), ())), preferred_element_type=F32
            )
    turned[...] = (summed / total).T
    heads = turned.shape[0] // new_count
    for head in range(heads):
        out_ref[:, head * head_size : (head + 1) * head_size] = turned[
            pl.ds(head, new_count, stride=heads), :
        ].astype(BF16)


def project_kernel(tile, rows_ref, weight_ref, out_ref):
    rows = rows_ref[...]
    width = out_ref.shape[2]
    for part in range(out_ref.shape[0]):
        for column in range(0, width, tile):
            at = part * width + column
            out_ref[part, :, column : column + tile] = dot(
                rows, weight_ref[:, at : at + tile]
            )


def project_more_kernel(tile, own, rows_ref, weight_ref, before_ref, *refs):
    out_ref = refs[-1]
    core = lax.axis_index("tensor") % 2
    part = core if own else 1 - core
    rows = rows_ref[...]
    width = out_ref.shape[1]
    for column in range(0, width, tile):
        at = pl.multiple_of(part * width + column, tile)
        value = before_ref[part, :, column : column + tile] + dot(
            rows, weight_ref[:, pl.ds(at, tile)]
        )
        out_ref[:, column : column + tile] = value


def square_shards(key_value_rows, queries, w_comp, latent_gain, w_up, w_out, replica_order):
    orders = list(itertools.permutations(range(lax.axis_size("rep"))))
    _, new_count, heads, head_size = queries.shape
    _, tokens, all_groups, width = key_value_rows.shape
    latent_width = w_comp.shape[1]
    rows = heads // 2 * new_count

    chunks = 3 if tokens % 48 == 0 else 1
    latent, query, index = call(
        lambda *refs: compress_kernel(chunks, *refs),
        "compress",
        [shape((tokens, latent_width), BF16), shape((rows, head_size), BF16), shape((1,), jnp.int32)],
        [replica_order, key_value_rows, w_comp, latent_gain, queries],
        16,
        scratch=[
            pltpu.SMEM(replica_order.shape, jnp.int32),
            pltpu.VMEM(key_value_rows.shape[1:], BF16),
            pltpu.VMEM(w_comp.shape, BF16),
            pltpu.VMEM(latent_gain.shape, BF16),
            pltpu.VMEM(queries.shape[1:], BF16),
            pltpu.VMEM((width // 128, tokens * all_groups, 128), F32),
            pltpu.VMEM((tokens, all_groups * width), BF16),
            pltpu.SemaphoreType.DMA((3 + chunks + all_groups,)),
        ],
        hbm_in=5,
        smem_out=True,
        cost=cost(2 * tokens * all_groups * width * latent_width, 2 * tokens * all_groups * width),
    )

    def branch(order):
        return lambda *operands: after_compress(order, new_count, *operands)

    return lax.switch(index[0], [branch(o) for o in orders], latent, query, w_up, w_out)


def after_compress(order, new_count, latent, query, w_up, w_out):
    tensor_at = lax.axis_index("tensor")
    core_at, chip_at = tensor_at % 2, tensor_at // 2
    tokens = latent.shape[0]
    rows, head_size = query.shape
    near = cross(latent, 0)
    far = cross(latent, 1)
    beside = swap(latent, "tensor", 1)
    query = lax.ppermute(query, "rep", route_pairs(order, False))
    corner = cross(near, 1)
    near_beside = swap(near, "tensor", 1)
    far_beside = swap(far, "tensor", 1)
    *first, held = score_call("score_chip", [latent, beside], w_up, query, w_out, True)
    *second, held_other = score_call(
        "score_next", [near, near_beside, far, far_beside], w_up, query, w_out, False
    )
    corner, first[2], second[2] = lax.optimization_barrier((corner, first[2], second[2]))
    corner_beside = swap(corner, "tensor", 1)
    third = score_call("score_corner", [corner, corner_beside], w_up, query)
    depth = rows // new_count * head_size
    (attended,) = call(
        lambda *refs: attend_kernel(new_count, tokens, *refs),
        "attend",
        [shape((new_count, depth), BF16)],
        [*first, *second, *third],
        16,
        scratch=[pltpu.VMEM((rows, head_size), F32)],
        cost=cost(2 * 8 * tokens * rows * head_size, 8 * tokens * rows * 4, 8 * tokens * rows),
    )

    attended = lax.ppermute(attended, "rep", route_pairs(order, True))
    attended_other = swap(attended, "seq", 1)
    columns = w_out.shape[1]
    tile = min(512, columns // 2)
    (partial,) = call(
        lambda *refs: project_kernel(tile, *refs),
        "project",
        [shape((2, new_count, columns // 2), F32)],
        [attended, held],
        12,
        cost=cost(2 * new_count * depth * columns, 2 * depth * columns),
    )

    def project_more(own, name):
        return call(
            lambda *refs: project_more_kernel(tile, own, *refs),
            name,
            [shape((new_count, columns // 2), F32)],
            [attended_other, held_other, partial],
            12,
            cost=cost(new_count * depth * columns, depth * columns),
        )[0]

    sent = swap(project_more(False, "project_sent"), "tensor", 1)
    half = project_more(True, "project_own") + sent
    quarter = half.shape[1] // 2
    low, high = half[:, :quarter], half[:, quarter:]
    upper = chip_at == 1
    arrived = swap(jnp.where(upper, low, high), "tensor", 2)
    summed = (jnp.where(upper, high, low) + arrived).astype(BF16)
    summed_across = swap(summed, "tensor", 2)
    half = jnp.where(
        upper,
        jnp.concatenate([summed_across, summed], axis=1),
        jnp.concatenate([summed, summed_across], axis=1),
    )
    half_beside = swap(half, "tensor", 1)
    whole = jnp.where(
        core_at == 1,
        jnp.concatenate([half_beside, half], axis=1),
        jnp.concatenate([half, half_beside], axis=1),
    )
    return whole[None]


def shards(key_value_rows, queries, w_comp, latent_gain, w_up, w_out, replica_order):
    orders = list(itertools.permutations(range(lax.axis_size("rep"))))
    index = order_index(replica_order, orders)
    query = route(queries[0], index, orders, False)
    rows = key_value_rows[0]
    latent = compress(rows.reshape(rows.shape[0], -1), w_comp, latent_gain)
    latent = lax.all_gather(latent, "tensor", axis=0, tiled=True)
    groups = w_up.shape[0]
    lifted = jnp.einsum("tf,gfy->tgy", latent, w_up, preferred_element_type=F32).astype(BF16)
    head_size = query.shape[-1]
    new_count = query.shape[0]
    keys = lifted[..., :head_size]
    values = lifted[..., head_size:]
    grouped_heads = query.reshape(new_count, groups, -1, head_size)
    scores = jnp.einsum(
        "nghd,tgd->nght", grouped_heads, keys, preferred_element_type=F32
    ) * head_size ** (-0.5)
    top = lax.pmax(jnp.max(scores, axis=-1), "seq")
    expo = jnp.exp(scores - top[..., None])
    total = jnp.sum(expo, axis=-1)
    summed = jnp.einsum("nght,tgd->nghd", expo.astype(BF16), values, preferred_element_type=F32)
    summed, total = lax.psum((summed, total), "seq")
    attended = (summed / total[..., None]).astype(BF16).reshape(new_count, -1)
    attended = route(attended, index, orders, True)
    return lax.psum(dot(attended, w_out), "tensor").astype(BF16)[None]


def solution(mesh):
    placed = (
        P("rep", ("seq", "tensor"), None, None),
        P("rep", None, "tensor", None),
        P(),
        P(),
        P("tensor", None, None),
        P("tensor", "seq"),
        P(),
    )
    square = mesh.shape["seq"] == 2 and mesh.shape["tensor"] == 4
    return jax.shard_map(
        square_shards if square else shards,
        mesh=mesh,
        in_specs=placed,
        out_specs=P("rep", None, "seq"),
        check_vma=False,
    )
```

```python
import itertools
import math

import jax
import jax.numpy as jnp
from jax import lax
from jax.experimental import pallas as pl
from jax.experimental.pallas import tpu as pltpu
from jax.sharding import PartitionSpec as P

BF16, F32 = jnp.bfloat16, jnp.float32
MIB = 1024 * 1024
IN_VMEM = pl.BlockSpec(memory_space=pltpu.VMEM)
IN_SMEM = pl.BlockSpec(memory_space=pltpu.SMEM)
IN_HBM = pl.BlockSpec(memory_space=pltpu.HBM)
COPIES = 8


def shape(dims, dtype):
    return jax.ShapeDtypeStruct(dims, dtype)


def call(body, name, outs, operands, vmem, scratch=(), smem_in=0, smem_out=False, hbm_in=0, cost=None):
    kept = len(operands) - hbm_in
    specs = [IN_SMEM] * smem_in + [IN_VMEM] * (kept - smem_in) + [IN_HBM] * hbm_in
    operands = [
        *operands[:kept],
        *(pltpu.with_memory_space_constraint(operand, pltpu.HBM) for operand in operands[kept:]),
    ]
    out_specs = [IN_VMEM] * len(outs)
    if smem_out:
        out_specs[-1] = IN_SMEM
    return pl.pallas_call(
        body,
        out_shape=outs,
        in_specs=specs,
        out_specs=out_specs,
        scratch_shapes=list(scratch),
        compiler_params=pltpu.CompilerParams(vmem_limit_bytes=vmem * MIB),
        cost_estimate=cost,
        name=name,
    )(*operands)


def cost(flops, moved, exps=0):
    return pl.CostEstimate(flops=int(flops), bytes_accessed=int(moved), transcendentals=int(exps))


def dot(a, b):
    return jnp.dot(a, b, preferred_element_type=F32)


def compress(rows, weight, gain):
    projected = dot(rows, weight)
    scale = lax.rsqrt(jnp.mean(projected * projected, axis=-1, keepdims=True) + 1e-06)
    return (projected * scale * gain.astype(F32)[None]).astype(BF16)


def order_index(replica_order, orders):
    table = jnp.array(orders, jnp.int32)
    match = jnp.all(table == replica_order[None], axis=1)
    return jnp.sum(jnp.where(match, lax.iota(jnp.int32, len(orders)), 0))


def route_pairs(order, back):
    return [(p, r) if back else (r, p) for r, p in enumerate(order)]


def route(value, index, orders, back):
    def branch(order):
        return lambda v: lax.ppermute(v, "rep", route_pairs(order, back))

    return lax.switch(index, [branch(o) for o in orders], value)


def shift(value, axis, hops):
    size = lax.axis_size(axis)
    return lax.ppermute(value, axis, [(i, (i + hops) % size) for i in range(size)])


def swap(value, axis, bit):
    pairs = [(i, i ^ bit) for i in range(lax.axis_size(axis))]
    return lax.ppermute(value, axis, pairs)


def cross(value, seq_core):
    pairs = [(i, i ^ (4 if i % 2 == seq_core else 2)) for i in range(8)]
    return lax.ppermute(value, ("seq", "tensor"), pairs)


def compress_kernel(chunks, *refs):
    (order_hbm, rows_hbm, weight_hbm, gain_hbm, query_hbm, latent_ref, half_ref, index_ref) = refs[:8]
    (order_ref, rows_ref, weight_ref, gain_ref, query_ref, wide, packed, sems) = refs[8:]
    tokens, groups, width = rows_ref.shape
    chunk = tokens // chunks
    copies = [pltpu.make_async_copy(order_hbm, order_ref, sems.at[0])]
    for i in range(chunks):
        at = pl.ds(i * chunk, chunk)
        copies.append(pltpu.make_async_copy(rows_hbm.at[0, at], rows_ref.at[at], sems.at[1 + i]))
    for group in range(groups):
        at = pl.ds(group * width, width)
        copies.append(
            pltpu.make_async_copy(weight_hbm.at[at], weight_ref.at[at], sems.at[1 + chunks + group])
        )
    copies.append(pltpu.make_async_copy(gain_hbm, gain_ref, sems.at[1 + chunks + groups]))
    copies.append(pltpu.make_async_copy(query_hbm.at[0], query_ref, sems.at[2 + chunks + groups]))
    for copy in copies:
        copy.start()

    copies[0].wait()
    count = order_ref.shape[0]
    index = 0
    for i in range(count):
        smaller = 0
        for j in range(i + 1, count):
            smaller = smaller + (order_ref[j] < order_ref[i]).astype(jnp.int32)
        index = index + smaller * math.factorial(count - 1 - i)
    index_ref[0] = index

    lanes = wide.shape[2]
    for i in range(chunks):
        copies[1 + i].wait()
        at = slice(i * chunk * groups, (i + 1) * chunk * groups)
        for part in range(wide.shape[0]):
            values = rows_ref[i * chunk : (i + 1) * chunk, :, part * lanes : (part + 1) * lanes]
            wide[part, at] = values.astype(F32).reshape(chunk * groups, lanes)
        for group in range(groups):
            for part in range(wide.shape[0]):
                start = group * width + part * lanes
                picked = wide[part, pl.ds(at.start + group, chunk, stride=groups), :]
                packed[i * chunk : (i + 1) * chunk, start : start + lanes] = picked.astype(BF16)
    for group in range(groups):
        copies[1 + chunks + group].wait()
    copies[1 + chunks + groups].wait()
    gain = gain_ref[...].astype(F32)[None]
    for i in range(chunks):
        at = slice(i * chunk, (i + 1) * chunk)
        projected = dot(packed[at], weight_ref[...])
        scale = lax.rsqrt(jnp.mean(projected * projected, axis=-1, keepdims=True) + 1e-06)
        latent_ref[at] = (projected * scale * gain).astype(BF16)

    copies[2 + chunks + groups].wait()
    new_count, heads, head_size = query_ref.shape
    query = query_ref[...].astype(F32)
    upper = lax.axis_index("seq") == 1
    query = jnp.where(upper, query[:, heads // 2 :], query[:, : heads // 2])
    half_ref[...] = query.reshape(half_ref.shape).astype(BF16)


def score_kernel(parts, *refs):
    latent_refs, (lift_ref, query_ref), (score_ref, value_ref, top_ref) = (
        refs[:parts],
        refs[parts : parts + 2],
        refs[parts + 2 :],
    )
    head_size = query_ref.shape[-1]
    lift = lift_ref[lax.axis_index("seq")]
    query = query_ref[...]
    top = None
    for part, latent_ref in enumerate(latent_refs):
        tokens = latent_ref.shape[0]
        at = slice(part * tokens, (part + 1) * tokens)
        lifted = dot(latent_ref[...], lift).astype(BF16)
        score = lax.dot_general(
            lifted[:, :head_size], query, (((1,), (1,)), ((), ())), preferred_element_type=F32
        )
        score_ref[at] = score
        value_ref[at] = lifted[:, head_size:]
        part_top = jnp.max(score, axis=0, keepdims=True)
        top = part_top if top is None else jnp.maximum(top, part_top)
    top_ref[...] = jnp.broadcast_to(top, top_ref.shape)


def weight_copies(own, weight_ref, held_ref, sems):
    rows = held_ref.shape[0] // COPIES
    half = lax.axis_index("seq") if own else 1 - lax.axis_index("seq")
    copies = []
    for i in range(COPIES):
        start = pl.multiple_of(half * held_ref.shape[0] + i * rows, rows)
        source = weight_ref.at[pl.ds(start, rows)]
        copies.append(
            pltpu.make_async_copy(source, held_ref.at[pl.ds(i * rows, rows)], sems.at[i])
        )
    return copies


def score_and_fetch_kernel(parts, *refs):
    *refs, held_ref, sems = refs
    copies = weight_copies(True, refs.pop(parts + 2), held_ref, sems)
    for copy in copies:
        copy.start()
    score_kernel(parts, *refs)
    for copy in copies:
        copy.wait()


def score_call(name, latents, lift, query, weight=None):
    tokens = sum(latent.shape[0] for latent in latents)
    rows, head_size = query.shape
    flops = 2 * tokens * (lift.shape[1] * lift.shape[2] + rows * head_size)
    outs = [shape((tokens, rows), F32), shape((tokens, head_size), BF16), shape((8, rows), F32)]
    operands = [*latents, lift, query]
    if weight is None:
        body = lambda *refs: score_kernel(len(latents), *refs)
        return call(body, name, outs, operands, 16, cost=cost(flops, 6 * tokens * rows))
    held = (weight.shape[0] // 2, weight.shape[1])
    return call(
        lambda *refs: score_and_fetch_kernel(len(latents), *refs),
        name,
        [*outs, pltpu.VMEM(held, weight.dtype)],
        [*operands, weight],
        16,
        scratch=[pltpu.SemaphoreType.DMA((COPIES,))],
        hbm_in=1,
        cost=cost(flops, 2 * held[0] * held[1]),
    )


def attend_kernel(new_count, block, *refs):
    (*score_refs, out_ref, turned) = refs
    triples = [score_refs[i : i + 3] for i in range(0, len(score_refs), 3)]
    head_size = triples[0][1].shape[-1]
    coef = head_size ** (-0.5) * math.log2(math.e)
    top = triples[0][2][:1]
    for triple in triples[1:]:
        top = jnp.maximum(top, triple[2][:1])
    total = jnp.zeros_like(top)
    summed = jnp.zeros((head_size, top.shape[1]), F32)
    for score_ref, value_ref, _ in triples:
        for start in range(0, score_ref.shape[0], block):
            at = slice(start, start + block)
            expo = jnp.exp2((score_ref[at] - top) * coef)
            total += jnp.sum(expo, axis=0, keepdims=True)
            summed += lax.dot_general(
                value_ref[at], expo.astype(BF16), (((0,), (0,)), ((), ())), preferred_element_type=F32
            )
    turned[...] = (summed / total).T
    heads = turned.shape[0] // new_count
    for head in range(heads):
        out_ref[:, head * head_size : (head + 1) * head_size] = turned[
            pl.ds(head, new_count, stride=heads), :
        ].astype(BF16)


def project_kernel(tile, rows_ref, weight_ref, all_ref, out_ref, held_ref, sems):
    copies = weight_copies(False, all_ref, held_ref, sems)
    for copy in copies:
        copy.start()
    rows = rows_ref[...]
    width = out_ref.shape[2]
    for part in range(out_ref.shape[0]):
        for column in range(0, width, tile):
            at = part * width + column
            out_ref[part, :, column : column + tile] = dot(
                rows, weight_ref[:, at : at + tile]
            )
    for copy in copies:
        copy.wait()


def project_more_kernel(tile, own, rows_ref, weight_ref, before_ref, *refs):
    out_ref = refs[-1]
    core = lax.axis_index("tensor") % 2
    part = core if own else 1 - core
    rows = rows_ref[...]
    width = out_ref.shape[1]
    for column in range(0, width, tile):
        at = pl.multiple_of(part * width + column, tile)
        value = before_ref[part, :, column : column + tile] + dot(
            rows, weight_ref[:, pl.ds(at, tile)]
        )
        out_ref[:, column : column + tile] = value


def square_shards(key_value_rows, queries, w_comp, latent_gain, w_up, w_out, replica_order):
    orders = list(itertools.permutations(range(lax.axis_size("rep"))))
    tensor_at = lax.axis_index("tensor")
    core_at, chip_at = tensor_at % 2, tensor_at // 2
    _, new_count, heads, head_size = queries.shape
    _, tokens, all_groups, width = key_value_rows.shape
    latent_width = w_comp.shape[1]
    rows = heads // 2 * new_count

    chunks = 3 if tokens % 48 == 0 else 1
    latent, query, index = call(
        lambda *refs: compress_kernel(chunks, *refs),
        "compress",
        [shape((tokens, latent_width), BF16), shape((rows, head_size), BF16), shape((1,), jnp.int32)],
        [replica_order, key_value_rows, w_comp, latent_gain, queries],
        16,
        scratch=[
            pltpu.SMEM(replica_order.shape, jnp.int32),
            pltpu.VMEM(key_value_rows.shape[1:], BF16),
            pltpu.VMEM(w_comp.shape, BF16),
            pltpu.VMEM(latent_gain.shape, BF16),
            pltpu.VMEM(queries.shape[1:], BF16),
            pltpu.VMEM((width // 128, tokens * all_groups, 128), F32),
            pltpu.VMEM((tokens, all_groups * width), BF16),
            pltpu.SemaphoreType.DMA((3 + chunks + all_groups,)),
        ],
        hbm_in=5,
        smem_out=True,
        cost=cost(2 * tokens * all_groups * width * latent_width, 2 * tokens * all_groups * width),
    )

    def branch(order):
        def run(latent, query):
            return (
                cross(latent, 0),
                cross(latent, 1),
                swap(latent, "tensor", 1),
                lax.ppermute(query, "rep", route_pairs(order, False)),
            )

        return run

    near, far, beside, query = lax.switch(index[0], [branch(o) for o in orders], latent, query)
    corner = cross(near, 1)
    near_beside = swap(near, "tensor", 1)
    far_beside = swap(far, "tensor", 1)
    *first, held = score_call("score_chip", [latent, beside], w_up, query, w_out)
    *second, = score_call("score_next", [near, near_beside, far, far_beside], w_up, query)
    corner, first[2], second[2] = lax.optimization_barrier((corner, first[2], second[2]))
    corner_beside = swap(corner, "tensor", 1)
    third = score_call("score_corner", [corner, corner_beside], w_up, query)
    depth = rows // new_count * head_size
    (attended,) = call(
        lambda *refs: attend_kernel(new_count, tokens, *refs),
        "attend",
        [shape((new_count, depth), BF16)],
        [*first, *second, *third],
        16,
        scratch=[pltpu.VMEM((rows, head_size), F32)],
        cost=cost(2 * 8 * tokens * rows * head_size, 8 * tokens * rows * 4, 8 * tokens * rows),
    )

    attended_other = swap(attended, "seq", 1)
    columns = w_out.shape[1]
    tile = min(512, columns // 2)
    partial, held_other = call(
        lambda *refs: project_kernel(tile, *refs),
        "project",
        [shape((2, new_count, columns // 2), F32), pltpu.VMEM(held.shape, held.dtype)],
        [attended, held, w_out],
        12,
        scratch=[pltpu.SemaphoreType.DMA((COPIES,))],
        hbm_in=1,
        cost=cost(2 * new_count * depth * columns, 2 * depth * columns),
    )

    def project_more(own, name):
        return call(
            lambda *refs: project_more_kernel(tile, own, *refs),
            name,
            [shape((new_count, columns // 2), F32)],
            [attended_other, held_other, partial],
            12,
            cost=cost(new_count * depth * columns, depth * columns),
        )[0]

    sent = swap(project_more(False, "project_sent"), "tensor", 1)
    half = project_more(True, "project_own") + sent
    quarter = half.shape[1] // 2
    low, high = half[:, :quarter], half[:, quarter:]
    upper = chip_at == 1
    arrived = swap(jnp.where(upper, low, high), "tensor", 2)
    summed = (jnp.where(upper, high, low) + arrived).astype(BF16)

    def reply(order):
        def run(value):
            pairs = [(p * 4 + t, r * 4 + t) for r, p in enumerate(order) for t in range(4)]
            crossed = [(source, target ^ 2) for source, target in pairs]
            axes = ("rep", "tensor")
            return lax.ppermute(value, axes, pairs), lax.ppermute(value, axes, crossed)

        return run

    summed, summed_across = lax.switch(index[0], [reply(o) for o in orders], summed)
    half = jnp.where(
        upper,
        jnp.concatenate([summed_across, summed], axis=1),
        jnp.concatenate([summed, summed_across], axis=1),
    )
    half_beside = swap(half, "tensor", 1)
    whole = jnp.where(
        core_at == 1,
        jnp.concatenate([half_beside, half], axis=1),
        jnp.concatenate([half, half_beside], axis=1),
    )
    return whole[None]


def shards(key_value_rows, queries, w_comp, latent_gain, w_up, w_out, replica_order):
    orders = list(itertools.permutations(range(lax.axis_size("rep"))))
    index = order_index(replica_order, orders)
    query = route(queries[0], index, orders, False)
    rows = key_value_rows[0]
    latent = compress(rows.reshape(rows.shape[0], -1), w_comp, latent_gain)
    latent = lax.all_gather(latent, "tensor", axis=0, tiled=True)
    groups = w_up.shape[0]
    lifted = jnp.einsum("tf,gfy->tgy", latent, w_up, preferred_element_type=F32).astype(BF16)
    head_size = query.shape[-1]
    new_count = query.shape[0]
    keys = lifted[..., :head_size]
    values = lifted[..., head_size:]
    grouped_heads = query.reshape(new_count, groups, -1, head_size)
    scores = jnp.einsum(
        "nghd,tgd->nght", grouped_heads, keys, preferred_element_type=F32
    ) * head_size ** (-0.5)
    top = lax.pmax(jnp.max(scores, axis=-1), "seq")
    expo = jnp.exp(scores - top[..., None])
    total = jnp.sum(expo, axis=-1)
    summed = jnp.einsum("nght,tgd->nghd", expo.astype(BF16), values, preferred_element_type=F32)
    summed, total = lax.psum((summed, total), "seq")
    attended = (summed / total[..., None]).astype(BF16).reshape(new_count, -1)
    attended = route(attended, index, orders, True)
    return lax.psum(dot(attended, w_out), "tensor").astype(BF16)[None]


def solution(mesh):
    placed = (
        P("rep", ("seq", "tensor"), None, None),
        P("rep", None, "tensor", None),
        P(),
        P(),
        P("tensor", None, None),
        P("tensor", "seq"),
        P(),
    )
    square = mesh.shape["seq"] == 2 and mesh.shape["tensor"] == 4
    return jax.shard_map(
        square_shards if square else shards,
        mesh=mesh,
        in_specs=placed,
        out_specs=P("rep", None, "seq"),
        check_vma=False,
    )
```

```python
import itertools
import math

import jax
import jax.numpy as jnp
from jax import lax
from jax.experimental import pallas as pl
from jax.experimental.pallas import tpu as pltpu
from jax.sharding import PartitionSpec as P

BF16, F32 = jnp.bfloat16, jnp.float32
MIB = 1024 * 1024
IN_VMEM = pl.BlockSpec(memory_space=pltpu.VMEM)
IN_SMEM = pl.BlockSpec(memory_space=pltpu.SMEM)
IN_HBM = pl.BlockSpec(memory_space=pltpu.HBM)
COPIES = 8


def shape(dims, dtype):
    return jax.ShapeDtypeStruct(dims, dtype)


def call(body, name, outs, operands, vmem, scratch=(), smem_in=0, smem_out=False, hbm_in=0, cost=None):
    kept = len(operands) - hbm_in
    specs = [IN_SMEM] * smem_in + [IN_VMEM] * (kept - smem_in) + [IN_HBM] * hbm_in
    operands = [
        *operands[:kept],
        *(pltpu.with_memory_space_constraint(operand, pltpu.HBM) for operand in operands[kept:]),
    ]
    out_specs = [IN_VMEM] * len(outs)
    if smem_out:
        out_specs[-1] = IN_SMEM
    return pl.pallas_call(
        body,
        out_shape=outs,
        in_specs=specs,
        out_specs=out_specs,
        scratch_shapes=list(scratch),
        compiler_params=pltpu.CompilerParams(vmem_limit_bytes=vmem * MIB),
        cost_estimate=cost,
        name=name,
    )(*operands)


def cost(flops, moved, exps=0):
    return pl.CostEstimate(flops=int(flops), bytes_accessed=int(moved), transcendentals=int(exps))


def dot(a, b):
    return jnp.dot(a, b, preferred_element_type=F32)


def compress(rows, weight, gain):
    projected = dot(rows, weight)
    scale = lax.rsqrt(jnp.mean(projected * projected, axis=-1, keepdims=True) + 1e-06)
    return (projected * scale * gain.astype(F32)[None]).astype(BF16)


def order_index(replica_order, orders):
    table = jnp.array(orders, jnp.int32)
    match = jnp.all(table == replica_order[None], axis=1)
    return jnp.sum(jnp.where(match, lax.iota(jnp.int32, len(orders)), 0))


def route_pairs(order, back):
    return [(p, r) if back else (r, p) for r, p in enumerate(order)]


def route(value, index, orders, back):
    def branch(order):
        return lambda v: lax.ppermute(v, "rep", route_pairs(order, back))

    return lax.switch(index, [branch(o) for o in orders], value)


def shift(value, axis, hops):
    size = lax.axis_size(axis)
    return lax.ppermute(value, axis, [(i, (i + hops) % size) for i in range(size)])


def swap(value, axis, bit):
    pairs = [(i, i ^ bit) for i in range(lax.axis_size(axis))]
    return lax.ppermute(value, axis, pairs)


def cross(value, seq_core):
    pairs = [(i, i ^ (4 if i % 2 == seq_core else 2)) for i in range(8)]
    return lax.ppermute(value, ("seq", "tensor"), pairs)


def compress_kernel(chunks, *refs):
    (order_hbm, rows_hbm, weight_hbm, gain_hbm, query_hbm, latent_ref, half_ref, index_ref) = refs[:8]
    (order_ref, rows_ref, weight_ref, gain_ref, query_ref, wide, packed, sems) = refs[8:]
    tokens, groups, width = rows_ref.shape
    chunk = tokens // chunks
    copies = [pltpu.make_async_copy(order_hbm, order_ref, sems.at[0])]
    for i in range(chunks):
        at = pl.ds(i * chunk, chunk)
        copies.append(pltpu.make_async_copy(rows_hbm.at[0, at], rows_ref.at[at], sems.at[1 + i]))
    for group in range(groups):
        at = pl.ds(group * width, width)
        copies.append(
            pltpu.make_async_copy(weight_hbm.at[at], weight_ref.at[at], sems.at[1 + chunks + group])
        )
    copies.append(pltpu.make_async_copy(gain_hbm, gain_ref, sems.at[1 + chunks + groups]))
    copies.append(pltpu.make_async_copy(query_hbm.at[0], query_ref, sems.at[2 + chunks + groups]))
    for copy in copies:
        copy.start()

    copies[0].wait()
    count = order_ref.shape[0]
    index = 0
    for i in range(count):
        smaller = 0
        for j in range(i + 1, count):
            smaller = smaller + (order_ref[j] < order_ref[i]).astype(jnp.int32)
        index = index + smaller * math.factorial(count - 1 - i)
    index_ref[0] = index

    lanes = wide.shape[2]
    for i in range(chunks):
        copies[1 + i].wait()
        at = slice(i * chunk * groups, (i + 1) * chunk * groups)
        for part in range(wide.shape[0]):
            values = rows_ref[i * chunk : (i + 1) * chunk, :, part * lanes : (part + 1) * lanes]
            wide[part, at] = values.astype(F32).reshape(chunk * groups, lanes)
        for group in range(groups):
            for part in range(wide.shape[0]):
                start = group * width + part * lanes
                picked = wide[part, pl.ds(at.start + group, chunk, stride=groups), :]
                packed[i * chunk : (i + 1) * chunk, start : start + lanes] = picked.astype(BF16)
    for group in range(groups):
        copies[1 + chunks + group].wait()
    copies[1 + chunks + groups].wait()
    gain = gain_ref[...].astype(F32)[None]
    for i in range(chunks):
        at = slice(i * chunk, (i + 1) * chunk)
        projected = dot(packed[at], weight_ref[...])
        scale = lax.rsqrt(jnp.mean(projected * projected, axis=-1, keepdims=True) + 1e-06)
        latent_ref[at] = (projected * scale * gain).astype(BF16)

    copies[2 + chunks + groups].wait()
    new_count, heads, head_size = query_ref.shape
    query = query_ref[...].astype(F32)
    upper = lax.axis_index("seq") == 1
    query = jnp.where(upper, query[:, heads // 2 :], query[:, : heads // 2])
    half_ref[...] = query.reshape(half_ref.shape).astype(BF16)


def score_kernel(parts, *refs):
    latent_refs, (lift_ref, query_ref), (score_ref, value_ref, top_ref) = (
        refs[:parts],
        refs[parts : parts + 2],
        refs[parts + 2 :],
    )
    head_size = query_ref.shape[-1]
    lift = lift_ref[lax.axis_index("seq")]
    query = query_ref[...]
    top = None
    for part, latent_ref in enumerate(latent_refs):
        tokens = latent_ref.shape[0]
        at = slice(part * tokens, (part + 1) * tokens)
        lifted = dot(latent_ref[...], lift).astype(BF16)
        score = lax.dot_general(
            lifted[:, :head_size], query, (((1,), (1,)), ((), ())), preferred_element_type=F32
        )
        score_ref[at] = score
        value_ref[at] = lifted[:, head_size:]
        part_top = jnp.max(score, axis=0, keepdims=True)
        top = part_top if top is None else jnp.maximum(top, part_top)
    top_ref[...] = jnp.broadcast_to(top, top_ref.shape)


def weight_copies(own, core, weight_ref, held_ref, sems):
    depth, columns = held_ref.shape
    rows = depth // COPIES
    half = lax.axis_index("seq") if own else 1 - lax.axis_index("seq")
    first = 0 if core is None else core * columns
    copies = []
    for i in range(COPIES):
        start = pl.multiple_of(half * depth + i * rows, rows)
        source = weight_ref.at[pl.ds(start, rows), pl.ds(pl.multiple_of(first, columns), columns)]
        copies.append(
            pltpu.make_async_copy(source, held_ref.at[pl.ds(i * rows, rows)], sems.at[i])
        )
    return copies


def score_and_fetch_kernel(parts, *refs):
    *refs, held_ref, sems = refs
    copies = weight_copies(True, None, refs.pop(parts + 2), held_ref, sems)
    for copy in copies:
        copy.start()
    score_kernel(parts, *refs)
    for copy in copies:
        copy.wait()


def score_call(name, latents, lift, query, weight=None):
    tokens = sum(latent.shape[0] for latent in latents)
    rows, head_size = query.shape
    flops = 2 * tokens * (lift.shape[1] * lift.shape[2] + rows * head_size)
    outs = [shape((tokens, rows), F32), shape((tokens, head_size), BF16), shape((8, rows), F32)]
    operands = [*latents, lift, query]
    if weight is None:
        body = lambda *refs: score_kernel(len(latents), *refs)
        return call(body, name, outs, operands, 16, cost=cost(flops, 6 * tokens * rows))
    held = (weight.shape[0] // 2, weight.shape[1])
    return call(
        lambda *refs: score_and_fetch_kernel(len(latents), *refs),
        name,
        [*outs, pltpu.VMEM(held, weight.dtype)],
        [*operands, weight],
        16,
        scratch=[pltpu.SemaphoreType.DMA((COPIES,))],
        hbm_in=1,
        cost=cost(flops, 2 * held[0] * held[1]),
    )


def attend_kernel(new_count, block, *refs):
    (*score_refs, out_ref, turned) = refs
    triples = [score_refs[i : i + 3] for i in range(0, len(score_refs), 3)]
    head_size = triples[0][1].shape[-1]
    coef = head_size ** (-0.5) * math.log2(math.e)
    top = triples[0][2][:1]
    for triple in triples[1:]:
        top = jnp.maximum(top, triple[2][:1])
    total = jnp.zeros_like(top)
    summed = jnp.zeros((head_size, top.shape[1]), F32)
    for score_ref, value_ref, _ in triples:
        for start in range(0, score_ref.shape[0], block):
            at = slice(start, start + block)
            expo = jnp.exp2((score_ref[at] - top) * coef)
            total += jnp.sum(expo, axis=0, keepdims=True)
            summed += lax.dot_general(
                value_ref[at], expo.astype(BF16), (((0,), (0,)), ((), ())), preferred_element_type=F32
            )
    turned[...] = (summed / total).T
    heads = turned.shape[0] // new_count
    for head in range(heads):
        out_ref[:, head * head_size : (head + 1) * head_size] = turned[
            pl.ds(head, new_count, stride=heads), :
        ].astype(BF16)


def project_kernel(tile, rows_ref, weight_ref, all_ref, out_ref, sent_ref, kept_ref, sems):
    core = lax.axis_index("tensor") % 2
    copies = weight_copies(False, 1 - core, all_ref, sent_ref, sems.at[0])
    copies += weight_copies(False, core, all_ref, kept_ref, sems.at[1])
    for copy in copies:
        copy.start()
    rows = rows_ref[...]
    width = out_ref.shape[2]
    for part in range(out_ref.shape[0]):
        for column in range(0, width, tile):
            at = part * width + column
            out_ref[part, :, column : column + tile] = dot(
                rows, weight_ref[:, at : at + tile]
            )
    for copy in copies:
        copy.wait()


def project_more_kernel(tile, own, rows_ref, weight_ref, before_ref, *refs):
    out_ref = refs[-1]
    core = lax.axis_index("tensor") % 2
    part = core if own else 1 - core
    rows = rows_ref[...]
    width = out_ref.shape[1]
    for column in range(0, width, tile):
        value = before_ref[part, :, column : column + tile] + dot(
            rows, weight_ref[:, column : column + tile]
        )
        out_ref[:, column : column + tile] = value


def square_shards(key_value_rows, queries, w_comp, latent_gain, w_up, w_out, replica_order):
    orders = list(itertools.permutations(range(lax.axis_size("rep"))))
    tensor_at = lax.axis_index("tensor")
    core_at, chip_at = tensor_at % 2, tensor_at // 2
    _, new_count, heads, head_size = queries.shape
    _, tokens, all_groups, width = key_value_rows.shape
    latent_width = w_comp.shape[1]
    rows = heads // 2 * new_count

    chunks = 3 if tokens % 48 == 0 else 1
    latent, query, index = call(
        lambda *refs: compress_kernel(chunks, *refs),
        "compress",
        [shape((tokens, latent_width), BF16), shape((rows, head_size), BF16), shape((1,), jnp.int32)],
        [replica_order, key_value_rows, w_comp, latent_gain, queries],
        16,
        scratch=[
            pltpu.SMEM(replica_order.shape, jnp.int32),
            pltpu.VMEM(key_value_rows.shape[1:], BF16),
            pltpu.VMEM(w_comp.shape, BF16),
            pltpu.VMEM(latent_gain.shape, BF16),
            pltpu.VMEM(queries.shape[1:], BF16),
            pltpu.VMEM((width // 128, tokens * all_groups, 128), F32),
            pltpu.VMEM((tokens, all_groups * width), BF16),
            pltpu.SemaphoreType.DMA((3 + chunks + all_groups,)),
        ],
        hbm_in=5,
        smem_out=True,
        cost=cost(2 * tokens * all_groups * width * latent_width, 2 * tokens * all_groups * width),
    )

    def branch(order):
        def run(latent, query):
            return (
                cross(latent, 0),
                cross(latent, 1),
                swap(latent, "tensor", 1),
                lax.ppermute(query, "rep", route_pairs(order, False)),
            )

        return run

    near, far, beside, query = lax.switch(index[0], [branch(o) for o in orders], latent, query)
    corner = cross(near, 1)
    near_beside = swap(near, "tensor", 1)
    far_beside = swap(far, "tensor", 1)
    *first, held = score_call("score_chip", [latent, beside], w_up, query, w_out)
    *second, = score_call("score_next", [near, near_beside, far, far_beside], w_up, query)
    corner, first[2], second[2] = lax.optimization_barrier((corner, first[2], second[2]))
    corner_beside = swap(corner, "tensor", 1)
    third = score_call("score_corner", [corner, corner_beside], w_up, query)
    depth = rows // new_count * head_size
    (attended,) = call(
        lambda *refs: attend_kernel(new_count, tokens, *refs),
        "attend",
        [shape((new_count, depth), BF16)],
        [*first, *second, *third],
        16,
        scratch=[pltpu.VMEM((rows, head_size), F32)],
        cost=cost(2 * 8 * tokens * rows * head_size, 8 * tokens * rows * 4, 8 * tokens * rows),
    )

    attended_other = swap(attended, "seq", 1)
    columns = w_out.shape[1]
    tile = min(512, columns // 2)
    half_shape = (held.shape[0], held.shape[1] // 2)
    partial, held_sent, held_kept = call(
        lambda *refs: project_kernel(tile, *refs),
        "project",
        [shape((2, new_count, columns // 2), F32), *[pltpu.VMEM(half_shape, held.dtype)] * 2],
        [attended, held, w_out],
        12,
        scratch=[pltpu.SemaphoreType.DMA((2, COPIES))],
        hbm_in=1,
        cost=cost(2 * new_count * depth * columns, 2 * depth * columns),
    )

    def project_more(own, name, weight):
        return call(
            lambda *refs: project_more_kernel(tile, own, *refs),
            name,
            [shape((new_count, columns // 2), F32)],
            [attended_other, weight, partial],
            12,
            cost=cost(new_count * depth * columns, depth * columns),
        )[0]

    sent = swap(project_more(False, "project_sent", held_sent), "tensor", 1)
    half = project_more(True, "project_own", held_kept) + sent
    quarter = half.shape[1] // 2
    low, high = half[:, :quarter], half[:, quarter:]
    upper = chip_at == 1
    arrived = swap(jnp.where(upper, low, high), "tensor", 2)
    summed = (jnp.where(upper, high, low) + arrived).astype(BF16)

    summed = route(summed, index[0], orders, True)
    summed_across = swap(summed, "tensor", 2)
    half = jnp.where(
        upper,
        jnp.concatenate([summed_across, summed], axis=1),
        jnp.concatenate([summed, summed_across], axis=1),
    )
    half_beside = swap(half, "tensor", 1)
    whole = jnp.where(
        core_at == 1,
        jnp.concatenate([half_beside, half], axis=1),
        jnp.concatenate([half, half_beside], axis=1),
    )
    return whole[None]


def shards(key_value_rows, queries, w_comp, latent_gain, w_up, w_out, replica_order):
    orders = list(itertools.permutations(range(lax.axis_size("rep"))))
    index = order_index(replica_order, orders)
    query = route(queries[0], index, orders, False)
    rows = key_value_rows[0]
    latent = compress(rows.reshape(rows.shape[0], -1), w_comp, latent_gain)
    latent = lax.all_gather(latent, "tensor", axis=0, tiled=True)
    groups = w_up.shape[0]
    lifted = jnp.einsum("tf,gfy->tgy", latent, w_up, preferred_element_type=F32).astype(BF16)
    head_size = query.shape[-1]
    new_count = query.shape[0]
    keys = lifted[..., :head_size]
    values = lifted[..., head_size:]
    grouped_heads = query.reshape(new_count, groups, -1, head_size)
    scores = jnp.einsum(
        "nghd,tgd->nght", grouped_heads, keys, preferred_element_type=F32
    ) * head_size ** (-0.5)
    top = lax.pmax(jnp.max(scores, axis=-1), "seq")
    expo = jnp.exp(scores - top[..., None])
    total = jnp.sum(expo, axis=-1)
    summed = jnp.einsum("nght,tgd->nghd", expo.astype(BF16), values, preferred_element_type=F32)
    summed, total = lax.psum((summed, total), "seq")
    attended = (summed / total[..., None]).astype(BF16).reshape(new_count, -1)
    attended = route(attended, index, orders, True)
    return lax.psum(dot(attended, w_out), "tensor").astype(BF16)[None]


def solution(mesh):
    placed = (
        P("rep", ("seq", "tensor"), None, None),
        P("rep", None, "tensor", None),
        P(),
        P(),
        P("tensor", None, None),
        P("tensor", "seq"),
        P(),
    )
    square = mesh.shape["seq"] == 2 and mesh.shape["tensor"] == 4
    return jax.shard_map(
        square_shards if square else shards,
        mesh=mesh,
        in_specs=placed,
        out_specs=P("rep", None, "seq"),
        check_vma=False,
    )
```

```python
import itertools
import math

import jax
import jax.numpy as jnp
from jax import lax
from jax.experimental import pallas as pl
from jax.experimental.pallas import tpu as pltpu
from jax.sharding import PartitionSpec as P

BF16, F32 = jnp.bfloat16, jnp.float32
MIB = 1024 * 1024
IN_VMEM = pl.BlockSpec(memory_space=pltpu.VMEM)
IN_SMEM = pl.BlockSpec(memory_space=pltpu.SMEM)
IN_HBM = pl.BlockSpec(memory_space=pltpu.HBM)
COPIES = 8


def shape(dims, dtype):
    return jax.ShapeDtypeStruct(dims, dtype)


def call(body, name, outs, operands, vmem, scratch=(), smem_in=0, smem_out=False, hbm_in=0, cost=None):
    kept = len(operands) - hbm_in
    specs = [IN_SMEM] * smem_in + [IN_VMEM] * (kept - smem_in) + [IN_HBM] * hbm_in
    operands = [
        *operands[:kept],
        *(pltpu.with_memory_space_constraint(operand, pltpu.HBM) for operand in operands[kept:]),
    ]
    out_specs = [IN_VMEM] * len(outs)
    if smem_out:
        out_specs[-1] = IN_SMEM
    return pl.pallas_call(
        body,
        out_shape=outs,
        in_specs=specs,
        out_specs=out_specs,
        scratch_shapes=list(scratch),
        compiler_params=pltpu.CompilerParams(vmem_limit_bytes=vmem * MIB),
        cost_estimate=cost,
        name=name,
    )(*operands)


def cost(flops, moved, exps=0):
    return pl.CostEstimate(flops=int(flops), bytes_accessed=int(moved), transcendentals=int(exps))


def dot(a, b):
    return jnp.dot(a, b, preferred_element_type=F32)


def compress(rows, weight, gain):
    projected = dot(rows, weight)
    scale = lax.rsqrt(jnp.mean(projected * projected, axis=-1, keepdims=True) + 1e-06)
    return (projected * scale * gain.astype(F32)[None]).astype(BF16)


def order_index(replica_order, orders):
    table = jnp.array(orders, jnp.int32)
    match = jnp.all(table == replica_order[None], axis=1)
    return jnp.sum(jnp.where(match, lax.iota(jnp.int32, len(orders)), 0))


def route_pairs(order, back):
    return [(p, r) if back else (r, p) for r, p in enumerate(order)]


def route(value, index, orders, back):
    def branch(order):
        return lambda v: lax.ppermute(v, "rep", route_pairs(order, back))

    return lax.switch(index, [branch(o) for o in orders], value)


def shift(value, axis, hops):
    size = lax.axis_size(axis)
    return lax.ppermute(value, axis, [(i, (i + hops) % size) for i in range(size)])


def swap(value, axis, bit):
    pairs = [(i, i ^ bit) for i in range(lax.axis_size(axis))]
    return lax.ppermute(value, axis, pairs)


def cross(value, seq_core):
    pairs = [(i, i ^ (4 if i % 2 == seq_core else 2)) for i in range(8)]
    return lax.ppermute(value, ("seq", "tensor"), pairs)


def compress_kernel(chunks, *refs):
    (order_hbm, rows_hbm, weight_hbm, gain_hbm, query_hbm, latent_ref, half_ref, index_ref) = refs[:8]
    (order_ref, rows_ref, weight_ref, gain_ref, query_ref, wide, packed, sems) = refs[8:]
    tokens, groups, width = rows_ref.shape
    chunk = tokens // chunks
    copies = [pltpu.make_async_copy(order_hbm, order_ref, sems.at[0])]
    for i in range(chunks):
        at = pl.ds(i * chunk, chunk)
        copies.append(pltpu.make_async_copy(rows_hbm.at[0, at], rows_ref.at[at], sems.at[1 + i]))
    for group in range(groups):
        at = pl.ds(group * width, width)
        copies.append(
            pltpu.make_async_copy(weight_hbm.at[at], weight_ref.at[at], sems.at[1 + chunks + group])
        )
    copies.append(pltpu.make_async_copy(gain_hbm, gain_ref, sems.at[1 + chunks + groups]))
    copies.append(pltpu.make_async_copy(query_hbm.at[0], query_ref, sems.at[2 + chunks + groups]))
    for copy in copies:
        copy.start()

    copies[0].wait()
    count = order_ref.shape[0]
    index = 0
    for i in range(count):
        smaller = 0
        for j in range(i + 1, count):
            smaller = smaller + (order_ref[j] < order_ref[i]).astype(jnp.int32)
        index = index + smaller * math.factorial(count - 1 - i)
    index_ref[0] = index

    lanes = wide.shape[2]
    for i in range(chunks):
        copies[1 + i].wait()
        at = slice(i * chunk * groups, (i + 1) * chunk * groups)
        for part in range(wide.shape[0]):
            values = rows_ref[i * chunk : (i + 1) * chunk, :, part * lanes : (part + 1) * lanes]
            wide[part, at] = values.astype(F32).reshape(chunk * groups, lanes)
        for group in range(groups):
            for part in range(wide.shape[0]):
                start = group * width + part * lanes
                picked = wide[part, pl.ds(at.start + group, chunk, stride=groups), :]
                packed[i * chunk : (i + 1) * chunk, start : start + lanes] = picked.astype(BF16)
    for group in range(groups):
        copies[1 + chunks + group].wait()
    copies[1 + chunks + groups].wait()
    gain = gain_ref[...].astype(F32)[None]
    for i in range(chunks):
        at = slice(i * chunk, (i + 1) * chunk)
        projected = dot(packed[at], weight_ref[...])
        scale = lax.rsqrt(jnp.mean(projected * projected, axis=-1, keepdims=True) + 1e-06)
        latent_ref[at] = (projected * scale * gain).astype(BF16)

    copies[2 + chunks + groups].wait()
    new_count, heads, head_size = query_ref.shape
    query = query_ref[...].astype(F32)
    upper = lax.axis_index("seq") == 1
    query = jnp.where(upper, query[:, heads // 2 :], query[:, : heads // 2])
    half_ref[...] = query.reshape(half_ref.shape).astype(BF16)


def score_kernel(parts, *refs):
    latent_refs, (lift_ref, query_ref), (score_ref, value_ref, top_ref) = (
        refs[:parts],
        refs[parts : parts + 2],
        refs[parts + 2 :],
    )
    head_size = query_ref.shape[-1]
    lift = lift_ref[lax.axis_index("seq")]
    query = query_ref[...]
    top = None
    for part, latent_ref in enumerate(latent_refs):
        tokens = latent_ref.shape[0]
        at = slice(part * tokens, (part + 1) * tokens)
        lifted = dot(latent_ref[...], lift).astype(BF16)
        score = lax.dot_general(
            lifted[:, :head_size], query, (((1,), (1,)), ((), ())), preferred_element_type=F32
        )
        score_ref[at] = score
        value_ref[at] = lifted[:, head_size:]
        part_top = jnp.max(score, axis=0, keepdims=True)
        top = part_top if top is None else jnp.maximum(top, part_top)
    top_ref[...] = jnp.broadcast_to(top, top_ref.shape)


def fetch_kernel(weight_ref, own_ref, sent_ref, kept_ref, sems):
    core = lax.axis_index("tensor") % 2
    depth, columns = sent_ref.shape
    rows = depth // COPIES
    group = lax.axis_index("seq")
    copies = []
    for part, (held_ref, half, first) in enumerate(
        ((own_ref, group, 0), (sent_ref, 1 - group, 1 - core), (kept_ref, 1 - group, core))
    ):
        first = pl.multiple_of(first * columns, columns)
        for i in range(COPIES):
            start = pl.multiple_of(half * depth + i * rows, rows)
            source = weight_ref.at[pl.ds(start, rows), pl.ds(first, held_ref.shape[1])]
            target = held_ref.at[pl.ds(i * rows, rows)]
            copies.append(pltpu.make_async_copy(source, target, sems.at[part, i]))
    for copy in copies:
        copy.start()
    for copy in copies:
        copy.wait()


def score_call(name, latents, lift, query):
    tokens = sum(latent.shape[0] for latent in latents)
    rows, head_size = query.shape
    flops = 2 * tokens * (lift.shape[1] * lift.shape[2] + rows * head_size)
    return call(
        lambda *refs: score_kernel(len(latents), *refs),
        name,
        [shape((tokens, rows), F32), shape((tokens, head_size), BF16), shape((8, rows), F32)],
        [*latents, lift, query],
        16,
        cost=cost(flops, 6 * tokens * rows),
    )


def attend_kernel(new_count, block, *refs):
    (*score_refs, out_ref, turned) = refs
    triples = [score_refs[i : i + 3] for i in range(0, len(score_refs), 3)]
    head_size = triples[0][1].shape[-1]
    coef = head_size ** (-0.5) * math.log2(math.e)
    top = triples[0][2][:1]
    for triple in triples[1:]:
        top = jnp.maximum(top, triple[2][:1])
    total = jnp.zeros_like(top)
    summed = jnp.zeros((head_size, top.shape[1]), F32)
    for score_ref, value_ref, _ in triples:
        for start in range(0, score_ref.shape[0], block):
            at = slice(start, start + block)
            expo = jnp.exp2((score_ref[at] - top) * coef)
            total += jnp.sum(expo, axis=0, keepdims=True)
            summed += lax.dot_general(
                value_ref[at], expo.astype(BF16), (((0,), (0,)), ((), ())), preferred_element_type=F32
            )
    turned[...] = (summed / total).T
    heads = turned.shape[0] // new_count
    for head in range(heads):
        out_ref[:, head * head_size : (head + 1) * head_size] = turned[
            pl.ds(head, new_count, stride=heads), :
        ].astype(BF16)


def project_kernel(tile, rows_ref, weight_ref, out_ref):
    rows = rows_ref[...]
    width = out_ref.shape[2]
    for part in range(out_ref.shape[0]):
        for column in range(0, width, tile):
            at = part * width + column
            out_ref[part, :, column : column + tile] = dot(
                rows, weight_ref[:, at : at + tile]
            )


def project_more_kernel(tile, own, rows_ref, weight_ref, before_ref, *refs):
    out_ref = refs[-1]
    core = lax.axis_index("tensor") % 2
    part = core if own else 1 - core
    rows = rows_ref[...]
    width = out_ref.shape[1]
    for column in range(0, width, tile):
        value = before_ref[part, :, column : column + tile] + dot(
            rows, weight_ref[:, column : column + tile]
        )
        out_ref[:, column : column + tile] = value


def square_shards(key_value_rows, queries, w_comp, latent_gain, w_up, w_out, replica_order):
    orders = list(itertools.permutations(range(lax.axis_size("rep"))))
    tensor_at = lax.axis_index("tensor")
    core_at, chip_at = tensor_at % 2, tensor_at // 2
    _, new_count, heads, head_size = queries.shape
    _, tokens, all_groups, width = key_value_rows.shape
    latent_width = w_comp.shape[1]
    rows = heads // 2 * new_count

    chunks = 3 if tokens % 48 == 0 else 1
    latent, query, index = call(
        lambda *refs: compress_kernel(chunks, *refs),
        "compress",
        [shape((tokens, latent_width), BF16), shape((rows, head_size), BF16), shape((1,), jnp.int32)],
        [replica_order, key_value_rows, w_comp, latent_gain, queries],
        16,
        scratch=[
            pltpu.SMEM(replica_order.shape, jnp.int32),
            pltpu.VMEM(key_value_rows.shape[1:], BF16),
            pltpu.VMEM(w_comp.shape, BF16),
            pltpu.VMEM(latent_gain.shape, BF16),
            pltpu.VMEM(queries.shape[1:], BF16),
            pltpu.VMEM((width // 128, tokens * all_groups, 128), F32),
            pltpu.VMEM((tokens, all_groups * width), BF16),
            pltpu.SemaphoreType.DMA((3 + chunks + all_groups,)),
        ],
        hbm_in=5,
        smem_out=True,
        cost=cost(2 * tokens * all_groups * width * latent_width, 2 * tokens * all_groups * width),
    )

    near = cross(latent, 0)
    far = cross(latent, 1)
    query = route(query, index[0], orders, False)
    weight, query = lax.optimization_barrier((w_out, query))
    held_shape = (w_out.shape[0] // 2, w_out.shape[1])
    half_shape = (held_shape[0], held_shape[1] // 2)
    held, held_sent, held_kept = call(
        fetch_kernel,
        "fetch",
        [pltpu.VMEM(dims, w_out.dtype) for dims in (held_shape, half_shape, half_shape)],
        [weight],
        4,
        scratch=[pltpu.SemaphoreType.DMA((3, COPIES))],
        hbm_in=1,
        cost=cost(0, 0),
    )
    near, far, held = lax.optimization_barrier((near, far, held))
    corner = cross(near, 1)
    beside = swap(latent, "tensor", 1)
    near_beside = swap(near, "tensor", 1)
    far_beside = swap(far, "tensor", 1)
    first = score_call("score_chip", [latent, beside], w_up, query)
    second = score_call("score_next", [near, near_beside, far, far_beside], w_up, query)
    first, second = list(first), list(second)
    corner, first[2], second[2] = lax.optimization_barrier((corner, first[2], second[2]))
    corner_beside = swap(corner, "tensor", 1)
    third = score_call("score_corner", [corner, corner_beside], w_up, query)
    depth = rows // new_count * head_size
    (attended,) = call(
        lambda *refs: attend_kernel(new_count, tokens, *refs),
        "attend",
        [shape((new_count, depth), BF16)],
        [*first, *second, *third],
        16,
        scratch=[pltpu.VMEM((rows, head_size), F32)],
        cost=cost(2 * 8 * tokens * rows * head_size, 8 * tokens * rows * 4, 8 * tokens * rows),
    )

    attended_other = swap(attended, "seq", 1)
    columns = w_out.shape[1]
    tile = min(512, columns // 2)
    (partial,) = call(
        lambda *refs: project_kernel(tile, *refs),
        "project",
        [shape((2, new_count, columns // 2), F32)],
        [attended, held],
        12,
        cost=cost(2 * new_count * depth * columns, 2 * depth * columns),
    )

    def project_more(own, name, weight):
        return call(
            lambda *refs: project_more_kernel(tile, own, *refs),
            name,
            [shape((new_count, columns // 2), F32)],
            [attended_other, weight, partial],
            12,
            cost=cost(new_count * depth * columns, depth * columns),
        )[0]

    sent = swap(project_more(False, "project_sent", held_sent), "tensor", 1)
    half = project_more(True, "project_own", held_kept) + sent
    quarter = half.shape[1] // 2
    low, high = half[:, :quarter], half[:, quarter:]
    upper = chip_at == 1
    arrived = swap(jnp.where(upper, low, high), "tensor", 2)
    summed = (jnp.where(upper, high, low) + arrived).astype(BF16)

    summed = route(summed, index[0], orders, True)
    summed_across = swap(summed, "tensor", 2)
    half = jnp.where(
        upper,
        jnp.concatenate([summed_across, summed], axis=1),
        jnp.concatenate([summed, summed_across], axis=1),
    )
    half_beside = swap(half, "tensor", 1)
    whole = jnp.where(
        core_at == 1,
        jnp.concatenate([half_beside, half], axis=1),
        jnp.concatenate([half, half_beside], axis=1),
    )
    return whole[None]


def shards(key_value_rows, queries, w_comp, latent_gain, w_up, w_out, replica_order):
    orders = list(itertools.permutations(range(lax.axis_size("rep"))))
    index = order_index(replica_order, orders)
    query = route(queries[0], index, orders, False)
    rows = key_value_rows[0]
    latent = compress(rows.reshape(rows.shape[0], -1), w_comp, latent_gain)
    latent = lax.all_gather(latent, "tensor", axis=0, tiled=True)
    groups = w_up.shape[0]
    lifted = jnp.einsum("tf,gfy->tgy", latent, w_up, preferred_element_type=F32).astype(BF16)
    head_size = query.shape[-1]
    new_count = query.shape[0]
    keys = lifted[..., :head_size]
    values = lifted[..., head_size:]
    grouped_heads = query.reshape(new_count, groups, -1, head_size)
    scores = jnp.einsum(
        "nghd,tgd->nght", grouped_heads, keys, preferred_element_type=F32
    ) * head_size ** (-0.5)
    top = lax.pmax(jnp.max(scores, axis=-1), "seq")
    expo = jnp.exp(scores - top[..., None])
    total = jnp.sum(expo, axis=-1)
    summed = jnp.einsum("nght,tgd->nghd", expo.astype(BF16), values, preferred_element_type=F32)
    summed, total = lax.psum((summed, total), "seq")
    attended = (summed / total[..., None]).astype(BF16).reshape(new_count, -1)
    attended = route(attended, index, orders, True)
    return lax.psum(dot(attended, w_out), "tensor").astype(BF16)[None]


def solution(mesh):
    placed = (
        P("rep", ("seq", "tensor"), None, None),
        P("rep", None, "tensor", None),
        P(),
        P(),
        P("tensor", None, None),
        P("tensor", "seq"),
        P(),
    )
    square = mesh.shape["seq"] == 2 and mesh.shape["tensor"] == 4
    return jax.shard_map(
        square_shards if square else shards,
        mesh=mesh,
        in_specs=placed,
        out_specs=P("rep", None, "seq"),
        check_vma=False,
    )
```

```python
import itertools
import math

import jax
import jax.numpy as jnp
from jax import lax
from jax.experimental import pallas as pl
from jax.experimental.pallas import tpu as pltpu
from jax.sharding import PartitionSpec as P

BF16, F32 = jnp.bfloat16, jnp.float32
MIB = 1024 * 1024
IN_VMEM = pl.BlockSpec(memory_space=pltpu.VMEM)
IN_SMEM = pl.BlockSpec(memory_space=pltpu.SMEM)
IN_HBM = pl.BlockSpec(memory_space=pltpu.HBM)
COPIES = 8


def shape(dims, dtype):
    return jax.ShapeDtypeStruct(dims, dtype)


def call(body, name, outs, operands, vmem, scratch=(), smem_in=0, smem_out=0, hbm_in=0, cost=None):
    kept = len(operands) - hbm_in
    specs = [IN_SMEM] * smem_in + [IN_VMEM] * (kept - smem_in) + [IN_HBM] * hbm_in
    operands = [
        *operands[:kept],
        *(pltpu.with_memory_space_constraint(operand, pltpu.HBM) for operand in operands[kept:]),
    ]
    out_specs = [IN_VMEM] * (len(outs) - smem_out) + [IN_SMEM] * smem_out
    return pl.pallas_call(
        body,
        out_shape=outs,
        in_specs=specs,
        out_specs=out_specs,
        scratch_shapes=list(scratch),
        compiler_params=pltpu.CompilerParams(vmem_limit_bytes=vmem * MIB),
        cost_estimate=cost,
        name=name,
    )(*operands)


def cost(flops, moved, exps=0):
    return pl.CostEstimate(flops=int(flops), bytes_accessed=int(moved), transcendentals=int(exps))


def dot(a, b):
    return jnp.dot(a, b, preferred_element_type=F32)


def compress(rows, weight, gain):
    projected = dot(rows, weight)
    scale = lax.rsqrt(jnp.mean(projected * projected, axis=-1, keepdims=True) + 1e-06)
    return (projected * scale * gain.astype(F32)[None]).astype(BF16)


def order_index(replica_order, orders):
    table = jnp.array(orders, jnp.int32)
    match = jnp.all(table == replica_order[None], axis=1)
    return jnp.sum(jnp.where(match, lax.iota(jnp.int32, len(orders)), 0))


def route_pairs(order, back):
    return [(p, r) if back else (r, p) for r, p in enumerate(order)]


def route(value, index, orders, back):
    def branch(order):
        return lambda v: lax.ppermute(v, "rep", route_pairs(order, back))

    return lax.switch(index, [branch(o) for o in orders], value)


def shift(value, axis, hops):
    size = lax.axis_size(axis)
    return lax.ppermute(value, axis, [(i, (i + hops) % size) for i in range(size)])


def swap(value, axis, bit):
    pairs = [(i, i ^ bit) for i in range(lax.axis_size(axis))]
    return lax.ppermute(value, axis, pairs)


def cross(value, seq_core):
    pairs = [(i, i ^ (4 if i % 2 == seq_core else 2)) for i in range(8)]
    return lax.ppermute(value, ("seq", "tensor"), pairs)


def compress_kernel(chunks, *refs):
    (order_hbm, rows_hbm, weight_hbm, gain_hbm, query_hbm, latent_ref, half_ref, index_ref, picks_ref) = refs[:9]
    (order_ref, rows_ref, weight_ref, gain_ref, query_ref, wide, packed, sems) = refs[9:]
    tokens, groups, width = rows_ref.shape
    chunk = tokens // chunks
    copies = [pltpu.make_async_copy(order_hbm, order_ref, sems.at[0])]
    for i in range(chunks):
        at = pl.ds(i * chunk, chunk)
        copies.append(pltpu.make_async_copy(rows_hbm.at[0, at], rows_ref.at[at], sems.at[1 + i]))
    for group in range(groups):
        at = pl.ds(group * width, width)
        copies.append(
            pltpu.make_async_copy(weight_hbm.at[at], weight_ref.at[at], sems.at[1 + chunks + group])
        )
    copies.append(pltpu.make_async_copy(gain_hbm, gain_ref, sems.at[1 + chunks + groups]))
    copies.append(pltpu.make_async_copy(query_hbm.at[0], query_ref, sems.at[2 + chunks + groups]))
    for copy in copies:
        copy.start()

    copies[0].wait()
    count = order_ref.shape[0]
    here = lax.axis_index("rep")
    index, wanted, wanted_beside = 0, 0, 0
    for i in range(count):
        wanted = jnp.where(order_ref[i] == here, i, wanted)
        wanted_beside = jnp.where(order_ref[i] == (here ^ 1), i, wanted_beside)
        smaller = 0
        for j in range(i + 1, count):
            smaller = smaller + (order_ref[j] < order_ref[i]).astype(jnp.int32)
        index = index + smaller * math.factorial(count - 1 - i)
    index_ref[0] = index
    picks_ref[0] = (wanted_beside == (here ^ 2)).astype(jnp.int32)
    picks_ref[1] = jnp.where(wanted == here, 0, jnp.where(wanted == (here ^ 2), 1, 2))

    lanes = wide.shape[2]
    for i in range(chunks):
        copies[1 + i].wait()
        at = slice(i * chunk * groups, (i + 1) * chunk * groups)
        for part in range(wide.shape[0]):
            values = rows_ref[i * chunk : (i + 1) * chunk, :, part * lanes : (part + 1) * lanes]
            wide[part, at] = values.astype(F32).reshape(chunk * groups, lanes)
        for group in range(groups):
            for part in range(wide.shape[0]):
                start = group * width + part * lanes
                picked = wide[part, pl.ds(at.start + group, chunk, stride=groups), :]
                packed[i * chunk : (i + 1) * chunk, start : start + lanes] = picked.astype(BF16)
    for group in range(groups):
        copies[1 + chunks + group].wait()
    copies[1 + chunks + groups].wait()
    gain = gain_ref[...].astype(F32)[None]
    for i in range(chunks):
        at = slice(i * chunk, (i + 1) * chunk)
        projected = dot(packed[at], weight_ref[...])
        scale = lax.rsqrt(jnp.mean(projected * projected, axis=-1, keepdims=True) + 1e-06)
        latent_ref[at] = (projected * scale * gain).astype(BF16)

    copies[2 + chunks + groups].wait()
    new_count, heads, head_size = query_ref.shape
    query = query_ref[...].astype(F32)
    upper = lax.axis_index("seq") == 1
    query = jnp.where(upper, query[:, heads // 2 :], query[:, : heads // 2])
    half_ref[...] = query.reshape(half_ref.shape).astype(BF16)


def score_kernel(parts, *refs):
    latent_refs, (lift_ref, query_ref), (score_ref, value_ref, top_ref) = (
        refs[:parts],
        refs[parts : parts + 2],
        refs[parts + 2 :],
    )
    head_size = query_ref.shape[-1]
    lift = lift_ref[lax.axis_index("seq")]
    query = query_ref[...]
    top = None
    for part, latent_ref in enumerate(latent_refs):
        tokens = latent_ref.shape[0]
        at = slice(part * tokens, (part + 1) * tokens)
        lifted = dot(latent_ref[...], lift).astype(BF16)
        score = lax.dot_general(
            lifted[:, :head_size], query, (((1,), (1,)), ((), ())), preferred_element_type=F32
        )
        score_ref[at] = score
        value_ref[at] = lifted[:, head_size:]
        part_top = jnp.max(score, axis=0, keepdims=True)
        top = part_top if top is None else jnp.maximum(top, part_top)
    top_ref[...] = jnp.broadcast_to(top, top_ref.shape)


def fetch_kernel(weight_ref, own_ref, sent_ref, kept_ref, sems):
    core = lax.axis_index("tensor") % 2
    depth, columns = sent_ref.shape
    rows = depth // COPIES
    group = lax.axis_index("seq")
    copies = []
    for part, (held_ref, half, first) in enumerate(
        ((own_ref, group, 0), (sent_ref, 1 - group, 1 - core), (kept_ref, 1 - group, core))
    ):
        first = pl.multiple_of(first * columns, columns)
        for i in range(COPIES):
            start = pl.multiple_of(half * depth + i * rows, rows)
            source = weight_ref.at[pl.ds(start, rows), pl.ds(first, held_ref.shape[1])]
            target = held_ref.at[pl.ds(i * rows, rows)]
            copies.append(pltpu.make_async_copy(source, target, sems.at[part, i]))
    for copy in copies:
        copy.start()
    for copy in copies:
        copy.wait()


def choose(pick, refs, out_ref):
    for i, ref in enumerate(refs):

        @pl.when(pick == i)
        def _():
            out_ref[...] = ref[...]


def pass_kernel(picks_ref, own_ref, second_ref, out_ref):
    choose(picks_ref[0], (own_ref, second_ref), out_ref)


def choose_and_score_kernel(parts, picks_ref, *refs):
    *refs, score_ref, value_ref, top_ref, query_ref = refs
    choose(picks_ref[1], refs[parts + 1 :], query_ref)
    score_kernel(parts, *refs[: parts + 1], query_ref, score_ref, value_ref, top_ref)


def score_call(name, latents, lift, query, picks=None):
    queries = [query] if picks is None else query
    tokens = sum(latent.shape[0] for latent in latents)
    rows, head_size = queries[0].shape
    flops = 2 * tokens * (lift.shape[1] * lift.shape[2] + rows * head_size)
    outs = [shape((tokens, rows), F32), shape((tokens, head_size), BF16), shape((8, rows), F32)]
    operands = [*latents, lift, *queries]
    estimate = cost(flops, 6 * tokens * rows)
    if picks is None:
        body = lambda *refs: score_kernel(len(latents), *refs)
        return call(body, name, outs, operands, 16, cost=estimate)
    body = lambda *refs: choose_and_score_kernel(len(latents), *refs)
    outs.append(shape((rows, head_size), BF16))
    return call(body, name, outs, [picks, *operands], 16, smem_in=1, cost=estimate)


def attend_kernel(new_count, block, *refs):
    (*score_refs, out_ref, turned) = refs
    triples = [score_refs[i : i + 3] for i in range(0, len(score_refs), 3)]
    head_size = triples[0][1].shape[-1]
    coef = head_size ** (-0.5) * math.log2(math.e)
    top = triples[0][2][:1]
    for triple in triples[1:]:
        top = jnp.maximum(top, triple[2][:1])
    total = jnp.zeros_like(top)
    summed = jnp.zeros((head_size, top.shape[1]), F32)
    for score_ref, value_ref, _ in triples:
        for start in range(0, score_ref.shape[0], block):
            at = slice(start, start + block)
            expo = jnp.exp2((score_ref[at] - top) * coef)
            total += jnp.sum(expo, axis=0, keepdims=True)
            summed += lax.dot_general(
                value_ref[at], expo.astype(BF16), (((0,), (0,)), ((), ())), preferred_element_type=F32
            )
    turned[...] = (summed / total).T
    heads = turned.shape[0] // new_count
    for head in range(heads):
        out_ref[:, head * head_size : (head + 1) * head_size] = turned[
            pl.ds(head, new_count, stride=heads), :
        ].astype(BF16)


def project_kernel(tile, rows_ref, weight_ref, out_ref):
    rows = rows_ref[...]
    width = out_ref.shape[2]
    for part in range(out_ref.shape[0]):
        for column in range(0, width, tile):
            at = part * width + column
            out_ref[part, :, column : column + tile] = dot(
                rows, weight_ref[:, at : at + tile]
            )


def project_more_kernel(tile, own, rows_ref, weight_ref, before_ref, *refs):
    out_ref = refs[-1]
    core = lax.axis_index("tensor") % 2
    part = core if own else 1 - core
    rows = rows_ref[...]
    width = out_ref.shape[1]
    for column in range(0, width, tile):
        value = before_ref[part, :, column : column + tile] + dot(
            rows, weight_ref[:, column : column + tile]
        )
        out_ref[:, column : column + tile] = value


def split_kernel(own_ref, other_ref, given_ref, kept_ref):
    chip = lax.axis_index("tensor") // 2
    width = given_ref.shape[1]
    for out_ref, part in ((given_ref, 1 - chip), (kept_ref, chip)):
        at = pl.ds(pl.multiple_of(part * width, width), width)
        out_ref[...] = own_ref[:, at] + other_ref[:, at]


def sum_kernel(kept_ref, arrived_ref, out_ref):
    out_ref[...] = (kept_ref[...] + arrived_ref[...]).astype(out_ref.dtype)


def join_kernel(*refs):
    *quarters, out_ref, sems = refs
    here = lax.axis_index("tensor")
    core, chip = here % 2, here // 2
    width = quarters[0].shape[1]
    copies = []
    for i, quarter in enumerate(quarters):
        at = 2 * (core if i < 2 else 1 - core) + (1 - chip if i % 2 else chip)
        at = pl.ds(pl.multiple_of(at * width, width), width)
        copies.append(pltpu.make_async_copy(quarter, out_ref.at[0, :, at], sems.at[i]))
    for copy in copies:
        copy.start()
    for copy in copies:
        copy.wait()


def square_shards(key_value_rows, queries, w_comp, latent_gain, w_up, w_out, replica_order):
    orders = list(itertools.permutations(range(lax.axis_size("rep"))))
    _, new_count, heads, head_size = queries.shape
    _, tokens, all_groups, width = key_value_rows.shape
    latent_width = w_comp.shape[1]
    rows = heads // 2 * new_count

    chunks = 3 if tokens % 48 == 0 else 1
    latent, query, index, picks = call(
        lambda *refs: compress_kernel(chunks, *refs),
        "compress",
        [shape((tokens, latent_width), BF16), shape((rows, head_size), BF16), *[shape((n,), jnp.int32) for n in (1, 2)]],
        [replica_order, key_value_rows, w_comp, latent_gain, queries],
        16,
        scratch=[
            pltpu.SMEM(replica_order.shape, jnp.int32),
            pltpu.VMEM(key_value_rows.shape[1:], BF16),
            pltpu.VMEM(w_comp.shape, BF16),
            pltpu.VMEM(latent_gain.shape, BF16),
            pltpu.VMEM(queries.shape[1:], BF16),
            pltpu.VMEM((width // 128, tokens * all_groups, 128), F32),
            pltpu.VMEM((tokens, all_groups * width), BF16),
            pltpu.SemaphoreType.DMA((3 + chunks + all_groups,)),
        ],
        hbm_in=5,
        smem_out=2,
        cost=cost(2 * tokens * all_groups * width * latent_width, 2 * tokens * all_groups * width),
    )

    near = cross(latent, 0)
    far = cross(latent, 1)
    second_query = swap(query, "rep", 2)
    held_shape = (w_out.shape[0] // 2, w_out.shape[1])
    half_shape = (held_shape[0], held_shape[1] // 2)
    held, held_sent, held_kept = call(
        fetch_kernel,
        "fetch",
        [pltpu.VMEM(dims, w_out.dtype) for dims in (held_shape, half_shape, half_shape)],
        [w_out],
        4,
        scratch=[pltpu.SemaphoreType.DMA((3, COPIES))],
        hbm_in=1,
        cost=cost(0, 0),
    )
    near, far, second_query, held = lax.optimization_barrier((near, far, second_query, held))
    (passed,) = call(
        pass_kernel,
        "pass",
        [shape(query.shape, query.dtype)],
        [picks, query, second_query],
        4,
        smem_in=1,
        cost=cost(0, 0),
    )
    passed = swap(passed, "rep", 1)
    corner = cross(near, 1)
    beside = swap(latent, "tensor", 1)
    near_beside = swap(near, "tensor", 1)
    far_beside = swap(far, "tensor", 1)
    choices = [query, second_query, passed]
    *first, query = score_call("score_chip", [latent, beside], w_up, choices, picks)
    second = score_call("score_next", [near, near_beside, far, far_beside], w_up, query)
    first, second = list(first), list(second)
    corner, first[2], second[2] = lax.optimization_barrier((corner, first[2], second[2]))
    corner_beside = swap(corner, "tensor", 1)
    third = score_call("score_corner", [corner, corner_beside], w_up, query)
    depth = rows // new_count * head_size
    (attended,) = call(
        lambda *refs: attend_kernel(new_count, tokens, *refs),
        "attend",
        [shape((new_count, depth), BF16)],
        [*first, *second, *third],
        16,
        scratch=[pltpu.VMEM((rows, head_size), F32)],
        cost=cost(2 * 8 * tokens * rows * head_size, 8 * tokens * rows * 4, 8 * tokens * rows),
    )

    attended_other = swap(attended, "seq", 1)
    columns = w_out.shape[1]
    tile = min(512, columns // 2)
    (partial,) = call(
        lambda *refs: project_kernel(tile, *refs),
        "project",
        [shape((2, new_count, columns // 2), F32)],
        [attended, held],
        12,
        cost=cost(2 * new_count * depth * columns, 2 * depth * columns),
    )

    def project_more(own, name, weight):
        return call(
            lambda *refs: project_more_kernel(tile, own, *refs),
            name,
            [shape((new_count, columns // 2), F32)],
            [attended_other, weight, partial],
            12,
            cost=cost(new_count * depth * columns, depth * columns),
        )[0]

    sent = swap(project_more(False, "project_sent", held_sent), "tensor", 1)
    kept = project_more(True, "project_own", held_kept)
    quarter_shape = (new_count, columns // 4)
    given, kept = call(split_kernel, "split", [shape(quarter_shape, F32)] * 2, [kept, sent], 8)
    given = swap(given, "tensor", 2)
    (own,) = call(sum_kernel, "sum", [shape(quarter_shape, BF16)], [kept, given], 8)
    own = route(own, index[0], orders, True)
    across = swap(own, "tensor", 2)
    quarters = [own, across, swap(own, "tensor", 1), swap(across, "tensor", 1)]
    return pl.pallas_call(
        join_kernel,
        out_shape=shape((1, new_count, columns), BF16),
        in_specs=[IN_VMEM] * 4,
        out_specs=IN_HBM,
        scratch_shapes=[pltpu.SemaphoreType.DMA((4,))],
        compiler_params=pltpu.CompilerParams(vmem_limit_bytes=4 * MIB),
        name="join",
    )(*quarters)


def shards(key_value_rows, queries, w_comp, latent_gain, w_up, w_out, replica_order):
    orders = list(itertools.permutations(range(lax.axis_size("rep"))))
    index = order_index(replica_order, orders)
    query = route(queries[0], index, orders, False)
    rows = key_value_rows[0]
    latent = compress(rows.reshape(rows.shape[0], -1), w_comp, latent_gain)
    latent = lax.all_gather(latent, "tensor", axis=0, tiled=True)
    groups = w_up.shape[0]
    lifted = jnp.einsum("tf,gfy->tgy", latent, w_up, preferred_element_type=F32).astype(BF16)
    head_size = query.shape[-1]
    new_count = query.shape[0]
    keys = lifted[..., :head_size]
    values = lifted[..., head_size:]
    grouped_heads = query.reshape(new_count, groups, -1, head_size)
    scores = jnp.einsum(
        "nghd,tgd->nght", grouped_heads, keys, preferred_element_type=F32
    ) * head_size ** (-0.5)
    top = lax.pmax(jnp.max(scores, axis=-1), "seq")
    expo = jnp.exp(scores - top[..., None])
    total = jnp.sum(expo, axis=-1)
    summed = jnp.einsum("nght,tgd->nghd", expo.astype(BF16), values, preferred_element_type=F32)
    summed, total = lax.psum((summed, total), "seq")
    attended = (summed / total[..., None]).astype(BF16).reshape(new_count, -1)
    attended = route(attended, index, orders, True)
    return lax.psum(dot(attended, w_out), "tensor").astype(BF16)[None]


def solution(mesh):
    placed = (
        P("rep", ("seq", "tensor"), None, None),
        P("rep", None, "tensor", None),
        P(),
        P(),
        P("tensor", None, None),
        P("tensor", "seq"),
        P(),
    )
    square = all(mesh.shape[axis] == size for axis, size in (("seq", 2), ("rep", 4), ("tensor", 4)))
    return jax.shard_map(
        square_shards if square else shards,
        mesh=mesh,
        in_specs=placed,
        out_specs=P("rep", None, "seq"),
        check_vma=False,
    )
```

```python
import itertools
import math

import jax
import jax.numpy as jnp
from jax import lax
from jax.experimental import pallas as pl
from jax.experimental.pallas import tpu as pltpu
from jax.sharding import PartitionSpec as P

BF16, F32 = jnp.bfloat16, jnp.float32
MIB = 1024 * 1024
IN_VMEM = pl.BlockSpec(memory_space=pltpu.VMEM)
IN_SMEM = pl.BlockSpec(memory_space=pltpu.SMEM)
IN_HBM = pl.BlockSpec(memory_space=pltpu.HBM)
COPIES = 8


def shape(dims, dtype):
    return jax.ShapeDtypeStruct(dims, dtype)


def call(body, name, outs, operands, vmem, scratch=(), smem_in=0, smem_out=0, hbm_in=0, cost=None):
    kept = len(operands) - hbm_in
    specs = [IN_SMEM] * smem_in + [IN_VMEM] * (kept - smem_in) + [IN_HBM] * hbm_in
    operands = [
        *operands[:kept],
        *(pltpu.with_memory_space_constraint(operand, pltpu.HBM) for operand in operands[kept:]),
    ]
    out_specs = [IN_VMEM] * (len(outs) - smem_out) + [IN_SMEM] * smem_out
    return pl.pallas_call(
        body,
        out_shape=outs,
        in_specs=specs,
        out_specs=out_specs,
        scratch_shapes=list(scratch),
        compiler_params=pltpu.CompilerParams(vmem_limit_bytes=vmem * MIB),
        cost_estimate=cost,
        name=name,
    )(*operands)


def cost(flops, moved, exps=0):
    return pl.CostEstimate(flops=int(flops), bytes_accessed=int(moved), transcendentals=int(exps))


def dot(a, b):
    return jnp.dot(a, b, preferred_element_type=F32)


def compress(rows, weight, gain):
    projected = dot(rows, weight)
    scale = lax.rsqrt(jnp.mean(projected * projected, axis=-1, keepdims=True) + 1e-06)
    return (projected * scale * gain.astype(F32)[None]).astype(BF16)


def order_index(replica_order, orders):
    table = jnp.array(orders, jnp.int32)
    match = jnp.all(table == replica_order[None], axis=1)
    return jnp.sum(jnp.where(match, lax.iota(jnp.int32, len(orders)), 0))


def route_pairs(order, back):
    return [(p, r) if back else (r, p) for r, p in enumerate(order)]


def route(value, index, orders, back):
    def branch(order):
        return lambda v: lax.ppermute(v, "rep", route_pairs(order, back))

    return lax.switch(index, [branch(o) for o in orders], value)


def shift(value, axis, hops):
    size = lax.axis_size(axis)
    return lax.ppermute(value, axis, [(i, (i + hops) % size) for i in range(size)])


def swap(value, axis, bit):
    pairs = [(i, i ^ bit) for i in range(lax.axis_size(axis))]
    return lax.ppermute(value, axis, pairs)


def cross(value, seq_core):
    pairs = [(i, i ^ (4 if i % 2 == seq_core else 2)) for i in range(8)]
    return lax.ppermute(value, ("seq", "tensor"), pairs)


def compress_kernel(chunks, *refs):
    (order_hbm, rows_hbm, weight_hbm, gain_hbm, query_hbm, latent_ref, half_ref, index_ref, pick_ref) = refs[:9]
    (order_ref, rows_ref, weight_ref, gain_ref, query_ref, wide, packed, sems) = refs[9:]
    tokens, groups, width = rows_ref.shape
    chunk = tokens // chunks
    copies = [pltpu.make_async_copy(order_hbm, order_ref, sems.at[0])]
    for i in range(chunks):
        at = pl.ds(i * chunk, chunk)
        copies.append(pltpu.make_async_copy(rows_hbm.at[0, at], rows_ref.at[at], sems.at[1 + i]))
    for group in range(groups):
        at = pl.ds(group * width, width)
        copies.append(
            pltpu.make_async_copy(weight_hbm.at[at], weight_ref.at[at], sems.at[1 + chunks + group])
        )
    copies.append(pltpu.make_async_copy(gain_hbm, gain_ref, sems.at[1 + chunks + groups]))
    copies.append(pltpu.make_async_copy(query_hbm.at[0], query_ref, sems.at[2 + chunks + groups]))
    for copy in copies:
        copy.start()

    copies[0].wait()
    count = order_ref.shape[0]
    here = lax.axis_index("rep")
    index, wanted, wanted_beside = 0, 0, 0
    for i in range(count):
        wanted = jnp.where(order_ref[i] == here, i, wanted)
        wanted_beside = jnp.where(order_ref[i] == (here ^ 1), i, wanted_beside)
        smaller = 0
        for j in range(i + 1, count):
            smaller = smaller + (order_ref[j] < order_ref[i]).astype(jnp.int32)
        index = index + smaller * math.factorial(count - 1 - i)
    index_ref[0] = index
    pick_ref[0] = (wanted_beside == (here ^ 2)).astype(jnp.int32)
    pick_ref[1] = jnp.where(wanted == here, 0, jnp.where(wanted == (here ^ 2), 1, 2))

    lanes = wide.shape[2]
    for i in range(chunks):
        copies[1 + i].wait()
        at = slice(i * chunk * groups, (i + 1) * chunk * groups)
        for part in range(wide.shape[0]):
            values = rows_ref[i * chunk : (i + 1) * chunk, :, part * lanes : (part + 1) * lanes]
            wide[part, at] = values.astype(F32).reshape(chunk * groups, lanes)
        for group in range(groups):
            for part in range(wide.shape[0]):
                start = group * width + part * lanes
                picked = wide[part, pl.ds(at.start + group, chunk, stride=groups), :]
                packed[i * chunk : (i + 1) * chunk, start : start + lanes] = picked.astype(BF16)
    for group in range(groups):
        copies[1 + chunks + group].wait()
    copies[1 + chunks + groups].wait()
    gain = gain_ref[...].astype(F32)[None]
    for i in range(chunks):
        at = slice(i * chunk, (i + 1) * chunk)
        projected = dot(packed[at], weight_ref[...])
        scale = lax.rsqrt(jnp.mean(projected * projected, axis=-1, keepdims=True) + 1e-06)
        latent_ref[at] = (projected * scale * gain).astype(BF16)

    copies[2 + chunks + groups].wait()
    new_count, heads, head_size = query_ref.shape
    query = query_ref[...].astype(F32)
    upper = lax.axis_index("seq") == 1
    query = jnp.where(upper, query[:, heads // 2 :], query[:, : heads // 2])
    half_ref[...] = query.reshape(half_ref.shape).astype(BF16)


def score_kernel(parts, *refs):
    latent_refs, (lift_ref, query_ref), (score_ref, value_ref, top_ref) = (
        refs[:parts],
        refs[parts : parts + 2],
        refs[parts + 2 :],
    )
    head_size = query_ref.shape[-1]
    lift = lift_ref[lax.axis_index("seq")]
    query = query_ref[...]
    top = None
    for part, latent_ref in enumerate(latent_refs):
        tokens = latent_ref.shape[0]
        at = slice(part * tokens, (part + 1) * tokens)
        lifted = dot(latent_ref[...], lift).astype(BF16)
        score = lax.dot_general(
            lifted[:, :head_size], query, (((1,), (1,)), ((), ())), preferred_element_type=F32
        )
        score_ref[at] = score
        value_ref[at] = lifted[:, head_size:]
        part_top = jnp.max(score, axis=0, keepdims=True)
        top = part_top if top is None else jnp.maximum(top, part_top)
    top_ref[...] = jnp.broadcast_to(top, top_ref.shape)


def fetch_kernel(weight_ref, own_ref, sent_ref, kept_ref, sems):
    core = lax.axis_index("tensor") % 2
    depth, columns = sent_ref.shape
    rows = depth // COPIES
    group = lax.axis_index("seq")
    copies = []
    for part, (held_ref, half, first) in enumerate(
        ((own_ref, group, 0), (sent_ref, 1 - group, 1 - core), (kept_ref, 1 - group, core))
    ):
        first = pl.multiple_of(first * columns, columns)
        for i in range(COPIES):
            start = pl.multiple_of(half * depth + i * rows, rows)
            source = weight_ref.at[pl.ds(start, rows), pl.ds(first, held_ref.shape[1])]
            target = held_ref.at[pl.ds(i * rows, rows)]
            copies.append(pltpu.make_async_copy(source, target, sems.at[part, i]))
    for copy in copies:
        copy.start()
    for copy in copies:
        copy.wait()


def fetch(weight):
    depth, columns = weight.shape[0] // 2, weight.shape[1]
    return call(
        fetch_kernel,
        "fetch",
        [pltpu.VMEM((depth, width), weight.dtype) for width in (columns, columns // 2, columns // 2)],
        [weight],
        4,
        scratch=[pltpu.SemaphoreType.DMA((3, COPIES))],
        hbm_in=1,
        cost=cost(0, 0),
    )


def choose(pick, refs, out_ref):
    for i, ref in enumerate(refs):

        @pl.when(pick == i)
        def _():
            out_ref[...] = ref[...]


def pass_kernel(pick_ref, own_ref, second_ref, out_ref):
    choose(pick_ref[0], (own_ref, second_ref), out_ref)


def choose_and_score_kernel(parts, pick_ref, *refs):
    *refs, score_ref, value_ref, top_ref, query_ref = refs
    choose(pick_ref[1], refs[parts + 1 :], query_ref)
    score_kernel(parts, *refs[: parts + 1], query_ref, score_ref, value_ref, top_ref)


def score_call(name, latents, lift, query, pick=None):
    queries = [query] if pick is None else query
    tokens = sum(latent.shape[0] for latent in latents)
    rows, head_size = queries[0].shape
    outs = [shape((tokens, rows), F32), shape((tokens, head_size), BF16), shape((8, rows), F32)]
    operands = [*latents, lift, *queries]
    estimate = cost(0, 0)
    if pick is None:
        body = lambda *refs: score_kernel(len(latents), *refs)
        return call(body, name, outs, operands, 16, cost=estimate)
    body = lambda *refs: choose_and_score_kernel(len(latents), *refs)
    outs.append(shape((rows, head_size), BF16))
    return call(body, name, outs, [pick, *operands], 16, smem_in=1, cost=estimate)


def attend_kernel(new_count, block, *refs):
    (*score_refs, out_ref, turned) = refs
    triples = [score_refs[i : i + 3] for i in range(0, len(score_refs), 3)]
    head_size = triples[0][1].shape[-1]
    coef = head_size ** (-0.5) * math.log2(math.e)
    top = triples[0][2][:1]
    for triple in triples[1:]:
        top = jnp.maximum(top, triple[2][:1])
    total = jnp.zeros_like(top)
    summed = jnp.zeros((head_size, top.shape[1]), F32)
    for score_ref, value_ref, _ in triples:
        for start in range(0, score_ref.shape[0], block):
            at = slice(start, start + block)
            expo = jnp.exp2((score_ref[at] - top) * coef)
            total += jnp.sum(expo, axis=0, keepdims=True)
            summed += lax.dot_general(
                value_ref[at], expo.astype(BF16), (((0,), (0,)), ((), ())), preferred_element_type=F32
            )
    turned[...] = (summed / total).T
    heads = turned.shape[0] // new_count
    for head in range(heads):
        out_ref[:, head * head_size : (head + 1) * head_size] = turned[
            pl.ds(head, new_count, stride=heads), :
        ].astype(BF16)


def project_kernel(tile, rows_ref, weight_ref, out_ref):
    rows = rows_ref[...]
    width = out_ref.shape[2]
    for part in range(out_ref.shape[0]):
        for column in range(0, width, tile):
            at = part * width + column
            out_ref[part, :, column : column + tile] = dot(
                rows, weight_ref[:, at : at + tile]
            )


def project_more_kernel(tile, own, rows_ref, weight_ref, before_ref, *refs):
    out_ref = refs[-1]
    core = lax.axis_index("tensor") % 2
    part = core if own else 1 - core
    rows = rows_ref[...]
    width = out_ref.shape[1]
    for column in range(0, width, tile):
        value = before_ref[part, :, column : column + tile] + dot(
            rows, weight_ref[:, column : column + tile]
        )
        out_ref[:, column : column + tile] = value


def split_kernel(own_ref, other_ref, given_ref, kept_ref):
    chip = lax.axis_index("tensor") // 2
    width = given_ref.shape[1]
    for out_ref, part in ((given_ref, 1 - chip), (kept_ref, chip)):
        at = pl.ds(pl.multiple_of(part * width, width), width)
        out_ref[...] = own_ref[:, at] + other_ref[:, at]


def sum_kernel(kept_ref, arrived_ref, out_ref):
    out_ref[...] = (kept_ref[...] + arrived_ref[...]).astype(out_ref.dtype)


def join_kernel(places, *refs):
    quarters = refs[: len(places)]
    out_ref, sems = refs[-2:]
    here = lax.axis_index("tensor")
    core, chip = here % 2, here // 2
    width = quarters[0].shape[1]
    copies = []
    for i, place in enumerate(places):
        at = 2 * (1 - core if place // 2 else core) + (1 - chip if place % 2 else chip)
        at = pl.ds(pl.multiple_of(at * width, width), width)
        copies.append(pltpu.make_async_copy(quarters[i], out_ref.at[0, :, at], sems.at[i]))
    for copy in copies:
        copy.start()
    for copy in copies:
        copy.wait()


def join(name, places, quarters, before=None):
    new_count, width = quarters[0].shape
    return pl.pallas_call(
        lambda *refs: join_kernel(places, *refs),
        out_shape=shape((1, new_count, 4 * width), BF16),
        in_specs=[IN_VMEM] * len(places) + ([] if before is None else [IN_HBM]),
        out_specs=IN_HBM,
        scratch_shapes=[pltpu.SemaphoreType.DMA((len(places),))],
        input_output_aliases={} if before is None else {len(places): 0},
        compiler_params=pltpu.CompilerParams(vmem_limit_bytes=4 * MIB),
        name=name,
    )(*quarters, *([] if before is None else [before]))


def square_shards(key_value_rows, queries, w_comp, latent_gain, w_up, w_out, replica_order):
    orders = list(itertools.permutations(range(lax.axis_size("rep"))))
    _, new_count, heads, head_size = queries.shape
    _, tokens, all_groups, width = key_value_rows.shape
    latent_width = w_comp.shape[1]
    rows = heads // 2 * new_count

    chunks = 3 if tokens % 48 == 0 else 1
    latent, query, index, pick = call(
        lambda *refs: compress_kernel(chunks, *refs),
        "compress",
        [shape((tokens, latent_width), BF16), shape((rows, head_size), BF16), *[shape((n,), jnp.int32) for n in (1, 2)]],
        [replica_order, key_value_rows, w_comp, latent_gain, queries],
        16,
        scratch=[
            pltpu.SMEM(replica_order.shape, jnp.int32),
            pltpu.VMEM(key_value_rows.shape[1:], BF16),
            pltpu.VMEM(w_comp.shape, BF16),
            pltpu.VMEM(latent_gain.shape, BF16),
            pltpu.VMEM(queries.shape[1:], BF16),
            pltpu.VMEM((width // 128, tokens * all_groups, 128), F32),
            pltpu.VMEM((tokens, all_groups * width), BF16),
            pltpu.SemaphoreType.DMA((3 + chunks + all_groups,)),
        ],
        hbm_in=5,
        smem_out=2,
        cost=cost(2 * tokens * all_groups * width * latent_width, 2 * tokens * all_groups * width),
    )

    near = cross(latent, 0)
    far = cross(latent, 1)
    second_query = swap(query, "rep", 2)
    held, held_sent, held_kept = fetch(w_out)
    near, far, second_query, held = lax.optimization_barrier((near, far, second_query, held))
    corner = cross(near, 1)
    (passed,) = call(
        pass_kernel,
        "pass",
        [shape(query.shape, query.dtype)],
        [pick, query, second_query],
        4,
        smem_in=1,
        cost=cost(0, 0),
    )
    passed, given, near = lax.optimization_barrier((passed, latent, near))
    passed = swap(passed, "rep", 1)
    beside = swap(given, "tensor", 1)
    near_beside = swap(near, "tensor", 1)
    passed, far, corner = lax.optimization_barrier((passed, far, corner))
    far_beside = swap(far, "tensor", 1)
    corner_beside = swap(corner, "tensor", 1)
    choices = [query, second_query, passed]
    *first, query = score_call("score_chip", [latent, beside], w_up, choices, pick)
    second = score_call("score_next", [near, near_beside, far, far_beside], w_up, query)
    third = score_call("score_corner", [corner, corner_beside], w_up, query)
    depth = rows // new_count * head_size
    (attended,) = call(
        lambda *refs: attend_kernel(new_count, tokens, *refs),
        "attend",
        [shape((new_count, depth), BF16)],
        [*first, *second, *third],
        16,
        scratch=[pltpu.VMEM((rows, head_size), F32)],
        cost=cost(2 * 8 * tokens * rows * head_size, 8 * tokens * rows * 4, 8 * tokens * rows),
    )

    attended_other = swap(attended, "seq", 1)
    columns = w_out.shape[1]
    tile = min(512, columns // 2)
    (partial,) = call(
        lambda *refs: project_kernel(tile, *refs),
        "project",
        [shape((2, new_count, columns // 2), F32)],
        [attended, held],
        12,
        cost=cost(2 * new_count * depth * columns, 2 * depth * columns),
    )

    def project_more(own, name, weight):
        return call(
            lambda *refs: project_more_kernel(tile, own, *refs),
            name,
            [shape((new_count, columns // 2), F32)],
            [attended_other, weight, partial],
            12,
            cost=cost(new_count * depth * columns, depth * columns),
        )[0]

    sent = swap(project_more(False, "project_sent", held_sent), "tensor", 1)
    kept = project_more(True, "project_own", held_kept)
    quarter_shape = (new_count, columns // 4)
    given, kept = call(split_kernel, "split", [shape(quarter_shape, F32)] * 2, [kept, sent], 8)
    given = swap(given, "tensor", 2)
    (own,) = call(sum_kernel, "sum", [shape(quarter_shape, BF16)], [kept, given], 8)
    own = route(own, index[0], orders, True)
    across = swap(own, "tensor", 2)
    beside, across_beside = swap(own, "tensor", 1), swap(across, "tensor", 1)
    joined = join("join", (0, 1, 2), [own, across, beside])
    return join("join_last", (3,), [across_beside], joined)


def shards(key_value_rows, queries, w_comp, latent_gain, w_up, w_out, replica_order):
    orders = list(itertools.permutations(range(lax.axis_size("rep"))))
    index = order_index(replica_order, orders)
    query = route(queries[0], index, orders, False)
    rows = key_value_rows[0]
    latent = compress(rows.reshape(rows.shape[0], -1), w_comp, latent_gain)
    latent = lax.all_gather(latent, "tensor", axis=0, tiled=True)
    groups = w_up.shape[0]
    lifted = jnp.einsum("tf,gfy->tgy", latent, w_up, preferred_element_type=F32).astype(BF16)
    head_size = query.shape[-1]
    new_count = query.shape[0]
    keys = lifted[..., :head_size]
    values = lifted[..., head_size:]
    grouped_heads = query.reshape(new_count, groups, -1, head_size)
    scores = jnp.einsum(
        "nghd,tgd->nght", grouped_heads, keys, preferred_element_type=F32
    ) * head_size ** (-0.5)
    top = lax.pmax(jnp.max(scores, axis=-1), "seq")
    expo = jnp.exp(scores - top[..., None])
    total = jnp.sum(expo, axis=-1)
    summed = jnp.einsum("nght,tgd->nghd", expo.astype(BF16), values, preferred_element_type=F32)
    summed, total = lax.psum((summed, total), "seq")
    attended = (summed / total[..., None]).astype(BF16).reshape(new_count, -1)
    attended = route(attended, index, orders, True)
    return lax.psum(dot(attended, w_out), "tensor").astype(BF16)[None]


def solution(mesh):
    placed = (
        P("rep", ("seq", "tensor"), None, None),
        P("rep", None, "tensor", None),
        P(),
        P(),
        P("tensor", None, None),
        P("tensor", "seq"),
        P(),
    )
    square = all(mesh.shape[axis] == size for axis, size in (("seq", 2), ("rep", 4), ("tensor", 4)))
    return jax.shard_map(
        square_shards if square else shards,
        mesh=mesh,
        in_specs=placed,
        out_specs=P("rep", None, "seq"),
        check_vma=False,
    )
```

```python
import itertools
import math

import jax
import jax.numpy as jnp
from jax import lax
from jax.experimental import pallas as pl
from jax.experimental.pallas import tpu as pltpu
from jax.sharding import PartitionSpec as P

BF16, F32 = jnp.bfloat16, jnp.float32
MIB = 1024 * 1024
IN_VMEM = pl.BlockSpec(memory_space=pltpu.VMEM)
IN_SMEM = pl.BlockSpec(memory_space=pltpu.SMEM)
IN_HBM = pl.BlockSpec(memory_space=pltpu.HBM)
COPIES = 8
PARTS = 2


def shape(dims, dtype):
    return jax.ShapeDtypeStruct(dims, dtype)


def call(body, name, outs, operands, vmem, scratch=(), smem_in=0, smem_out=0, hbm_in=0, cost=None):
    kept = len(operands) - hbm_in
    specs = [IN_SMEM] * smem_in + [IN_VMEM] * (kept - smem_in) + [IN_HBM] * hbm_in
    operands = [
        *operands[:kept],
        *(pltpu.with_memory_space_constraint(operand, pltpu.HBM) for operand in operands[kept:]),
    ]
    out_specs = [IN_VMEM] * (len(outs) - smem_out) + [IN_SMEM] * smem_out
    return pl.pallas_call(
        body,
        out_shape=outs,
        in_specs=specs,
        out_specs=out_specs,
        scratch_shapes=list(scratch),
        compiler_params=pltpu.CompilerParams(vmem_limit_bytes=vmem * MIB),
        cost_estimate=cost,
        name=name,
    )(*operands)


def cost(flops, moved, exps=0):
    return pl.CostEstimate(flops=int(flops), bytes_accessed=int(moved), transcendentals=int(exps))


def dot(a, b):
    return jnp.dot(a, b, preferred_element_type=F32)


def compress(rows, weight, gain):
    projected = dot(rows, weight)
    scale = lax.rsqrt(jnp.mean(projected * projected, axis=-1, keepdims=True) + 1e-06)
    return (projected * scale * gain.astype(F32)[None]).astype(BF16)


def order_index(replica_order, orders):
    table = jnp.array(orders, jnp.int32)
    match = jnp.all(table == replica_order[None], axis=1)
    return jnp.sum(jnp.where(match, lax.iota(jnp.int32, len(orders)), 0))


def route_pairs(order, back):
    return [(p, r) if back else (r, p) for r, p in enumerate(order)]


def route(value, index, orders, back):
    def branch(order):
        return lambda v: lax.ppermute(v, "rep", route_pairs(order, back))

    return lax.switch(index, [branch(o) for o in orders], value)


def shift(value, axis, hops):
    size = lax.axis_size(axis)
    return lax.ppermute(value, axis, [(i, (i + hops) % size) for i in range(size)])


def swap(value, axis, bit):
    pairs = [(i, i ^ bit) for i in range(lax.axis_size(axis))]
    return lax.ppermute(value, axis, pairs)


def cross(value, seq_core):
    pairs = [(i, i ^ (4 if i % 2 == seq_core else 2)) for i in range(8)]
    return lax.ppermute(value, ("seq", "tensor"), pairs)


def compress_kernel(chunks, *refs):
    (order_hbm, rows_hbm, weight_hbm, gain_hbm, query_hbm, latent_ref, half_ref, index_ref, pick_ref) = refs[:9]
    (order_ref, rows_ref, weight_ref, gain_ref, query_ref, wide, packed, sems) = refs[9:]
    tokens, groups, width = rows_ref.shape
    chunk = tokens // chunks
    copies = [pltpu.make_async_copy(order_hbm, order_ref, sems.at[0])]
    for i in range(chunks):
        at = pl.ds(i * chunk, chunk)
        copies.append(pltpu.make_async_copy(rows_hbm.at[0, at], rows_ref.at[at], sems.at[1 + i]))
    for group in range(groups):
        at = pl.ds(group * width, width)
        copies.append(
            pltpu.make_async_copy(weight_hbm.at[at], weight_ref.at[at], sems.at[1 + chunks + group])
        )
    copies.append(pltpu.make_async_copy(gain_hbm, gain_ref, sems.at[1 + chunks + groups]))
    copies.append(pltpu.make_async_copy(query_hbm.at[0], query_ref, sems.at[2 + chunks + groups]))
    for copy in copies:
        copy.start()

    copies[0].wait()
    count = order_ref.shape[0]
    here = lax.axis_index("rep")
    index, wanted, wanted_beside = 0, 0, 0
    for i in range(count):
        wanted = jnp.where(order_ref[i] == here, i, wanted)
        wanted_beside = jnp.where(order_ref[i] == (here ^ 1), i, wanted_beside)
        smaller = 0
        for j in range(i + 1, count):
            smaller = smaller + (order_ref[j] < order_ref[i]).astype(jnp.int32)
        index = index + smaller * math.factorial(count - 1 - i)
    index_ref[0] = index
    pick_ref[0] = (wanted_beside == (here ^ 2)).astype(jnp.int32)
    pick_ref[1] = jnp.where(wanted == here, 0, jnp.where(wanted == (here ^ 2), 1, 2))

    lanes = wide.shape[2]
    for i in range(chunks):
        copies[1 + i].wait()
        at = slice(i * chunk * groups, (i + 1) * chunk * groups)
        for part in range(wide.shape[0]):
            values = rows_ref[i * chunk : (i + 1) * chunk, :, part * lanes : (part + 1) * lanes]
            wide[part, at] = values.astype(F32).reshape(chunk * groups, lanes)
        for group in range(groups):
            for part in range(wide.shape[0]):
                start = group * width + part * lanes
                picked = wide[part, pl.ds(at.start + group, chunk, stride=groups), :]
                packed[i * chunk : (i + 1) * chunk, start : start + lanes] = picked.astype(BF16)
    for group in range(groups):
        copies[1 + chunks + group].wait()
    copies[1 + chunks + groups].wait()
    gain = gain_ref[...].astype(F32)[None]
    for i in range(chunks):
        at = slice(i * chunk, (i + 1) * chunk)
        projected = dot(packed[at], weight_ref[...])
        scale = lax.rsqrt(jnp.mean(projected * projected, axis=-1, keepdims=True) + 1e-06)
        latent_ref[at] = (projected * scale * gain).astype(BF16)

    copies[2 + chunks + groups].wait()
    new_count, heads, head_size = query_ref.shape
    query = query_ref[...].astype(F32)
    upper = lax.axis_index("seq") == 1
    query = jnp.where(upper, query[:, heads // 2 :], query[:, : heads // 2])
    half_ref[...] = query.reshape(half_ref.shape).astype(BF16)


def score_kernel(parts, *refs):
    latent_refs, (lift_ref, query_ref), (score_ref, value_ref, top_ref) = (
        refs[:parts],
        refs[parts : parts + 2],
        refs[parts + 2 :],
    )
    head_size = query_ref.shape[-1]
    lift = lift_ref[lax.axis_index("seq")]
    query = query_ref[...]
    top = None
    for part, latent_ref in enumerate(latent_refs):
        tokens = latent_ref.shape[0]
        at = slice(part * tokens, (part + 1) * tokens)
        lifted = dot(latent_ref[...], lift).astype(BF16)
        score = lax.dot_general(
            lifted[:, :head_size], query, (((1,), (1,)), ((), ())), preferred_element_type=F32
        )
        score_ref[at] = score
        value_ref[at] = lifted[:, head_size:]
        part_top = jnp.max(score, axis=0, keepdims=True)
        top = part_top if top is None else jnp.maximum(top, part_top)
    top_ref[...] = jnp.broadcast_to(top, top_ref.shape)


def fetch_kernel(weight_ref, own_ref, sent_ref, kept_ref, sems):
    core = lax.axis_index("tensor") % 2
    depth, columns = sent_ref.shape
    rows = depth // COPIES
    group = lax.axis_index("seq")
    copies = []
    for part, (held_ref, half, first) in enumerate(
        ((own_ref, group, 0), (sent_ref, 1 - group, 1 - core), (kept_ref, 1 - group, core))
    ):
        first = pl.multiple_of(first * columns, columns)
        for i in range(COPIES):
            start = pl.multiple_of(half * depth + i * rows, rows)
            source = weight_ref.at[pl.ds(start, rows), pl.ds(first, held_ref.shape[1])]
            target = held_ref.at[pl.ds(i * rows, rows)]
            copies.append(pltpu.make_async_copy(source, target, sems.at[part, i]))
    for copy in copies:
        copy.start()
    for copy in copies:
        copy.wait()


def fetch(weight):
    depth, columns = weight.shape[0] // 2, weight.shape[1]
    return call(
        fetch_kernel,
        "fetch",
        [pltpu.VMEM((depth, width), weight.dtype) for width in (columns, columns // 2, columns // 2)],
        [weight],
        4,
        scratch=[pltpu.SemaphoreType.DMA((3, COPIES))],
        hbm_in=1,
        cost=cost(0, 0),
    )


def choose(pick, refs, out_ref):
    for i, ref in enumerate(refs):

        @pl.when(pick == i)
        def _():
            out_ref[...] = ref[...]


def pass_kernel(pick_ref, own_ref, second_ref, out_ref):
    choose(pick_ref[0], (own_ref, second_ref), out_ref)


def choose_and_score_kernel(parts, pick_ref, *refs):
    *refs, score_ref, value_ref, top_ref, query_ref = refs
    choose(pick_ref[1], refs[parts + 1 :], query_ref)
    score_kernel(parts, *refs[: parts + 1], query_ref, score_ref, value_ref, top_ref)


def score_call(name, latents, lift, query, pick=None):
    queries = [query] if pick is None else query
    tokens = sum(latent.shape[0] for latent in latents)
    rows, head_size = queries[0].shape
    outs = [shape((tokens, rows), F32), shape((tokens, head_size), BF16), shape((8, rows), F32)]
    operands = [*latents, lift, *queries]
    estimate = cost(0, 0)
    if pick is None:
        body = lambda *refs: score_kernel(len(latents), *refs)
        return call(body, name, outs, operands, 16, cost=estimate)
    body = lambda *refs: choose_and_score_kernel(len(latents), *refs)
    outs.append(shape((rows, head_size), BF16))
    return call(body, name, outs, [pick, *operands], 16, smem_in=1, cost=estimate)


def attend_kernel(part, block, *refs):
    (*score_refs, out_ref, turned) = refs
    new_count = out_ref.shape[0]
    rows = slice(part * turned.shape[0], (part + 1) * turned.shape[0])
    triples = [score_refs[i : i + 3] for i in range(0, len(score_refs), 3)]
    head_size = triples[0][1].shape[-1]
    coef = head_size ** (-0.5) * math.log2(math.e)
    top = triples[0][2][:1, rows]
    for triple in triples[1:]:
        top = jnp.maximum(top, triple[2][:1, rows])
    total = jnp.zeros_like(top)
    summed = jnp.zeros((head_size, top.shape[1]), F32)
    for score_ref, value_ref, _ in triples:
        for start in range(0, score_ref.shape[0], block):
            at = slice(start, start + block)
            expo = jnp.exp2((score_ref[at, rows] - top) * coef)
            total += jnp.sum(expo, axis=0, keepdims=True)
            summed += lax.dot_general(
                value_ref[at], expo.astype(BF16), (((0,), (0,)), ((), ())), preferred_element_type=F32
            )
    turned[...] = (summed / total).T
    heads = turned.shape[0] // new_count
    for head in range(heads):
        out_ref[:, head * head_size : (head + 1) * head_size] = turned[
            pl.ds(head, new_count, stride=heads), :
        ].astype(BF16)


def project_kernel(tile, *refs):
    *row_refs, weight_ref, out_ref = refs
    rows = jnp.concatenate([ref[...] for ref in row_refs], axis=0)
    width = out_ref.shape[2]
    for part in range(out_ref.shape[0]):
        for column in range(0, width, tile):
            at = part * width + column
            out_ref[part, :, column : column + tile] = dot(
                rows, weight_ref[:, at : at + tile]
            )


def project_more_kernel(tile, own, *refs):
    *row_refs, weight_ref, before_ref, out_ref = refs
    core = lax.axis_index("tensor") % 2
    part = core if own else 1 - core
    rows = jnp.concatenate([ref[...] for ref in row_refs], axis=0)
    width = out_ref.shape[1]
    for column in range(0, width, tile):
        value = before_ref[part, :, column : column + tile] + dot(
            rows, weight_ref[:, column : column + tile]
        )
        out_ref[:, column : column + tile] = value


def split_kernel(own_ref, other_ref, *refs):
    chip = lax.axis_index("tensor") // 2
    width = refs[0].shape[1]
    for i, out_ref in enumerate(refs):
        part = chip if i >= PARTS else 1 - chip
        at = pl.ds(pl.multiple_of((part * PARTS + i % PARTS) * width, width), width)
        out_ref[...] = own_ref[:, at] + other_ref[:, at]


def sum_kernel(kept_ref, arrived_ref, out_ref):
    out_ref[...] = (kept_ref[...] + arrived_ref[...]).astype(out_ref.dtype)


def join_kernel(places, *refs):
    pieces = refs[: len(places)]
    out_ref, sems = refs[-2:]
    here = lax.axis_index("tensor")
    core, chip = here % 2, here // 2
    width = pieces[0].shape[1]
    copies = []
    for i, (place, part) in enumerate(places):
        at = 2 * (1 - core if place // 2 else core) + (1 - chip if place % 2 else chip)
        at = pl.ds(pl.multiple_of((at * PARTS + part) * width, width), width)
        copies.append(pltpu.make_async_copy(pieces[i], out_ref.at[0, :, at], sems.at[i]))
    for copy in copies:
        copy.start()
    for copy in copies:
        copy.wait()


def join(places, pieces, before):
    new_count, width = pieces[0].shape
    return pl.pallas_call(
        lambda *refs: join_kernel(places, *refs),
        out_shape=shape((1, new_count, 4 * PARTS * width), BF16),
        in_specs=[IN_VMEM] * len(places) + ([] if before is None else [IN_HBM]),
        out_specs=IN_HBM,
        scratch_shapes=[pltpu.SemaphoreType.DMA((len(places),))],
        input_output_aliases={} if before is None else {len(places): 0},
        compiler_params=pltpu.CompilerParams(vmem_limit_bytes=4 * MIB),
        name="join",
    )(*pieces, *([] if before is None else [before]))


def square_shards(key_value_rows, queries, w_comp, latent_gain, w_up, w_out, replica_order):
    orders = list(itertools.permutations(range(lax.axis_size("rep"))))
    _, new_count, heads, head_size = queries.shape
    _, tokens, all_groups, width = key_value_rows.shape
    latent_width = w_comp.shape[1]
    rows = heads // 2 * new_count

    chunks = 3 if tokens % 48 == 0 else 1
    latent, query, index, pick = call(
        lambda *refs: compress_kernel(chunks, *refs),
        "compress",
        [shape((tokens, latent_width), BF16), shape((rows, head_size), BF16), *[shape((n,), jnp.int32) for n in (1, 2)]],
        [replica_order, key_value_rows, w_comp, latent_gain, queries],
        16,
        scratch=[
            pltpu.SMEM(replica_order.shape, jnp.int32),
            pltpu.VMEM(key_value_rows.shape[1:], BF16),
            pltpu.VMEM(w_comp.shape, BF16),
            pltpu.VMEM(latent_gain.shape, BF16),
            pltpu.VMEM(queries.shape[1:], BF16),
            pltpu.VMEM((width // 128, tokens * all_groups, 128), F32),
            pltpu.VMEM((tokens, all_groups * width), BF16),
            pltpu.SemaphoreType.DMA((3 + chunks + all_groups,)),
        ],
        hbm_in=5,
        smem_out=2,
        cost=cost(0, 0),
    )

    near = cross(latent, 0)
    far = cross(latent, 1)
    second_query = swap(query, "rep", 2)
    held, held_sent, held_kept = fetch(w_out)
    near, far, second_query, held = lax.optimization_barrier((near, far, second_query, held))
    corner = cross(near, 1)
    (passed,) = call(
        pass_kernel,
        "pass",
        [shape(query.shape, query.dtype)],
        [pick, query, second_query],
        4,
        smem_in=1,
        cost=cost(0, 0),
    )
    passed, given, near = lax.optimization_barrier((passed, latent, near))
    passed = swap(passed, "rep", 1)
    beside = swap(given, "tensor", 1)
    near_beside = swap(near, "tensor", 1)
    passed, far, corner = lax.optimization_barrier((passed, far, corner))
    far_beside = swap(far, "tensor", 1)
    corner_beside = swap(corner, "tensor", 1)
    choices = [query, second_query, passed]
    *first, query = score_call("score_chip", [latent, beside], w_up, choices, pick)
    second = score_call("score_next", [near, near_beside, far, far_beside], w_up, query)
    third = score_call("score_corner", [corner, corner_beside], w_up, query)
    depth = rows // new_count * head_size
    attended, attended_other = [], []
    for part in range(PARTS):
        (piece,) = call(
            lambda *refs: attend_kernel(part, tokens, *refs),
            "attend",
            [shape((new_count // PARTS, depth), BF16)],
            [*first, *second, *third],
            16,
            scratch=[pltpu.VMEM((rows // PARTS, head_size), F32)],
            cost=cost(0, 0),
        )
        piece, first[2] = lax.optimization_barrier((piece, first[2]))
        attended.append(piece)
        attended_other.append(swap(piece, "seq", 1))
    columns = w_out.shape[1]
    tile = min(512, columns // 2)
    (partial,) = call(
        lambda *refs: project_kernel(tile, *refs),
        "project",
        [shape((2, new_count, columns // 2), F32)],
        [*attended, held],
        12,
        cost=cost(0, 0),
    )

    def project_more(own, name, weight):
        return call(
            lambda *refs: project_more_kernel(tile, own, *refs),
            name,
            [shape((new_count, columns // 2), F32)],
            [*attended_other, weight, partial],
            12,
            cost=cost(0, 0),
        )[0]

    sent = swap(project_more(False, "project_sent", held_sent), "tensor", 1)
    kept = project_more(True, "project_own", held_kept)
    chunk = (new_count, columns // (4 * PARTS))
    pieces = call(split_kernel, "split", [shape(chunk, F32)] * (2 * PARTS), [kept, sent], 8, cost=cost(0, 0))
    given = [swap(piece, "tensor", 2) for piece in pieces[:PARTS]]
    own, across, beside = [], [], []
    for part in range(PARTS):
        operands = [pieces[PARTS + part], given[part]]
        (summed,) = call(sum_kernel, "sum", [shape(chunk, BF16)], operands, 8, cost=cost(0, 0))
        own.append(route(summed, index[0], orders, True))
        across.append(swap(own[part], "tensor", 2))
        beside.append(swap(own[part], "tensor", 1))
    corners = [swap(across[0], "tensor", 1)]
    joined = join(((0, 0), (2, 0), (0, 1), (1, 0)), [own[0], beside[0], own[1], across[0]], None)
    across[1], joined = lax.optimization_barrier((across[1], joined))
    corners.append(swap(across[1], "tensor", 1))
    joined = join(((2, 1), (1, 1), (3, 0)), [beside[1], across[1], corners[0]], joined)
    return join(((3, 1),), [corners[1]], joined)


def shards(key_value_rows, queries, w_comp, latent_gain, w_up, w_out, replica_order):
    orders = list(itertools.permutations(range(lax.axis_size("rep"))))
    index = order_index(replica_order, orders)
    query = route(queries[0], index, orders, False)
    rows = key_value_rows[0]
    latent = compress(rows.reshape(rows.shape[0], -1), w_comp, latent_gain)
    latent = lax.all_gather(latent, "tensor", axis=0, tiled=True)
    groups = w_up.shape[0]
    lifted = jnp.einsum("tf,gfy->tgy", latent, w_up, preferred_element_type=F32).astype(BF16)
    head_size = query.shape[-1]
    new_count = query.shape[0]
    keys = lifted[..., :head_size]
    values = lifted[..., head_size:]
    grouped_heads = query.reshape(new_count, groups, -1, head_size)
    scores = jnp.einsum(
        "nghd,tgd->nght", grouped_heads, keys, preferred_element_type=F32
    ) * head_size ** (-0.5)
    top = lax.pmax(jnp.max(scores, axis=-1), "seq")
    expo = jnp.exp(scores - top[..., None])
    total = jnp.sum(expo, axis=-1)
    summed = jnp.einsum("nght,tgd->nghd", expo.astype(BF16), values, preferred_element_type=F32)
    summed, total = lax.psum((summed, total), "seq")
    attended = (summed / total[..., None]).astype(BF16).reshape(new_count, -1)
    attended = route(attended, index, orders, True)
    return lax.psum(dot(attended, w_out), "tensor").astype(BF16)[None]


def solution(mesh):
    placed = (
        P("rep", ("seq", "tensor"), None, None),
        P("rep", None, "tensor", None),
        P(),
        P(),
        P("tensor", None, None),
        P("tensor", "seq"),
        P(),
    )
    square = all(mesh.shape[axis] == size for axis, size in (("seq", 2), ("rep", 4), ("tensor", 4)))
    return jax.shard_map(
        square_shards if square else shards,
        mesh=mesh,
        in_specs=placed,
        out_specs=P("rep", None, "seq"),
        check_vma=False,
    )
```

```python
import itertools
import math

import jax
import jax.numpy as jnp
from jax import lax
from jax.experimental import pallas as pl
from jax.experimental.pallas import tpu as pltpu
from jax.sharding import PartitionSpec as P

BF16, F32 = jnp.bfloat16, jnp.float32
MIB = 1024 * 1024
IN_VMEM = pl.BlockSpec(memory_space=pltpu.VMEM)
IN_SMEM = pl.BlockSpec(memory_space=pltpu.SMEM)
IN_HBM = pl.BlockSpec(memory_space=pltpu.HBM)
COPIES = 8
PARTS = 2


def shape(dims, dtype):
    return jax.ShapeDtypeStruct(dims, dtype)


def call(body, name, outs, operands, vmem, scratch=(), smem_in=0, smem_out=0, hbm_in=0, cost=None):
    kept = len(operands) - hbm_in
    specs = [IN_SMEM] * smem_in + [IN_VMEM] * (kept - smem_in) + [IN_HBM] * hbm_in
    operands = [
        *operands[:kept],
        *(pltpu.with_memory_space_constraint(operand, pltpu.HBM) for operand in operands[kept:]),
    ]
    out_specs = [IN_VMEM] * (len(outs) - smem_out) + [IN_SMEM] * smem_out
    return pl.pallas_call(
        body,
        out_shape=outs,
        in_specs=specs,
        out_specs=out_specs,
        scratch_shapes=list(scratch),
        compiler_params=pltpu.CompilerParams(vmem_limit_bytes=vmem * MIB),
        cost_estimate=cost,
        name=name,
    )(*operands)


def cost(flops, moved, exps=0):
    return pl.CostEstimate(flops=int(flops), bytes_accessed=int(moved), transcendentals=int(exps))


def dot(a, b):
    return jnp.dot(a, b, preferred_element_type=F32)


def compress(rows, weight, gain):
    projected = dot(rows, weight)
    scale = lax.rsqrt(jnp.mean(projected * projected, axis=-1, keepdims=True) + 1e-06)
    return (projected * scale * gain.astype(F32)[None]).astype(BF16)


def order_index(replica_order, orders):
    table = jnp.array(orders, jnp.int32)
    match = jnp.all(table == replica_order[None], axis=1)
    return jnp.sum(jnp.where(match, lax.iota(jnp.int32, len(orders)), 0))


def route_pairs(order, back):
    return [(p, r) if back else (r, p) for r, p in enumerate(order)]


def route(value, index, orders, back):
    def branch(order):
        return lambda v: lax.ppermute(v, "rep", route_pairs(order, back))

    return lax.switch(index, [branch(o) for o in orders], value)


def shift(value, axis, hops):
    size = lax.axis_size(axis)
    return lax.ppermute(value, axis, [(i, (i + hops) % size) for i in range(size)])


def swap(value, axis, bit):
    pairs = [(i, i ^ bit) for i in range(lax.axis_size(axis))]
    return lax.ppermute(value, axis, pairs)


def cross(value, seq_core):
    pairs = [(i, i ^ (4 if i % 2 == seq_core else 2)) for i in range(8)]
    return lax.ppermute(value, ("seq", "tensor"), pairs)


def compress_kernel(chunks, *refs):
    (order_hbm, rows_hbm, weight_hbm, gain_hbm, query_hbm, latent_ref, half_ref, index_ref, pick_ref) = refs[:9]
    (order_ref, rows_ref, weight_ref, gain_ref, query_ref, wide, packed, sems) = refs[9:]
    tokens, groups, width = rows_ref.shape
    chunk = tokens // chunks
    copies = [pltpu.make_async_copy(order_hbm, order_ref, sems.at[0])]
    for i in range(chunks):
        at = pl.ds(i * chunk, chunk)
        copies.append(pltpu.make_async_copy(rows_hbm.at[0, at], rows_ref.at[at], sems.at[1 + i]))
    for group in range(groups):
        at = pl.ds(group * width, width)
        copies.append(
            pltpu.make_async_copy(weight_hbm.at[at], weight_ref.at[at], sems.at[1 + chunks + group])
        )
    copies.append(pltpu.make_async_copy(gain_hbm, gain_ref, sems.at[1 + chunks + groups]))
    copies.append(pltpu.make_async_copy(query_hbm.at[0], query_ref, sems.at[2 + chunks + groups]))
    for copy in copies:
        copy.start()

    copies[0].wait()
    count = order_ref.shape[0]
    here = lax.axis_index("rep")
    index, wanted, wanted_beside = 0, 0, 0
    for i in range(count):
        wanted = jnp.where(order_ref[i] == here, i, wanted)
        wanted_beside = jnp.where(order_ref[i] == (here ^ 1), i, wanted_beside)
        smaller = 0
        for j in range(i + 1, count):
            smaller = smaller + (order_ref[j] < order_ref[i]).astype(jnp.int32)
        index = index + smaller * math.factorial(count - 1 - i)
    index_ref[0] = index
    pick_ref[0] = (wanted_beside == (here ^ 2)).astype(jnp.int32)
    pick_ref[1] = jnp.where(wanted == here, 0, jnp.where(wanted == (here ^ 2), 1, 2))

    lanes = wide.shape[2]
    for i in range(chunks):
        copies[1 + i].wait()
        at = slice(i * chunk * groups, (i + 1) * chunk * groups)
        for part in range(wide.shape[0]):
            values = rows_ref[i * chunk : (i + 1) * chunk, :, part * lanes : (part + 1) * lanes]
            wide[part, at] = values.astype(F32).reshape(chunk * groups, lanes)
        for group in range(groups):
            for part in range(wide.shape[0]):
                start = group * width + part * lanes
                picked = wide[part, pl.ds(at.start + group, chunk, stride=groups), :]
                packed[i * chunk : (i + 1) * chunk, start : start + lanes] = picked.astype(BF16)
    for group in range(groups):
        copies[1 + chunks + group].wait()
    copies[1 + chunks + groups].wait()
    gain = gain_ref[...].astype(F32)[None]
    projected = dot(packed[...], weight_ref[...])
    scale = lax.rsqrt(jnp.mean(projected * projected, axis=-1, keepdims=True) + 1e-06)
    latent_ref[...] = (projected * scale * gain).astype(BF16)

    copies[2 + chunks + groups].wait()
    new_count, heads, head_size = query_ref.shape
    query = query_ref[...].astype(F32)
    upper = lax.axis_index("seq") == 1
    query = jnp.where(upper, query[:, heads // 2 :], query[:, : heads // 2])
    half_ref[...] = query.reshape(half_ref.shape).astype(BF16)


def score_kernel(parts, *refs):
    latent_refs, (lift_ref, query_ref), (score_ref, value_ref, top_ref) = (
        refs[:parts],
        refs[parts : parts + 2],
        refs[parts + 2 :],
    )
    head_size = query_ref.shape[-1]
    lift = lift_ref[lax.axis_index("seq")]
    query = query_ref[...]
    top = None
    for part, latent_ref in enumerate(latent_refs):
        tokens = latent_ref.shape[0]
        at = slice(part * tokens, (part + 1) * tokens)
        lifted = dot(latent_ref[...], lift).astype(BF16)
        score = lax.dot_general(
            lifted[:, :head_size], query, (((1,), (1,)), ((), ())), preferred_element_type=F32
        )
        score_ref[at] = score
        value_ref[at] = lifted[:, head_size:]
        part_top = jnp.max(score, axis=0, keepdims=True)
        top = part_top if top is None else jnp.maximum(top, part_top)
    top_ref[...] = jnp.broadcast_to(top, top_ref.shape)


def fetch_kernel(own, weight_ref, *refs):
    *held_refs, sems = refs
    depth, columns = held_refs[0].shape
    rows = depth // COPIES
    group = lax.axis_index("seq") if own else 1 - lax.axis_index("seq")
    core = lax.axis_index("tensor") % 2
    copies = []
    for part, held_ref in enumerate(held_refs):
        first = 0 if own else pl.multiple_of((core if part else 1 - core) * columns, columns)
        for i in range(COPIES):
            start = pl.multiple_of(group * depth + i * rows, rows)
            source = weight_ref.at[pl.ds(start, rows), pl.ds(first, columns)]
            target = held_ref.at[pl.ds(i * rows, rows)]
            copies.append(pltpu.make_async_copy(source, target, sems.at[part, i]))
    for copy in copies:
        copy.start()
    for copy in copies:
        copy.wait()


def fetch(name, own, weight):
    depth, columns = weight.shape[0] // 2, weight.shape[1]
    blocks = [(depth, columns)] if own else [(depth, columns // 2)] * 2
    return call(
        lambda *refs: fetch_kernel(own, *refs),
        name,
        [pltpu.VMEM(block, weight.dtype) for block in blocks],
        [weight],
        4,
        scratch=[pltpu.SemaphoreType.DMA((len(blocks), COPIES))],
        hbm_in=1,
        cost=cost(0, 0),
    )


def choose(pick, refs, out_ref):
    for i, ref in enumerate(refs):

        @pl.when(pick == i)
        def _():
            out_ref[...] = ref[...]


def pass_kernel(pick_ref, own_ref, second_ref, out_ref):
    choose(pick_ref[0], (own_ref, second_ref), out_ref)


def choose_and_score_kernel(parts, pick_ref, *refs):
    *refs, score_ref, value_ref, top_ref, query_ref = refs
    choose(pick_ref[1], refs[parts + 1 :], query_ref)
    score_kernel(parts, *refs[: parts + 1], query_ref, score_ref, value_ref, top_ref)


def score_call(name, latents, lift, query, pick=None):
    queries = [query] if pick is None else query
    tokens = sum(latent.shape[0] for latent in latents)
    rows, head_size = queries[0].shape
    outs = [shape((tokens, rows), F32), shape((tokens, head_size), BF16), shape((8, rows), F32)]
    operands = [*latents, lift, *queries]
    estimate = cost(0, 0)
    if pick is None:
        body = lambda *refs: score_kernel(len(latents), *refs)
        return call(body, name, outs, operands, 16, cost=estimate)
    body = lambda *refs: choose_and_score_kernel(len(latents), *refs)
    outs.append(shape((rows, head_size), BF16))
    return call(body, name, outs, [pick, *operands], 16, smem_in=1, cost=estimate)


def attend_kernel(part, block, *refs):
    (*score_refs, out_ref, turned) = refs
    new_count = out_ref.shape[0]
    rows = slice(part * turned.shape[0], (part + 1) * turned.shape[0])
    triples = [score_refs[i : i + 3] for i in range(0, len(score_refs), 3)]
    head_size = triples[0][1].shape[-1]
    coef = head_size ** (-0.5) * math.log2(math.e)
    top = triples[0][2][:1, rows]
    for triple in triples[1:]:
        top = jnp.maximum(top, triple[2][:1, rows])
    total = jnp.zeros_like(top)
    summed = jnp.zeros((head_size, top.shape[1]), F32)
    for score_ref, value_ref, _ in triples:
        for start in range(0, score_ref.shape[0], block):
            at = slice(start, start + block)
            expo = jnp.exp2((score_ref[at, rows] - top) * coef)
            total += jnp.sum(expo, axis=0, keepdims=True)
            summed += lax.dot_general(
                value_ref[at], expo.astype(BF16), (((0,), (0,)), ((), ())), preferred_element_type=F32
            )
    turned[...] = (summed / total).T
    heads = turned.shape[0] // new_count
    for head in range(heads):
        out_ref[:, head * head_size : (head + 1) * head_size] = turned[
            pl.ds(head, new_count, stride=heads), :
        ].astype(BF16)


def project_kernel(tile, *refs):
    *row_refs, weight_ref, out_ref = refs
    rows = jnp.concatenate([ref[...] for ref in row_refs], axis=0)
    width = out_ref.shape[2]
    for part in range(out_ref.shape[0]):
        for column in range(0, width, tile):
            at = part * width + column
            out_ref[part, :, column : column + tile] = dot(
                rows, weight_ref[:, at : at + tile]
            )


def project_more_kernel(tile, own, *refs):
    *row_refs, weight_ref, before_ref, out_ref = refs
    core = lax.axis_index("tensor") % 2
    part = core if own else 1 - core
    rows = jnp.concatenate([ref[...] for ref in row_refs], axis=0)
    width = out_ref.shape[1]
    for column in range(0, width, tile):
        value = before_ref[part, :, column : column + tile] + dot(
            rows, weight_ref[:, column : column + tile]
        )
        out_ref[:, column : column + tile] = value


def split_kernel(own_ref, other_ref, *refs):
    chip = lax.axis_index("tensor") // 2
    width = refs[0].shape[1]
    for i, out_ref in enumerate(refs):
        part = chip if i >= PARTS else 1 - chip
        at = pl.ds(pl.multiple_of((part * PARTS + i % PARTS) * width, width), width)
        out_ref[...] = own_ref[:, at] + other_ref[:, at]


def sum_kernel(kept_ref, arrived_ref, out_ref):
    out_ref[...] = (kept_ref[...] + arrived_ref[...]).astype(out_ref.dtype)


def join_kernel(places, *refs):
    pieces = refs[: len(places)]
    out_ref, sems = refs[-2:]
    here = lax.axis_index("tensor")
    core, chip = here % 2, here // 2
    width = pieces[0].shape[1]
    copies = []
    for i, (place, part) in enumerate(places):
        at = 2 * (1 - core if place // 2 else core) + (1 - chip if place % 2 else chip)
        at = pl.ds(pl.multiple_of((at * PARTS + part) * width, width), width)
        copies.append(pltpu.make_async_copy(pieces[i], out_ref.at[0, :, at], sems.at[i]))
    for copy in copies:
        copy.start()
    for copy in copies:
        copy.wait()


def join(places, pieces, before):
    new_count, width = pieces[0].shape
    return pl.pallas_call(
        lambda *refs: join_kernel(places, *refs),
        out_shape=shape((1, new_count, 4 * PARTS * width), BF16),
        in_specs=[IN_VMEM] * len(places) + ([] if before is None else [IN_HBM]),
        out_specs=IN_HBM,
        scratch_shapes=[pltpu.SemaphoreType.DMA((len(places),))],
        input_output_aliases={} if before is None else {len(places): 0},
        compiler_params=pltpu.CompilerParams(vmem_limit_bytes=4 * MIB),
        name="join",
    )(*pieces, *([] if before is None else [before]))


def square_shards(key_value_rows, queries, w_comp, latent_gain, w_up, w_out, replica_order):
    orders = list(itertools.permutations(range(lax.axis_size("rep"))))
    _, new_count, heads, head_size = queries.shape
    _, tokens, all_groups, width = key_value_rows.shape
    latent_width = w_comp.shape[1]
    rows = heads // 2 * new_count

    chunks = 3 if tokens % 48 == 0 else 1
    latent, query, index, pick = call(
        lambda *refs: compress_kernel(chunks, *refs),
        "compress",
        [shape((tokens, latent_width), BF16), shape((rows, head_size), BF16), *[shape((n,), jnp.int32) for n in (1, 2)]],
        [replica_order, key_value_rows, w_comp, latent_gain, queries],
        16,
        scratch=[
            pltpu.SMEM(replica_order.shape, jnp.int32),
            pltpu.VMEM(key_value_rows.shape[1:], BF16),
            pltpu.VMEM(w_comp.shape, BF16),
            pltpu.VMEM(latent_gain.shape, BF16),
            pltpu.VMEM(queries.shape[1:], BF16),
            pltpu.VMEM((width // 128, tokens * all_groups, 128), F32),
            pltpu.VMEM((tokens, all_groups * width), BF16),
            pltpu.SemaphoreType.DMA((3 + chunks + all_groups,)),
        ],
        hbm_in=5,
        smem_out=2,
        cost=cost(0, 0),
    )

    near = cross(latent, 0)
    far = cross(latent, 1)
    second_query = swap(query, "rep", 2)
    (held,) = fetch("fetch_own", True, w_out)
    second_query, held = lax.optimization_barrier((second_query, held))
    (passed,) = call(
        pass_kernel,
        "pass",
        [shape(query.shape, query.dtype)],
        [pick, query, second_query],
        4,
        smem_in=1,
        cost=cost(0, 0),
    )
    beside = swap(latent, "tensor", 1)
    near, far, beside, _ = lax.optimization_barrier((near, far, beside, passed))
    passed = swap(passed, "rep", 1)
    corner = cross(near, 1)
    near, weight = lax.optimization_barrier((near, w_out))
    held_sent, held_kept = fetch("fetch_other", False, weight)
    near_beside = swap(near, "tensor", 1)
    passed, held_sent, far = lax.optimization_barrier((passed, held_sent, far))
    far_beside = swap(far, "tensor", 1)
    choices = [query, second_query, passed]
    *first, query = score_call("score_chip", [latent, beside], w_up, choices, pick)
    corner, first[2] = lax.optimization_barrier((corner, first[2]))
    corner_beside = swap(corner, "tensor", 1)
    second = score_call("score_next", [near, near_beside, far, far_beside], w_up, query)
    third = score_call("score_corner", [corner, corner_beside], w_up, query)
    depth = rows // new_count * head_size
    attended, attended_other = [], []
    for part in range(PARTS):
        (piece,) = call(
            lambda *refs: attend_kernel(part, tokens, *refs),
            "attend",
            [shape((new_count // PARTS, depth), BF16)],
            [*first, *second, *third],
            16,
            scratch=[pltpu.VMEM((rows // PARTS, head_size), F32)],
            cost=cost(0, 0),
        )
        piece, first[2] = lax.optimization_barrier((piece, first[2]))
        attended.append(piece)
        attended_other.append(swap(piece, "seq", 1))
    columns = w_out.shape[1]
    tile = min(512, columns // 2)
    (partial,) = call(
        lambda *refs: project_kernel(tile, *refs),
        "project",
        [shape((2, new_count, columns // 2), F32)],
        [*attended, held],
        12,
        cost=cost(0, 0),
    )

    def project_more(own, name, weight):
        return call(
            lambda *refs: project_more_kernel(tile, own, *refs),
            name,
            [shape((new_count, columns // 2), F32)],
            [*attended_other, weight, partial],
            12,
            cost=cost(0, 0),
        )[0]

    sent = swap(project_more(False, "project_sent", held_sent), "tensor", 1)
    kept = project_more(True, "project_own", held_kept)
    chunk = (new_count, columns // (4 * PARTS))
    pieces = call(split_kernel, "split", [shape(chunk, F32)] * (2 * PARTS), [kept, sent], 8, cost=cost(0, 0))
    given = [swap(piece, "tensor", 2) for piece in pieces[:PARTS]]
    own, across, beside = [], [], []
    for part in range(PARTS):
        operands = [pieces[PARTS + part], given[part]]
        (summed,) = call(sum_kernel, "sum", [shape(chunk, BF16)], operands, 8, cost=cost(0, 0))
        own.append(route(summed, index[0], orders, True))
        across.append(swap(own[part], "tensor", 2))
        beside.append(swap(own[part], "tensor", 1))
    corners = [swap(across[0], "tensor", 1)]
    joined = join(((0, 0), (2, 0), (0, 1), (1, 0)), [own[0], beside[0], own[1], across[0]], None)
    across[1], joined = lax.optimization_barrier((across[1], joined))
    corners.append(swap(across[1], "tensor", 1))
    joined = join(((2, 1), (1, 1), (3, 0)), [beside[1], across[1], corners[0]], joined)
    return join(((3, 1),), [corners[1]], joined)


def shards(key_value_rows, queries, w_comp, latent_gain, w_up, w_out, replica_order):
    orders = list(itertools.permutations(range(lax.axis_size("rep"))))
    index = order_index(replica_order, orders)
    query = route(queries[0], index, orders, False)
    rows = key_value_rows[0]
    latent = compress(rows.reshape(rows.shape[0], -1), w_comp, latent_gain)
    latent = lax.all_gather(latent, "tensor", axis=0, tiled=True)
    groups = w_up.shape[0]
    lifted = jnp.einsum("tf,gfy->tgy", latent, w_up, preferred_element_type=F32).astype(BF16)
    head_size = query.shape[-1]
    new_count = query.shape[0]
    keys = lifted[..., :head_size]
    values = lifted[..., head_size:]
    grouped_heads = query.reshape(new_count, groups, -1, head_size)
    scores = jnp.einsum(
        "nghd,tgd->nght", grouped_heads, keys, preferred_element_type=F32
    ) * head_size ** (-0.5)
    top = lax.pmax(jnp.max(scores, axis=-1), "seq")
    expo = jnp.exp(scores - top[..., None])
    total = jnp.sum(expo, axis=-1)
    summed = jnp.einsum("nght,tgd->nghd", expo.astype(BF16), values, preferred_element_type=F32)
    summed, total = lax.psum((summed, total), "seq")
    attended = (summed / total[..., None]).astype(BF16).reshape(new_count, -1)
    attended = route(attended, index, orders, True)
    return lax.psum(dot(attended, w_out), "tensor").astype(BF16)[None]


def solution(mesh):
    placed = (
        P("rep", ("seq", "tensor"), None, None),
        P("rep", None, "tensor", None),
        P(),
        P(),
        P("tensor", None, None),
        P("tensor", "seq"),
        P(),
    )
    square = all(mesh.shape[axis] == size for axis, size in (("seq", 2), ("rep", 4), ("tensor", 4)))
    return jax.shard_map(
        square_shards if square else shards,
        mesh=mesh,
        in_specs=placed,
        out_specs=P("rep", None, "seq"),
        check_vma=False,
    )
```

```python
import itertools
import math

import jax
import jax.numpy as jnp
from jax import lax
from jax.experimental import pallas as pl
from jax.experimental.pallas import tpu as pltpu
from jax.sharding import PartitionSpec as P

BF16, F32 = jnp.bfloat16, jnp.float32
MIB = 1024 * 1024
IN_VMEM = pl.BlockSpec(memory_space=pltpu.VMEM)
IN_SMEM = pl.BlockSpec(memory_space=pltpu.SMEM)
IN_HBM = pl.BlockSpec(memory_space=pltpu.HBM)
COPIES = 8
PARTS = 1


def shape(dims, dtype):
    return jax.ShapeDtypeStruct(dims, dtype)


def call(body, name, outs, operands, vmem, scratch=(), smem_in=0, smem_out=0, hbm_in=0, cost=None):
    kept = len(operands) - hbm_in
    specs = [IN_SMEM] * smem_in + [IN_VMEM] * (kept - smem_in) + [IN_HBM] * hbm_in
    operands = [
        *operands[:kept],
        *(pltpu.with_memory_space_constraint(operand, pltpu.HBM) for operand in operands[kept:]),
    ]
    out_specs = [IN_VMEM] * (len(outs) - smem_out) + [IN_SMEM] * smem_out
    return pl.pallas_call(
        body,
        out_shape=outs,
        in_specs=specs,
        out_specs=out_specs,
        scratch_shapes=list(scratch),
        compiler_params=pltpu.CompilerParams(vmem_limit_bytes=vmem * MIB),
        cost_estimate=cost,
        name=name,
    )(*operands)


def cost(flops, moved, exps=0):
    return pl.CostEstimate(flops=int(flops), bytes_accessed=int(moved), transcendentals=int(exps))


def dot(a, b):
    return jnp.dot(a, b, preferred_element_type=F32)


def compress(rows, weight, gain):
    projected = dot(rows, weight)
    scale = lax.rsqrt(jnp.mean(projected * projected, axis=-1, keepdims=True) + 1e-06)
    return (projected * scale * gain.astype(F32)[None]).astype(BF16)


def order_index(replica_order, orders):
    table = jnp.array(orders, jnp.int32)
    match = jnp.all(table == replica_order[None], axis=1)
    return jnp.sum(jnp.where(match, lax.iota(jnp.int32, len(orders)), 0))


def route_pairs(order, back):
    return [(p, r) if back else (r, p) for r, p in enumerate(order)]


def route(value, index, orders, back):
    def branch(order):
        return lambda v: lax.ppermute(v, "rep", route_pairs(order, back))

    return lax.switch(index, [branch(o) for o in orders], value)


def shift(value, axis, hops):
    size = lax.axis_size(axis)
    return lax.ppermute(value, axis, [(i, (i + hops) % size) for i in range(size)])


def swap(value, axis, bit):
    pairs = [(i, i ^ bit) for i in range(lax.axis_size(axis))]
    return lax.ppermute(value, axis, pairs)


def cross(value, seq_core):
    pairs = [(i, i ^ (4 if i % 2 == seq_core else 2)) for i in range(8)]
    return lax.ppermute(value, ("seq", "tensor"), pairs)


def compress_kernel(chunks, *refs):
    (order_hbm, rows_hbm, weight_hbm, gain_hbm, query_hbm, latent_ref, half_ref, index_ref, pick_ref) = refs[:9]
    (order_ref, rows_ref, weight_ref, gain_ref, query_ref, wide, packed, sems) = refs[9:]
    tokens, groups, width = rows_ref.shape
    chunk = tokens // chunks
    copies = [pltpu.make_async_copy(order_hbm, order_ref, sems.at[0])]
    for i in range(chunks):
        at = pl.ds(i * chunk, chunk)
        copies.append(pltpu.make_async_copy(rows_hbm.at[0, at], rows_ref.at[at], sems.at[1 + i]))
    for group in range(groups):
        at = pl.ds(group * width, width)
        copies.append(
            pltpu.make_async_copy(weight_hbm.at[at], weight_ref.at[at], sems.at[1 + chunks + group])
        )
    copies.append(pltpu.make_async_copy(gain_hbm, gain_ref, sems.at[1 + chunks + groups]))
    copies.append(pltpu.make_async_copy(query_hbm.at[0], query_ref, sems.at[2 + chunks + groups]))
    for copy in copies:
        copy.start()

    copies[0].wait()
    count = order_ref.shape[0]
    here = lax.axis_index("rep")
    index, wanted, wanted_beside = 0, 0, 0
    for i in range(count):
        wanted = jnp.where(order_ref[i] == here, i, wanted)
        wanted_beside = jnp.where(order_ref[i] == (here ^ 1), i, wanted_beside)
        smaller = 0
        for j in range(i + 1, count):
            smaller = smaller + (order_ref[j] < order_ref[i]).astype(jnp.int32)
        index = index + smaller * math.factorial(count - 1 - i)
    index_ref[0] = index
    pick_ref[0] = (wanted_beside == (here ^ 2)).astype(jnp.int32)
    pick_ref[1] = jnp.where(wanted == here, 0, jnp.where(wanted == (here ^ 2), 1, 2))

    lanes = wide.shape[2]
    for i in range(chunks):
        copies[1 + i].wait()
        at = slice(i * chunk * groups, (i + 1) * chunk * groups)
        for part in range(wide.shape[0]):
            values = rows_ref[i * chunk : (i + 1) * chunk, :, part * lanes : (part + 1) * lanes]
            wide[part, at] = values.astype(F32).reshape(chunk * groups, lanes)
        for group in range(groups):
            for part in range(wide.shape[0]):
                start = group * width + part * lanes
                picked = wide[part, pl.ds(at.start + group, chunk, stride=groups), :]
                packed[i * chunk : (i + 1) * chunk, start : start + lanes] = picked.astype(BF16)
    for group in range(groups):
        copies[1 + chunks + group].wait()
    copies[1 + chunks + groups].wait()
    gain = gain_ref[...].astype(F32)[None]
    projected = dot(packed[...], weight_ref[...])
    scale = lax.rsqrt(jnp.mean(projected * projected, axis=-1, keepdims=True) + 1e-06)
    latent_ref[...] = (projected * scale * gain).astype(BF16)

    copies[2 + chunks + groups].wait()
    new_count, heads, head_size = query_ref.shape
    query = query_ref[...].astype(F32)
    upper = lax.axis_index("seq") == 1
    query = jnp.where(upper, query[:, heads // 2 :], query[:, : heads // 2])
    half_ref[...] = query.reshape(half_ref.shape).astype(BF16)


def score_kernel(parts, *refs):
    latent_refs, (lift_ref, query_ref), (score_ref, value_ref, top_ref) = (
        refs[:parts],
        refs[parts : parts + 2],
        refs[parts + 2 :],
    )
    head_size = query_ref.shape[-1]
    lift = lift_ref[lax.axis_index("seq")]
    query = query_ref[...]
    top = None
    for part, latent_ref in enumerate(latent_refs):
        tokens = latent_ref.shape[0]
        at = slice(part * tokens, (part + 1) * tokens)
        lifted = dot(latent_ref[...], lift).astype(BF16)
        score = lax.dot_general(
            lifted[:, :head_size], query, (((1,), (1,)), ((), ())), preferred_element_type=F32
        )
        score_ref[at] = score
        value_ref[at] = lifted[:, head_size:]
        part_top = jnp.max(score, axis=0, keepdims=True)
        top = part_top if top is None else jnp.maximum(top, part_top)
    top_ref[...] = jnp.broadcast_to(top, top_ref.shape)


def fetch_kernel(own, weight_ref, *refs):
    *held_refs, sems = refs
    depth, columns = held_refs[0].shape
    rows = depth // COPIES
    group = lax.axis_index("seq") if own else 1 - lax.axis_index("seq")
    core = lax.axis_index("tensor") % 2
    copies = []
    for part, held_ref in enumerate(held_refs):
        first = 0 if own else pl.multiple_of((core if part else 1 - core) * columns, columns)
        for i in range(COPIES):
            start = pl.multiple_of(group * depth + i * rows, rows)
            source = weight_ref.at[pl.ds(start, rows), pl.ds(first, columns)]
            target = held_ref.at[pl.ds(i * rows, rows)]
            copies.append(pltpu.make_async_copy(source, target, sems.at[part, i]))
    for copy in copies:
        copy.start()
    for copy in copies:
        copy.wait()


def fetch(name, own, weight):
    depth, columns = weight.shape[0] // 2, weight.shape[1]
    blocks = [(depth, columns)] if own else [(depth, columns // 2)] * 2
    return call(
        lambda *refs: fetch_kernel(own, *refs),
        name,
        [pltpu.VMEM(block, weight.dtype) for block in blocks],
        [weight],
        4,
        scratch=[pltpu.SemaphoreType.DMA((len(blocks), COPIES))],
        hbm_in=1,
        cost=cost(0, 0),
    )


def choose(pick, refs, out_ref):
    for i, ref in enumerate(refs):

        @pl.when(pick == i)
        def _():
            out_ref[...] = ref[...]


def pass_kernel(pick_ref, own_ref, second_ref, near_ref, far_ref, out_ref, upper_ref, lower_ref):
    choose(pick_ref[0], (own_ref, second_ref), out_ref)
    half = upper_ref.shape[0]
    upper_ref[...] = near_ref[:half]
    lower_ref[...] = far_ref[half:]


def choose_and_score_kernel(parts, pick_ref, *refs):
    *refs, score_ref, value_ref, top_ref, query_ref = refs
    choose(pick_ref[1], refs[parts + 1 :], query_ref)
    score_kernel(parts, *refs[: parts + 1], query_ref, score_ref, value_ref, top_ref)


def score_call(name, latents, lift, query, pick=None):
    queries = [query] if pick is None else query
    tokens = sum(latent.shape[0] for latent in latents)
    rows, head_size = queries[0].shape
    outs = [shape((tokens, rows), F32), shape((tokens, head_size), BF16), shape((8, rows), F32)]
    operands = [*latents, lift, *queries]
    estimate = cost(0, 0)
    if pick is None:
        body = lambda *refs: score_kernel(len(latents), *refs)
        return call(body, name, outs, operands, 16, cost=estimate)
    body = lambda *refs: choose_and_score_kernel(len(latents), *refs)
    outs.append(shape((rows, head_size), BF16))
    return call(body, name, outs, [pick, *operands], 16, smem_in=1, cost=estimate)


def attend_kernel(part, block, *refs):
    (*score_refs, out_ref, turned) = refs
    new_count = out_ref.shape[0]
    rows = slice(part * turned.shape[0], (part + 1) * turned.shape[0])
    triples = [score_refs[i : i + 3] for i in range(0, len(score_refs), 3)]
    head_size = triples[0][1].shape[-1]
    coef = head_size ** (-0.5) * math.log2(math.e)
    top = triples[0][2][:1, rows]
    for triple in triples[1:]:
        top = jnp.maximum(top, triple[2][:1, rows])
    total = jnp.zeros_like(top)
    summed = jnp.zeros((head_size, top.shape[1]), F32)
    for score_ref, value_ref, _ in triples:
        for start in range(0, score_ref.shape[0], block):
            at = slice(start, start + block)
            expo = jnp.exp2((score_ref[at, rows] - top) * coef)
            total += jnp.sum(expo, axis=0, keepdims=True)
            summed += lax.dot_general(
                value_ref[at], expo.astype(BF16), (((0,), (0,)), ((), ())), preferred_element_type=F32
            )
    turned[...] = (summed / total).T
    heads = turned.shape[0] // new_count
    for head in range(heads):
        out_ref[:, head * head_size : (head + 1) * head_size] = turned[
            pl.ds(head, new_count, stride=heads), :
        ].astype(BF16)


def project_kernel(tile, *refs):
    *row_refs, weight_ref, out_ref = refs
    rows = jnp.concatenate([ref[...] for ref in row_refs], axis=0)
    width = out_ref.shape[2]
    for part in range(out_ref.shape[0]):
        for column in range(0, width, tile):
            at = part * width + column
            out_ref[part, :, column : column + tile] = dot(
                rows, weight_ref[:, at : at + tile]
            )


def project_more_kernel(tile, own, *refs):
    *row_refs, weight_ref, before_ref, out_ref = refs
    core = lax.axis_index("tensor") % 2
    part = core if own else 1 - core
    rows = jnp.concatenate([ref[...] for ref in row_refs], axis=0)
    width = out_ref.shape[1]
    for column in range(0, width, tile):
        value = before_ref[part, :, column : column + tile] + dot(
            rows, weight_ref[:, column : column + tile]
        )
        out_ref[:, column : column + tile] = value


def split_kernel(own_ref, other_ref, given_ref, kept_ref):
    chip = lax.axis_index("tensor") // 2
    width = given_ref.shape[1]
    for out_ref, part in ((given_ref, 1 - chip), (kept_ref, chip)):
        at = pl.ds(pl.multiple_of(part * width, width), width)
        out_ref[...] = own_ref[:, at] + other_ref[:, at]


def sum_kernel(kept_ref, arrived_ref, out_ref):
    out_ref[...] = (kept_ref[...] + arrived_ref[...]).astype(out_ref.dtype)


def join_kernel(places, *refs):
    pieces = refs[: len(places)]
    out_ref, sems = refs[-2:]
    here = lax.axis_index("tensor")
    core, chip = here % 2, here // 2
    width = pieces[0].shape[1]
    copies = []
    for i, place in enumerate(places):
        at = 2 * (1 - core if place // 2 else core) + (1 - chip if place % 2 else chip)
        at = pl.ds(pl.multiple_of(at * width, width), width)
        copies.append(pltpu.make_async_copy(pieces[i], out_ref.at[0, :, at], sems.at[i]))
    for copy in copies:
        copy.start()
    for copy in copies:
        copy.wait()


def join(places, pieces, before):
    new_count, width = pieces[0].shape
    return pl.pallas_call(
        lambda *refs: join_kernel(places, *refs),
        out_shape=shape((1, new_count, 4 * width), BF16),
        in_specs=[IN_VMEM] * len(places) + ([] if before is None else [IN_HBM]),
        out_specs=IN_HBM,
        scratch_shapes=[pltpu.SemaphoreType.DMA((len(places),))],
        input_output_aliases={} if before is None else {len(places): 0},
        compiler_params=pltpu.CompilerParams(vmem_limit_bytes=4 * MIB),
        name="join",
    )(*pieces, *([] if before is None else [before]))


def square_shards(key_value_rows, queries, w_comp, latent_gain, w_up, w_out, replica_order):
    orders = list(itertools.permutations(range(lax.axis_size("rep"))))
    _, new_count, heads, head_size = queries.shape
    _, tokens, all_groups, width = key_value_rows.shape
    latent_width = w_comp.shape[1]
    rows = heads // 2 * new_count

    chunks = 3 if tokens % 48 == 0 else 1
    latent, query, index, pick = call(
        lambda *refs: compress_kernel(chunks, *refs),
        "compress",
        [shape((tokens, latent_width), BF16), shape((rows, head_size), BF16), *[shape((n,), jnp.int32) for n in (1, 2)]],
        [replica_order, key_value_rows, w_comp, latent_gain, queries],
        16,
        scratch=[
            pltpu.SMEM(replica_order.shape, jnp.int32),
            pltpu.VMEM(key_value_rows.shape[1:], BF16),
            pltpu.VMEM(w_comp.shape, BF16),
            pltpu.VMEM(latent_gain.shape, BF16),
            pltpu.VMEM(queries.shape[1:], BF16),
            pltpu.VMEM((width // 128, tokens * all_groups, 128), F32),
            pltpu.VMEM((tokens, all_groups * width), BF16),
            pltpu.SemaphoreType.DMA((3 + chunks + all_groups,)),
        ],
        hbm_in=5,
        smem_out=2,
        cost=cost(0, 0),
    )

    near = cross(latent, 0)
    far = cross(latent, 1)
    second_query = swap(query, "rep", 2)
    (held,) = fetch("fetch_own", True, w_out)
    near, far, second_query, held = lax.optimization_barrier((near, far, second_query, held))
    passed, upper, lower = call(
        pass_kernel,
        "pass",
        [shape(query.shape, query.dtype)] + [shape((tokens // 2, latent_width), BF16)] * 2,
        [pick, query, second_query, near, far],
        4,
        smem_in=1,
        cost=cost(0, 0),
    )
    corner = [cross(upper, 1), cross(lower, 0)]
    passed = swap(passed, "rep", 1)
    weight, _ = lax.optimization_barrier((w_out, upper))
    held_sent, held_kept = fetch("fetch_other", False, weight)
    passed, held_sent, given, near, far = lax.optimization_barrier(
        (passed, held_sent, latent, near, far)
    )
    besides = [swap(piece, "tensor", 1) for piece in (given, near, far)]
    choices = [query, second_query, passed]
    *first, query = score_call("score_here", [given, near, far], w_up, choices, pick)
    corner, first[2] = lax.optimization_barrier((corner, first[2]))
    corner += [swap(piece, "tensor", 1) for piece in corner]
    second = list(score_call("score_beside", besides, w_up, query))
    corner[2], second[2] = lax.optimization_barrier((corner[2], second[2]))
    third = score_call("score_corner", corner, w_up, query)
    depth = rows // new_count * head_size
    attended, attended_other = [], []
    for part in range(PARTS):
        (piece,) = call(
            lambda *refs, part=part: attend_kernel(part, tokens, *refs),
            "attend",
            [shape((new_count // PARTS, depth), BF16)],
            [*first, *second, *third],
            16,
            scratch=[pltpu.VMEM((rows // PARTS, head_size), F32)],
            cost=cost(0, 0),
        )
        piece, first[2] = lax.optimization_barrier((piece, first[2]))
        attended.append(piece)
        attended_other.append(swap(piece, "seq", 1))
    columns = w_out.shape[1]
    tile = min(512, columns // 2)
    (partial,) = call(
        lambda *refs: project_kernel(tile, *refs),
        "project",
        [shape((2, new_count, columns // 2), F32)],
        [*attended, held],
        12,
        cost=cost(0, 0),
    )

    def project_more(own, name, weight):
        return call(
            lambda *refs: project_more_kernel(tile, own, *refs),
            name,
            [shape((new_count, columns // 2), F32)],
            [*attended_other, weight, partial],
            12,
            cost=cost(0, 0),
        )[0]

    sent = swap(project_more(False, "project_sent", held_sent), "tensor", 1)
    kept = project_more(True, "project_own", held_kept)
    quarter = (new_count, columns // 4)
    given, kept = call(split_kernel, "split", [shape(quarter, F32)] * 2, [kept, sent], 8, cost=cost(0, 0))
    given = swap(given, "tensor", 2)
    (own,) = call(sum_kernel, "sum", [shape(quarter, BF16)], [kept, given], 8, cost=cost(0, 0))
    own = route(own, index[0], orders, True)
    across = swap(own, "tensor", 2)
    beside = swap(own, "tensor", 1)
    joined = join((0, 2), [own, beside], None)
    across, joined = lax.optimization_barrier((across, joined))
    last = swap(across, "tensor", 1)
    joined = join((1,), [across], joined)
    return join((3,), [last], joined)


def shards(key_value_rows, queries, w_comp, latent_gain, w_up, w_out, replica_order):
    orders = list(itertools.permutations(range(lax.axis_size("rep"))))
    index = order_index(replica_order, orders)
    query = route(queries[0], index, orders, False)
    rows = key_value_rows[0]
    latent = compress(rows.reshape(rows.shape[0], -1), w_comp, latent_gain)
    latent = lax.all_gather(latent, "tensor", axis=0, tiled=True)
    groups = w_up.shape[0]
    lifted = jnp.einsum("tf,gfy->tgy", latent, w_up, preferred_element_type=F32).astype(BF16)
    head_size = query.shape[-1]
    new_count = query.shape[0]
    keys = lifted[..., :head_size]
    values = lifted[..., head_size:]
    grouped_heads = query.reshape(new_count, groups, -1, head_size)
    scores = jnp.einsum(
        "nghd,tgd->nght", grouped_heads, keys, preferred_element_type=F32
    ) * head_size ** (-0.5)
    top = lax.pmax(jnp.max(scores, axis=-1), "seq")
    expo = jnp.exp(scores - top[..., None])
    total = jnp.sum(expo, axis=-1)
    summed = jnp.einsum("nght,tgd->nghd", expo.astype(BF16), values, preferred_element_type=F32)
    summed, total = lax.psum((summed, total), "seq")
    attended = (summed / total[..., None]).astype(BF16).reshape(new_count, -1)
    attended = route(attended, index, orders, True)
    return lax.psum(dot(attended, w_out), "tensor").astype(BF16)[None]


def solution(mesh):
    placed = (
        P("rep", ("seq", "tensor"), None, None),
        P("rep", None, "tensor", None),
        P(),
        P(),
        P("tensor", None, None),
        P("tensor", "seq"),
        P(),
    )
    square = all(mesh.shape[axis] == size for axis, size in (("seq", 2), ("rep", 4), ("tensor", 4)))
    return jax.shard_map(
        square_shards if square else shards,
        mesh=mesh,
        in_specs=placed,
        out_specs=P("rep", None, "seq"),
        check_vma=False,
    )
```

```python
import itertools
import math

import jax
import jax.numpy as jnp
from jax import lax
from jax.experimental import pallas as pl
from jax.experimental.pallas import tpu as pltpu
from jax.sharding import PartitionSpec as P

BF16, F32 = jnp.bfloat16, jnp.float32
MIB = 1024 * 1024
IN_VMEM = pl.BlockSpec(memory_space=pltpu.VMEM)
IN_SMEM = pl.BlockSpec(memory_space=pltpu.SMEM)
IN_HBM = pl.BlockSpec(memory_space=pltpu.HBM)
COPIES = 8


def shape(dims, dtype):
    return jax.ShapeDtypeStruct(dims, dtype)


def call(body, name, outs, operands, vmem, scratch=(), smem_in=0, smem_out=0, hbm_in=0, cost=None):
    kept = len(operands) - hbm_in
    specs = [IN_SMEM] * smem_in + [IN_VMEM] * (kept - smem_in) + [IN_HBM] * hbm_in
    operands = [
        *operands[:kept],
        *(pltpu.with_memory_space_constraint(operand, pltpu.HBM) for operand in operands[kept:]),
    ]
    out_specs = [IN_VMEM] * (len(outs) - smem_out) + [IN_SMEM] * smem_out
    return pl.pallas_call(
        body,
        out_shape=outs,
        in_specs=specs,
        out_specs=out_specs,
        scratch_shapes=list(scratch),
        compiler_params=pltpu.CompilerParams(vmem_limit_bytes=vmem * MIB),
        cost_estimate=cost,
        name=name,
    )(*operands)


def cost(flops, moved, exps=0):
    return pl.CostEstimate(flops=int(flops), bytes_accessed=int(moved), transcendentals=int(exps))


def dot(a, b):
    return jnp.dot(a, b, preferred_element_type=F32)


def compress(rows, weight, gain):
    projected = dot(rows, weight)
    scale = lax.rsqrt(jnp.mean(projected * projected, axis=-1, keepdims=True) + 1e-06)
    return (projected * scale * gain.astype(F32)[None]).astype(BF16)


def order_index(replica_order, orders):
    table = jnp.array(orders, jnp.int32)
    match = jnp.all(table == replica_order[None], axis=1)
    return jnp.sum(jnp.where(match, lax.iota(jnp.int32, len(orders)), 0))


def route_pairs(order, back):
    return [(p, r) if back else (r, p) for r, p in enumerate(order)]


def route(value, index, orders, back):
    def branch(order):
        return lambda v: lax.ppermute(v, "rep", route_pairs(order, back))

    return lax.switch(index, [branch(o) for o in orders], value)


def shift(value, axis, hops):
    size = lax.axis_size(axis)
    return lax.ppermute(value, axis, [(i, (i + hops) % size) for i in range(size)])


def swap(value, axis, bit):
    pairs = [(i, i ^ bit) for i in range(lax.axis_size(axis))]
    return lax.ppermute(value, axis, pairs)


def cross(value, seq_core):
    pairs = [(i, i ^ (4 if i % 2 == seq_core else 2)) for i in range(8)]
    return lax.ppermute(value, ("seq", "tensor"), pairs)


def compress_kernel(chunks, *refs):
    (order_hbm, rows_hbm, weight_hbm, gain_hbm, query_hbm, latent_ref, half_ref, index_ref, pick_ref) = refs[:9]
    (order_ref, rows_ref, weight_ref, gain_ref, query_ref, wide, packed, sems) = refs[9:]
    tokens, groups, width = rows_ref.shape
    chunk = tokens // chunks
    copies = [pltpu.make_async_copy(order_hbm, order_ref, sems.at[0])]
    for i in range(chunks):
        at = pl.ds(i * chunk, chunk)
        copies.append(pltpu.make_async_copy(rows_hbm.at[0, at], rows_ref.at[at], sems.at[1 + i]))
    for group in range(groups):
        at = pl.ds(group * width, width)
        copies.append(
            pltpu.make_async_copy(weight_hbm.at[at], weight_ref.at[at], sems.at[1 + chunks + group])
        )
    copies.append(pltpu.make_async_copy(gain_hbm, gain_ref, sems.at[1 + chunks + groups]))
    copies.append(pltpu.make_async_copy(query_hbm.at[0], query_ref, sems.at[2 + chunks + groups]))
    for copy in copies:
        copy.start()

    copies[0].wait()
    count = order_ref.shape[0]
    here = lax.axis_index("rep")
    index, wanted, wanted_beside = 0, 0, 0
    for i in range(count):
        wanted = jnp.where(order_ref[i] == here, i, wanted)
        wanted_beside = jnp.where(order_ref[i] == (here ^ 1), i, wanted_beside)
        smaller = 0
        for j in range(i + 1, count):
            smaller = smaller + (order_ref[j] < order_ref[i]).astype(jnp.int32)
        index = index + smaller * math.factorial(count - 1 - i)
    index_ref[0] = index
    pick_ref[0] = (wanted_beside == (here ^ 2)).astype(jnp.int32)
    pick_ref[1] = jnp.where(wanted == here, 0, jnp.where(wanted == (here ^ 2), 1, 2))

    lanes = wide.shape[2]
    for i in range(chunks):
        copies[1 + i].wait()
        at = slice(i * chunk * groups, (i + 1) * chunk * groups)
        for part in range(wide.shape[0]):
            values = rows_ref[i * chunk : (i + 1) * chunk, :, part * lanes : (part + 1) * lanes]
            wide[part, at] = values.astype(F32).reshape(chunk * groups, lanes)
        for group in range(groups):
            for part in range(wide.shape[0]):
                start = group * width + part * lanes
                picked = wide[part, pl.ds(at.start + group, chunk, stride=groups), :]
                packed[i * chunk : (i + 1) * chunk, start : start + lanes] = picked.astype(BF16)
    for group in range(groups):
        copies[1 + chunks + group].wait()
    copies[1 + chunks + groups].wait()
    gain = gain_ref[...].astype(F32)[None]
    projected = dot(packed[...], weight_ref[...])
    scale = lax.rsqrt(jnp.mean(projected * projected, axis=-1, keepdims=True) + 1e-06)
    latent_ref[...] = (projected * scale * gain).astype(BF16)

    copies[2 + chunks + groups].wait()
    new_count, heads, head_size = query_ref.shape
    query = query_ref[...].astype(F32)
    upper = lax.axis_index("seq") == 1
    query = jnp.where(upper, query[:, heads // 2 :], query[:, : heads // 2])
    half_ref[...] = query.reshape(half_ref.shape).astype(BF16)


def score_kernel(parts, *refs):
    latent_refs, (lift_ref, query_ref), (score_ref, value_ref, top_ref) = (
        refs[:parts],
        refs[parts : parts + 2],
        refs[parts + 2 :],
    )
    head_size = query_ref.shape[-1]
    lift = lift_ref[lax.axis_index("seq")]
    query = query_ref[...]
    top = None
    for part, latent_ref in enumerate(latent_refs):
        tokens = latent_ref.shape[0]
        at = slice(part * tokens, (part + 1) * tokens)
        lifted = dot(latent_ref[...], lift).astype(BF16)
        score = lax.dot_general(
            lifted[:, :head_size], query, (((1,), (1,)), ((), ())), preferred_element_type=F32
        )
        score_ref[at] = score
        value_ref[at] = lifted[:, head_size:]
        part_top = jnp.max(score, axis=0, keepdims=True)
        top = part_top if top is None else jnp.maximum(top, part_top)
    top_ref[...] = jnp.broadcast_to(top, top_ref.shape)


def fetch_kernel(weight_ref, own_ref, sent_ref, kept_ref, sems):
    core = lax.axis_index("tensor") % 2
    depth, columns = sent_ref.shape
    rows = depth // COPIES
    group = lax.axis_index("seq")
    copies = []
    for part, (held_ref, half, first) in enumerate(
        ((own_ref, group, 0), (sent_ref, 1 - group, 1 - core), (kept_ref, 1 - group, core))
    ):
        first = pl.multiple_of(first * columns, columns)
        for i in range(COPIES):
            start = pl.multiple_of(half * depth + i * rows, rows)
            source = weight_ref.at[pl.ds(start, rows), pl.ds(first, held_ref.shape[1])]
            target = held_ref.at[pl.ds(i * rows, rows)]
            copies.append(pltpu.make_async_copy(source, target, sems.at[part, i]))
    for copy in copies:
        copy.start()
    for copy in copies:
        copy.wait()


def fetch(weight):
    depth, columns = weight.shape[0] // 2, weight.shape[1]
    return call(
        fetch_kernel,
        "fetch",
        [pltpu.VMEM((depth, width), weight.dtype) for width in (columns, columns // 2, columns // 2)],
        [weight],
        4,
        scratch=[pltpu.SemaphoreType.DMA((3, COPIES))],
        hbm_in=1,
        cost=cost(0, 0),
    )


def choose(pick, refs, out_ref):
    for i, ref in enumerate(refs):

        @pl.when(pick == i)
        def _():
            out_ref[...] = ref[...]


def pass_kernel(pick_ref, own_ref, second_ref, near_ref, far_ref, out_ref, upper_ref, lower_ref):
    choose(pick_ref[0], (own_ref, second_ref), out_ref)
    half = upper_ref.shape[0]
    upper_ref[...] = near_ref[:half]
    lower_ref[...] = far_ref[half:]


def choose_and_score_kernel(parts, pick_ref, *refs):
    *refs, score_ref, value_ref, top_ref, query_ref = refs
    choose(pick_ref[1], refs[parts + 1 :], query_ref)
    score_kernel(parts, *refs[: parts + 1], query_ref, score_ref, value_ref, top_ref)


def score_call(name, latents, lift, query, pick=None):
    queries = [query] if pick is None else query
    tokens = sum(latent.shape[0] for latent in latents)
    rows, head_size = queries[0].shape
    outs = [shape((tokens, rows), F32), shape((tokens, head_size), BF16), shape((8, rows), F32)]
    operands = [*latents, lift, *queries]
    estimate = cost(0, 0)
    if pick is None:
        body = lambda *refs: score_kernel(len(latents), *refs)
        return call(body, name, outs, operands, 16, cost=estimate)
    body = lambda *refs: choose_and_score_kernel(len(latents), *refs)
    outs.append(shape((rows, head_size), BF16))
    return call(body, name, outs, [pick, *operands], 16, smem_in=1, cost=estimate)


def attend_kernel(block, *refs):
    (*score_refs, out_ref, turned) = refs
    new_count = out_ref.shape[0]
    triples = [score_refs[i : i + 3] for i in range(0, len(score_refs), 3)]
    head_size = triples[0][1].shape[-1]
    coef = head_size ** (-0.5) * math.log2(math.e)
    top = triples[0][2][:1]
    for triple in triples[1:]:
        top = jnp.maximum(top, triple[2][:1])
    total = jnp.zeros_like(top)
    summed = jnp.zeros((head_size, top.shape[1]), F32)
    for score_ref, value_ref, _ in triples:
        for start in range(0, score_ref.shape[0], block):
            at = slice(start, start + block)
            expo = jnp.exp2((score_ref[at] - top) * coef)
            total += jnp.sum(expo, axis=0, keepdims=True)
            summed += lax.dot_general(
                value_ref[at], expo.astype(BF16), (((0,), (0,)), ((), ())), preferred_element_type=F32
            )
    turned[...] = (summed / total).T
    heads = turned.shape[0] // new_count
    for head in range(heads):
        out_ref[:, head * head_size : (head + 1) * head_size] = turned[
            pl.ds(head, new_count, stride=heads), :
        ].astype(BF16)


def project_kernel(tile, rows_ref, weight_ref, out_ref):
    rows = rows_ref[...]
    width = out_ref.shape[2]
    for part in range(out_ref.shape[0]):
        for column in range(0, width, tile):
            at = part * width + column
            out_ref[part, :, column : column + tile] = dot(
                rows, weight_ref[:, at : at + tile]
            )


def project_more_kernel(tile, own, kept, rows_ref, weight_ref, before_ref, out_ref):
    here = lax.axis_index("tensor")
    core, chip = here % 2, here // 2
    half = core if own else 1 - core
    width = out_ref.shape[1]
    start = (chip if kept else 1 - chip) * width
    rows = rows_ref[...]
    for column in range(0, width, tile):
        at = pl.ds(pl.multiple_of(start + column, tile), tile)
        out_ref[:, column : column + tile] = before_ref[half, :, at] + dot(rows, weight_ref[:, at])


def add_kernel(one_ref, other_ref, out_ref):
    out_ref[...] = one_ref[...] + other_ref[...]


def sum_kernel(own_ref, beside_ref, across_ref, out_ref):
    out_ref[...] = (own_ref[...] + beside_ref[...] + across_ref[...]).astype(out_ref.dtype)


def join_kernel(places, *refs):
    pieces = refs[: len(places)]
    out_ref, sems = refs[-2:]
    here = lax.axis_index("tensor")
    core, chip = here % 2, here // 2
    width = pieces[0].shape[1]
    copies = []
    for i, place in enumerate(places):
        at = 2 * (1 - core if place // 2 else core) + (1 - chip if place % 2 else chip)
        at = pl.ds(pl.multiple_of(at * width, width), width)
        copies.append(pltpu.make_async_copy(pieces[i], out_ref.at[0, :, at], sems.at[i]))
    for copy in copies:
        copy.start()
    for copy in copies:
        copy.wait()


def join(places, pieces, before):
    new_count, width = pieces[0].shape
    return pl.pallas_call(
        lambda *refs: join_kernel(places, *refs),
        out_shape=shape((1, new_count, 4 * width), BF16),
        in_specs=[IN_VMEM] * len(places) + ([] if before is None else [IN_HBM]),
        out_specs=IN_HBM,
        scratch_shapes=[pltpu.SemaphoreType.DMA((len(places),))],
        input_output_aliases={} if before is None else {len(places): 0},
        compiler_params=pltpu.CompilerParams(vmem_limit_bytes=4 * MIB),
        name="join",
    )(*pieces, *([] if before is None else [before]))


def square_shards(key_value_rows, queries, w_comp, latent_gain, w_up, w_out, replica_order):
    orders = list(itertools.permutations(range(lax.axis_size("rep"))))
    _, new_count, heads, head_size = queries.shape
    _, tokens, all_groups, width = key_value_rows.shape
    latent_width = w_comp.shape[1]
    rows = heads // 2 * new_count

    chunks = 3 if tokens % 48 == 0 else 1
    latent, query, index, pick = call(
        lambda *refs: compress_kernel(chunks, *refs),
        "compress",
        [shape((tokens, latent_width), BF16), shape((rows, head_size), BF16), *[shape((n,), jnp.int32) for n in (1, 2)]],
        [replica_order, key_value_rows, w_comp, latent_gain, queries],
        16,
        scratch=[
            pltpu.SMEM(replica_order.shape, jnp.int32),
            pltpu.VMEM(key_value_rows.shape[1:], BF16),
            pltpu.VMEM(w_comp.shape, BF16),
            pltpu.VMEM(latent_gain.shape, BF16),
            pltpu.VMEM(queries.shape[1:], BF16),
            pltpu.VMEM((width // 128, tokens * all_groups, 128), F32),
            pltpu.VMEM((tokens, all_groups * width), BF16),
            pltpu.SemaphoreType.DMA((3 + chunks + all_groups,)),
        ],
        hbm_in=5,
        smem_out=2,
        cost=cost(0, 0),
    )

    near = cross(latent, 0)
    far = cross(latent, 1)
    second_query = swap(query, "rep", 2)
    held, held_sent, held_kept = fetch(w_out)
    near, far, second_query, held = lax.optimization_barrier((near, far, second_query, held))
    passed, upper, lower = call(
        pass_kernel,
        "pass",
        [shape(query.shape, query.dtype)] + [shape((tokens // 2, latent_width), BF16)] * 2,
        [pick, query, second_query, near, far],
        4,
        smem_in=1,
        cost=cost(0, 0),
    )
    corner = [cross(upper, 1), cross(lower, 0)]
    passed = swap(passed, "rep", 1)
    given, near, far, _ = lax.optimization_barrier((latent, near, far, upper))
    besides = [swap(piece, "tensor", 1) for piece in (given, near, far)]
    choices = [query, second_query, passed]
    *first, query = score_call("score_here", [given, near, far], w_up, choices, pick)
    corner, first[2] = lax.optimization_barrier((corner, first[2]))
    corner += [swap(piece, "tensor", 1) for piece in corner]
    second = list(score_call("score_beside", besides, w_up, query))
    corner[2], second[2] = lax.optimization_barrier((corner[2], second[2]))
    third = score_call("score_corner", corner, w_up, query)
    depth = rows // new_count * head_size
    (attended,) = call(
        lambda *refs: attend_kernel(tokens, *refs),
        "attend",
        [shape((new_count, depth), BF16)],
        [*first, *second, *third],
        16,
        scratch=[pltpu.VMEM((rows, head_size), F32)],
        cost=cost(0, 0),
    )
    attended_other = swap(attended, "seq", 1)
    columns = w_out.shape[1]
    tile = min(512, columns // 2)
    (partial,) = call(
        lambda *refs: project_kernel(tile, *refs),
        "project",
        [shape((2, new_count, columns // 2), F32)],
        [attended, held],
        12,
        cost=cost(0, 0),
    )

    quarter = (new_count, columns // 4)

    def project_more(other, own, kept):
        return call(
            lambda *refs: project_more_kernel(tile, own, kept, *refs),
            "project_own" if own else "project_sent",
            [shape(quarter, F32)],
            [other, held_kept if own else held_sent, partial],
            12,
            cost=cost(0, 0),
        )[0]

    given = swap(project_more(attended_other, False, False), "tensor", 1)
    operands = [project_more(attended_other, True, False), given]
    operands[0], other = lax.optimization_barrier((operands[0], attended_other))
    kept = project_more(other, False, True)
    (given,) = call(add_kernel, "add", [shape(quarter, F32)], operands, 8, cost=cost(0, 0))
    other, given, kept = lax.optimization_barrier((attended_other, given, kept))
    given = swap(given, "tensor", 2)
    kept = swap(kept, "tensor", 1)
    operands = [project_more(other, True, True), kept, given]
    (own,) = call(sum_kernel, "sum", [shape(quarter, BF16)], operands, 8, cost=cost(0, 0))
    own = route(own, index[0], orders, True)
    across = swap(own, "tensor", 2)
    beside = swap(own, "tensor", 1)
    joined = join((0, 2), [own, beside], None)
    across, joined = lax.optimization_barrier((across, joined))
    last = swap(across, "tensor", 1)
    joined = join((1,), [across], joined)
    return join((3,), [last], joined)


def shards(key_value_rows, queries, w_comp, latent_gain, w_up, w_out, replica_order):
    orders = list(itertools.permutations(range(lax.axis_size("rep"))))
    index = order_index(replica_order, orders)
    query = route(queries[0], index, orders, False)
    rows = key_value_rows[0]
    latent = compress(rows.reshape(rows.shape[0], -1), w_comp, latent_gain)
    latent = lax.all_gather(latent, "tensor", axis=0, tiled=True)
    groups = w_up.shape[0]
    lifted = jnp.einsum("tf,gfy->tgy", latent, w_up, preferred_element_type=F32).astype(BF16)
    head_size = query.shape[-1]
    new_count = query.shape[0]
    keys = lifted[..., :head_size]
    values = lifted[..., head_size:]
    grouped_heads = query.reshape(new_count, groups, -1, head_size)
    scores = jnp.einsum(
        "nghd,tgd->nght", grouped_heads, keys, preferred_element_type=F32
    ) * head_size ** (-0.5)
    top = lax.pmax(jnp.max(scores, axis=-1), "seq")
    expo = jnp.exp(scores - top[..., None])
    total = jnp.sum(expo, axis=-1)
    summed = jnp.einsum("nght,tgd->nghd", expo.astype(BF16), values, preferred_element_type=F32)
    summed, total = lax.psum((summed, total), "seq")
    attended = (summed / total[..., None]).astype(BF16).reshape(new_count, -1)
    attended = route(attended, index, orders, True)
    return lax.psum(dot(attended, w_out), "tensor").astype(BF16)[None]


def solution(mesh):
    placed = (
        P("rep", ("seq", "tensor"), None, None),
        P("rep", None, "tensor", None),
        P(),
        P(),
        P("tensor", None, None),
        P("tensor", "seq"),
        P(),
    )
    square = all(mesh.shape[axis] == size for axis, size in (("seq", 2), ("rep", 4), ("tensor", 4)))
    return jax.shard_map(
        square_shards if square else shards,
        mesh=mesh,
        in_specs=placed,
        out_specs=P("rep", None, "seq"),
        check_vma=False,
    )
```

```python
import itertools
import math

import jax
import jax.numpy as jnp
from jax import lax
from jax.experimental import pallas as pl
from jax.experimental.pallas import tpu as pltpu
from jax.sharding import PartitionSpec as P

BF16, F32 = jnp.bfloat16, jnp.float32
MIB = 1024 * 1024
IN_VMEM = pl.BlockSpec(memory_space=pltpu.VMEM)
IN_SMEM = pl.BlockSpec(memory_space=pltpu.SMEM)
IN_HBM = pl.BlockSpec(memory_space=pltpu.HBM)
COPIES = 8


def shape(dims, dtype):
    return jax.ShapeDtypeStruct(dims, dtype)


def call(body, name, outs, operands, vmem, scratch=(), smem_in=0, smem_out=0, hbm_in=0, cost=None):
    kept = len(operands) - hbm_in
    specs = [IN_SMEM] * smem_in + [IN_VMEM] * (kept - smem_in) + [IN_HBM] * hbm_in
    operands = [
        *operands[:kept],
        *(pltpu.with_memory_space_constraint(operand, pltpu.HBM) for operand in operands[kept:]),
    ]
    out_specs = [IN_VMEM] * (len(outs) - smem_out) + [IN_SMEM] * smem_out
    return pl.pallas_call(
        body,
        out_shape=outs,
        in_specs=specs,
        out_specs=out_specs,
        scratch_shapes=list(scratch),
        compiler_params=pltpu.CompilerParams(vmem_limit_bytes=vmem * MIB),
        cost_estimate=cost,
        name=name,
    )(*operands)


def cost(flops, moved, exps=0):
    return pl.CostEstimate(flops=int(flops), bytes_accessed=int(moved), transcendentals=int(exps))


def dot(a, b):
    return jnp.dot(a, b, preferred_element_type=F32)


def compress(rows, weight, gain):
    projected = dot(rows, weight)
    scale = lax.rsqrt(jnp.mean(projected * projected, axis=-1, keepdims=True) + 1e-06)
    return (projected * scale * gain.astype(F32)[None]).astype(BF16)


def order_index(replica_order, orders):
    table = jnp.array(orders, jnp.int32)
    match = jnp.all(table == replica_order[None], axis=1)
    return jnp.sum(jnp.where(match, lax.iota(jnp.int32, len(orders)), 0))


def route_pairs(order, back):
    return [(p, r) if back else (r, p) for r, p in enumerate(order)]


def route(value, index, orders, back):
    def branch(order):
        return lambda v: lax.ppermute(v, "rep", route_pairs(order, back))

    return lax.switch(index, [branch(o) for o in orders], value)


def shift(value, axis, hops):
    size = lax.axis_size(axis)
    return lax.ppermute(value, axis, [(i, (i + hops) % size) for i in range(size)])


def swap(value, axis, bit):
    pairs = [(i, i ^ bit) for i in range(lax.axis_size(axis))]
    return lax.ppermute(value, axis, pairs)


def compress_kernel(chunks, *refs):
    (order_hbm, rows_hbm, weight_hbm, gain_hbm, query_hbm, latent_ref, half_ref, index_ref, pick_ref) = refs[:9]
    (order_ref, rows_ref, weight_ref, gain_ref, query_ref, wide, packed, sems) = refs[9:]
    tokens, groups, width = rows_ref.shape
    chunk = tokens // chunks
    copies = [pltpu.make_async_copy(order_hbm, order_ref, sems.at[0])]
    for i in range(chunks):
        at = pl.ds(i * chunk, chunk)
        copies.append(pltpu.make_async_copy(rows_hbm.at[0, at], rows_ref.at[at], sems.at[1 + i]))
    for group in range(groups):
        at = pl.ds(group * width, width)
        copies.append(
            pltpu.make_async_copy(weight_hbm.at[at], weight_ref.at[at], sems.at[1 + chunks + group])
        )
    copies.append(pltpu.make_async_copy(gain_hbm, gain_ref, sems.at[1 + chunks + groups]))
    copies.append(pltpu.make_async_copy(query_hbm.at[0], query_ref, sems.at[2 + chunks + groups]))
    for copy in copies:
        copy.start()

    copies[0].wait()
    count = order_ref.shape[0]
    here = lax.axis_index("rep")
    index, wanted, wanted_beside = 0, 0, 0
    for i in range(count):
        wanted = jnp.where(order_ref[i] == here, i, wanted)
        wanted_beside = jnp.where(order_ref[i] == (here ^ 1), i, wanted_beside)
        smaller = 0
        for j in range(i + 1, count):
            smaller = smaller + (order_ref[j] < order_ref[i]).astype(jnp.int32)
        index = index + smaller * math.factorial(count - 1 - i)
    index_ref[0] = index
    pick_ref[0] = (wanted_beside == (here ^ 2)).astype(jnp.int32)
    pick_ref[1] = jnp.where(wanted == here, 0, jnp.where(wanted == (here ^ 2), 1, 2))

    lanes = wide.shape[2]
    for i in range(chunks):
        copies[1 + i].wait()
        at = slice(i * chunk * groups, (i + 1) * chunk * groups)
        for part in range(wide.shape[0]):
            values = rows_ref[i * chunk : (i + 1) * chunk, :, part * lanes : (part + 1) * lanes]
            wide[part, at] = values.astype(F32).reshape(chunk * groups, lanes)
        for group in range(groups):
            for part in range(wide.shape[0]):
                start = group * width + part * lanes
                picked = wide[part, pl.ds(at.start + group, chunk, stride=groups), :]
                packed[i * chunk : (i + 1) * chunk, start : start + lanes] = picked.astype(BF16)
    for group in range(groups):
        copies[1 + chunks + group].wait()
    copies[1 + chunks + groups].wait()
    gain = gain_ref[...].astype(F32)[None]
    projected = dot(packed[...], weight_ref[...])
    scale = lax.rsqrt(jnp.mean(projected * projected, axis=-1, keepdims=True) + 1e-06)
    latent_ref[...] = (projected * scale * gain).astype(BF16)

    copies[2 + chunks + groups].wait()
    new_count, heads, head_size = query_ref.shape
    query = query_ref[...].astype(F32)
    upper = lax.axis_index("seq") == 1
    query = jnp.where(upper, query[:, heads // 2 :], query[:, : heads // 2])
    half_ref[...] = query.reshape(half_ref.shape).astype(BF16)


def score_kernel(parts, *refs):
    latent_refs, (lift_ref, query_ref), (score_ref, value_ref, top_ref) = (
        refs[:parts],
        refs[parts : parts + 2],
        refs[parts + 2 :],
    )
    head_size = query_ref.shape[-1]
    lift = lift_ref[lax.axis_index("seq")]
    query = query_ref[...]
    top = None
    for part, latent_ref in enumerate(latent_refs):
        tokens = latent_ref.shape[0]
        at = slice(part * tokens, (part + 1) * tokens)
        lifted = dot(latent_ref[...], lift).astype(BF16)
        score = lax.dot_general(
            lifted[:, :head_size], query, (((1,), (1,)), ((), ())), preferred_element_type=F32
        )
        score_ref[at] = score
        value_ref[at] = lifted[:, head_size:]
        part_top = jnp.max(score, axis=0, keepdims=True)
        top = part_top if top is None else jnp.maximum(top, part_top)
    top_ref[...] = jnp.broadcast_to(top, top_ref.shape)


def fetch_kernel(weight_ref, own_ref, sent_ref, kept_ref, sems):
    core = lax.axis_index("tensor") % 2
    depth, columns = sent_ref.shape
    rows = depth // COPIES
    group = lax.axis_index("seq")
    copies = []
    for part, (held_ref, half, first) in enumerate(
        ((own_ref, group, 0), (sent_ref, 1 - group, 1 - core), (kept_ref, 1 - group, core))
    ):
        first = pl.multiple_of(first * columns, columns)
        for i in range(COPIES):
            start = pl.multiple_of(half * depth + i * rows, rows)
            source = weight_ref.at[pl.ds(start, rows), pl.ds(first, held_ref.shape[1])]
            target = held_ref.at[pl.ds(i * rows, rows)]
            copies.append(pltpu.make_async_copy(source, target, sems.at[part, i]))
    for copy in copies:
        copy.start()
    for copy in copies:
        copy.wait()


def fetch(weight):
    depth, columns = weight.shape[0] // 2, weight.shape[1]
    return call(
        fetch_kernel,
        "fetch",
        [pltpu.VMEM((depth, width), weight.dtype) for width in (columns, columns // 2, columns // 2)],
        [weight],
        4,
        scratch=[pltpu.SemaphoreType.DMA((3, COPIES))],
        hbm_in=1,
        cost=cost(0, 0),
    )


def choose(pick, refs, out_ref):
    for i, ref in enumerate(refs):

        @pl.when(pick == i)
        def _():
            out_ref[...] = ref[...]


def pass_kernel(pick_ref, own_ref, second_ref, near_ref, far_ref, out_ref, upper_ref, lower_ref):
    choose(pick_ref[0], (own_ref, second_ref), out_ref)
    half = upper_ref.shape[0]
    upper_ref[...] = near_ref[:half]
    lower_ref[...] = far_ref[half:]


def choose_and_score_kernel(parts, pick_ref, *refs):
    *refs, score_ref, value_ref, top_ref, query_ref = refs
    choose(pick_ref[1], refs[parts + 1 :], query_ref)
    score_kernel(parts, *refs[: parts + 1], query_ref, score_ref, value_ref, top_ref)


def score_call(name, latents, lift, query, pick=None):
    queries = [query] if pick is None else query
    tokens = sum(latent.shape[0] for latent in latents)
    rows, head_size = queries[0].shape
    outs = [shape((tokens, rows), F32), shape((tokens, head_size), BF16), shape((8, rows), F32)]
    operands = [*latents, lift, *queries]
    estimate = cost(0, 0)
    if pick is None:
        body = lambda *refs: score_kernel(len(latents), *refs)
        return call(body, name, outs, operands, 16, cost=estimate)
    body = lambda *refs: choose_and_score_kernel(len(latents), *refs)
    outs.append(shape((rows, head_size), BF16))
    return call(body, name, outs, [pick, *operands], 16, smem_in=1, cost=estimate)


def attend_kernel(block, *refs):
    (*score_refs, out_ref, turned) = refs
    new_count = out_ref.shape[0]
    triples = [score_refs[i : i + 3] for i in range(0, len(score_refs), 3)]
    head_size = triples[0][1].shape[-1]
    coef = head_size ** (-0.5) * math.log2(math.e)
    top = triples[0][2][:1]
    for triple in triples[1:]:
        top = jnp.maximum(top, triple[2][:1])
    total = jnp.zeros_like(top)
    summed = jnp.zeros((head_size, top.shape[1]), F32)
    for score_ref, value_ref, _ in triples:
        for start in range(0, score_ref.shape[0], block):
            at = slice(start, start + block)
            expo = jnp.exp2((score_ref[at] - top) * coef)
            total += jnp.sum(expo, axis=0, keepdims=True)
            summed += lax.dot_general(
                value_ref[at], expo.astype(BF16), (((0,), (0,)), ((), ())), preferred_element_type=F32
            )
    turned[...] = (summed / total).T
    heads = turned.shape[0] // new_count
    for head in range(heads):
        out_ref[:, head * head_size : (head + 1) * head_size] = turned[
            pl.ds(head, new_count, stride=heads), :
        ].astype(BF16)


def project_kernel(tile, rows_ref, weight_ref, out_ref):
    rows = rows_ref[...]
    width = out_ref.shape[2]
    for part in range(out_ref.shape[0]):
        for column in range(0, width, tile):
            at = part * width + column
            out_ref[part, :, column : column + tile] = dot(
                rows, weight_ref[:, at : at + tile]
            )


def project_more_kernel(tile, own, kept, rows_ref, weight_ref, before_ref, out_ref):
    here = lax.axis_index("tensor")
    core, chip = here % 2, here // 2
    half = core if own else 1 - core
    width = out_ref.shape[1]
    start = (chip if kept else 1 - chip) * width
    rows = rows_ref[...]
    for column in range(0, width, tile):
        at = pl.ds(pl.multiple_of(start + column, tile), tile)
        out_ref[:, column : column + tile] = before_ref[half, :, at] + dot(rows, weight_ref[:, at])


def add_kernel(one_ref, other_ref, out_ref):
    out_ref[...] = one_ref[...] + other_ref[...]


def sum_kernel(own_ref, beside_ref, across_ref, out_ref):
    out_ref[...] = (own_ref[...] + beside_ref[...] + across_ref[...]).astype(out_ref.dtype)


def join_kernel(places, *refs):
    pieces = refs[: len(places)]
    out_ref, sems = refs[-2:]
    here = lax.axis_index("tensor")
    core, chip = here % 2, here // 2
    width = pieces[0].shape[1]
    copies = []
    for i, place in enumerate(places):
        at = 2 * (1 - core if place // 2 else core) + (1 - chip if place % 2 else chip)
        at = pl.ds(pl.multiple_of(at * width, width), width)
        copies.append(pltpu.make_async_copy(pieces[i], out_ref.at[0, :, at], sems.at[i]))
    for copy in copies:
        copy.start()
    for copy in copies:
        copy.wait()


def join(places, pieces, before):
    new_count, width = pieces[0].shape
    return pl.pallas_call(
        lambda *refs: join_kernel(places, *refs),
        out_shape=shape((1, new_count, 4 * width), BF16),
        in_specs=[IN_VMEM] * len(places) + ([] if before is None else [IN_HBM]),
        out_specs=IN_HBM,
        scratch_shapes=[pltpu.SemaphoreType.DMA((len(places),))],
        input_output_aliases={} if before is None else {len(places): 0},
        compiler_params=pltpu.CompilerParams(vmem_limit_bytes=4 * MIB),
        name="join",
    )(*pieces, *([] if before is None else [before]))


def square_shards(key_value_rows, queries, w_comp, latent_gain, w_up, w_out, replica_order):
    orders = list(itertools.permutations(range(lax.axis_size("rep"))))
    _, new_count, heads, head_size = queries.shape
    _, tokens, all_groups, width = key_value_rows.shape
    latent_width = w_comp.shape[1]
    rows = heads // 2 * new_count

    chunks = 3 if tokens % 48 == 0 else 1
    latent, query, index, pick = call(
        lambda *refs: compress_kernel(chunks, *refs),
        "compress",
        [shape((tokens, latent_width), BF16), shape((rows, head_size), BF16), *[shape((n,), jnp.int32) for n in (1, 2)]],
        [replica_order, key_value_rows, w_comp, latent_gain, queries],
        16,
        scratch=[
            pltpu.SMEM(replica_order.shape, jnp.int32),
            pltpu.VMEM(key_value_rows.shape[1:], BF16),
            pltpu.VMEM(w_comp.shape, BF16),
            pltpu.VMEM(latent_gain.shape, BF16),
            pltpu.VMEM(queries.shape[1:], BF16),
            pltpu.VMEM((width // 128, tokens * all_groups, 128), F32),
            pltpu.VMEM((tokens, all_groups * width), BF16),
            pltpu.SemaphoreType.DMA((3 + chunks + all_groups,)),
        ],
        hbm_in=5,
        smem_out=2,
        cost=cost(0, 0),
    )

    near = swap(latent, "seq", 1)
    far = swap(latent, "tensor", 2)
    second_query = swap(query, "rep", 2)
    held, held_sent, held_kept = fetch(w_out)
    near, far, second_query, held = lax.optimization_barrier((near, far, second_query, held))
    passed, upper, lower = call(
        pass_kernel,
        "pass",
        [shape(query.shape, query.dtype)] + [shape((tokens // 2, latent_width), BF16)] * 2,
        [pick, query, second_query, near, far],
        4,
        smem_in=1,
        cost=cost(0, 0),
    )
    corner = [swap(upper, "tensor", 2), swap(lower, "seq", 1)]
    passed = swap(passed, "rep", 1)
    given, near, far, _ = lax.optimization_barrier((latent, near, far, upper))
    besides = [swap(piece, "tensor", 1) for piece in (given, near, far)]
    choices = [query, second_query, passed]
    *first, query = score_call("score_here", [given, near, far], w_up, choices, pick)
    corner, first[2] = lax.optimization_barrier((corner, first[2]))
    corner += [swap(piece, "tensor", 1) for piece in corner]
    second = list(score_call("score_beside", besides, w_up, query))
    corner[2], second[2] = lax.optimization_barrier((corner[2], second[2]))
    third = score_call("score_corner", corner, w_up, query)
    depth = rows // new_count * head_size
    (attended,) = call(
        lambda *refs: attend_kernel(tokens, *refs),
        "attend",
        [shape((new_count, depth), BF16)],
        [*first, *second, *third],
        16,
        scratch=[pltpu.VMEM((rows, head_size), F32)],
        cost=cost(0, 0),
    )
    attended_other = swap(attended, "seq", 1)
    columns = w_out.shape[1]
    tile = min(512, columns // 2)
    (partial,) = call(
        lambda *refs: project_kernel(tile, *refs),
        "project",
        [shape((2, new_count, columns // 2), F32)],
        [attended, held],
        12,
        cost=cost(0, 0),
    )

    quarter = (new_count, columns // 4)

    def project_more(other, own, kept):
        return call(
            lambda *refs: project_more_kernel(tile, own, kept, *refs),
            "project_own" if own else "project_sent",
            [shape(quarter, F32)],
            [other, held_kept if own else held_sent, partial],
            12,
            cost=cost(0, 0),
        )[0]

    given = swap(project_more(attended_other, False, False), "tensor", 1)
    operands = [project_more(attended_other, True, False), given]
    operands[0], other = lax.optimization_barrier((operands[0], attended_other))
    kept = project_more(other, False, True)
    (given,) = call(add_kernel, "add", [shape(quarter, F32)], operands, 8, cost=cost(0, 0))
    other, given, kept = lax.optimization_barrier((attended_other, given, kept))
    given = swap(given, "tensor", 2)
    kept = swap(kept, "tensor", 1)
    operands = [project_more(other, True, True), kept, given]
    (own,) = call(sum_kernel, "sum", [shape(quarter, BF16)], operands, 8, cost=cost(0, 0))

    def reply(order):
        pairs = [(p * 4 + t, r * 4 + t) for r, p in enumerate(order) for t in range(4)]
        crossed = [(source, target ^ 2) for source, target in pairs]
        axes = ("rep", "tensor")

        def run(value):
            across = lax.ppermute(value, axes, crossed)
            if order == tuple(range(len(order))):
                return value, across
            return lax.ppermute(value, axes, pairs), across

        return run

    own, across = lax.switch(index[0], [reply(order) for order in orders], own)
    beside, last = swap(own, "tensor", 1), swap(across, "tensor", 1)
    joined = join((0, 1), [own, across], None)
    return join((2, 3), [beside, last], joined)


def shards(key_value_rows, queries, w_comp, latent_gain, w_up, w_out, replica_order):
    orders = list(itertools.permutations(range(lax.axis_size("rep"))))
    index = order_index(replica_order, orders)
    query = route(queries[0], index, orders, False)
    rows = key_value_rows[0]
    latent = compress(rows.reshape(rows.shape[0], -1), w_comp, latent_gain)
    latent = lax.all_gather(latent, "tensor", axis=0, tiled=True)
    groups = w_up.shape[0]
    lifted = jnp.einsum("tf,gfy->tgy", latent, w_up, preferred_element_type=F32).astype(BF16)
    head_size = query.shape[-1]
    new_count = query.shape[0]
    keys = lifted[..., :head_size]
    values = lifted[..., head_size:]
    grouped_heads = query.reshape(new_count, groups, -1, head_size)
    scores = jnp.einsum(
        "nghd,tgd->nght", grouped_heads, keys, preferred_element_type=F32
    ) * head_size ** (-0.5)
    top = lax.pmax(jnp.max(scores, axis=-1), "seq")
    expo = jnp.exp(scores - top[..., None])
    total = jnp.sum(expo, axis=-1)
    summed = jnp.einsum("nght,tgd->nghd", expo.astype(BF16), values, preferred_element_type=F32)
    summed, total = lax.psum((summed, total), "seq")
    attended = (summed / total[..., None]).astype(BF16).reshape(new_count, -1)
    attended = route(attended, index, orders, True)
    return lax.psum(dot(attended, w_out), "tensor").astype(BF16)[None]


def solution(mesh):
    placed = (
        P("rep", ("seq", "tensor"), None, None),
        P("rep", None, "tensor", None),
        P(),
        P(),
        P("tensor", None, None),
        P("tensor", "seq"),
        P(),
    )
    square = all(mesh.shape[axis] == size for axis, size in (("seq", 2), ("rep", 4), ("tensor", 4)))
    return jax.shard_map(
        square_shards if square else shards,
        mesh=mesh,
        in_specs=placed,
        out_specs=P("rep", None, "seq"),
        check_vma=False,
    )
```

```python
import itertools
import math

import jax
import jax.numpy as jnp
from jax import lax
from jax.experimental import pallas as pl
from jax.experimental.pallas import tpu as pltpu
from jax.sharding import PartitionSpec as P

BF16, F32 = jnp.bfloat16, jnp.float32
MIB = 1024 * 1024
IN_VMEM = pl.BlockSpec(memory_space=pltpu.VMEM)
IN_SMEM = pl.BlockSpec(memory_space=pltpu.SMEM)
IN_HBM = pl.BlockSpec(memory_space=pltpu.HBM)
COPIES = 8


def shape(dims, dtype):
    return jax.ShapeDtypeStruct(dims, dtype)


def call(body, name, outs, operands, vmem, scratch=(), smem_in=0, smem_out=0, hbm_in=0, cost=None):
    kept = len(operands) - hbm_in
    specs = [IN_SMEM] * smem_in + [IN_VMEM] * (kept - smem_in) + [IN_HBM] * hbm_in
    operands = [
        *operands[:kept],
        *(pltpu.with_memory_space_constraint(operand, pltpu.HBM) for operand in operands[kept:]),
    ]
    out_specs = [IN_VMEM] * (len(outs) - smem_out) + [IN_SMEM] * smem_out
    return pl.pallas_call(
        body,
        out_shape=outs,
        in_specs=specs,
        out_specs=out_specs,
        scratch_shapes=list(scratch),
        compiler_params=pltpu.CompilerParams(vmem_limit_bytes=vmem * MIB),
        cost_estimate=cost,
        name=name,
    )(*operands)


def cost(flops, moved, exps=0):
    return pl.CostEstimate(flops=int(flops), bytes_accessed=int(moved), transcendentals=int(exps))


def dot(a, b):
    return jnp.dot(a, b, preferred_element_type=F32)


def compress(rows, weight, gain):
    projected = dot(rows, weight)
    scale = lax.rsqrt(jnp.mean(projected * projected, axis=-1, keepdims=True) + 1e-06)
    return (projected * scale * gain.astype(F32)[None]).astype(BF16)


def order_index(replica_order, orders):
    table = jnp.array(orders, jnp.int32)
    match = jnp.all(table == replica_order[None], axis=1)
    return jnp.sum(jnp.where(match, lax.iota(jnp.int32, len(orders)), 0))


def route_pairs(order, back):
    return [(p, r) if back else (r, p) for r, p in enumerate(order)]


def route(value, index, orders, back):
    def branch(order):
        return lambda v: lax.ppermute(v, "rep", route_pairs(order, back))

    return lax.switch(index, [branch(o) for o in orders], value)


def shift(value, axis, hops):
    size = lax.axis_size(axis)
    return lax.ppermute(value, axis, [(i, (i + hops) % size) for i in range(size)])


def swap(value, axis, bit):
    pairs = [(i, i ^ bit) for i in range(lax.axis_size(axis))]
    return lax.ppermute(value, axis, pairs)


def compress_kernel(chunks, *refs):
    (order_hbm, rows_hbm, weight_hbm, gain_hbm, query_hbm, latent_ref, half_ref, index_ref, pick_ref) = refs[:9]
    (order_ref, rows_ref, weight_ref, gain_ref, query_ref, wide, packed, sems) = refs[9:]
    tokens, groups, width = rows_ref.shape
    chunk = tokens // chunks
    copies = [pltpu.make_async_copy(order_hbm, order_ref, sems.at[0])]
    for i in range(chunks):
        at = pl.ds(i * chunk, chunk)
        copies.append(pltpu.make_async_copy(rows_hbm.at[0, at], rows_ref.at[at], sems.at[1 + i]))
    for group in range(groups):
        at = pl.ds(group * width, width)
        copies.append(
            pltpu.make_async_copy(weight_hbm.at[at], weight_ref.at[at], sems.at[1 + chunks + group])
        )
    copies.append(pltpu.make_async_copy(gain_hbm, gain_ref, sems.at[1 + chunks + groups]))
    copies.append(pltpu.make_async_copy(query_hbm.at[0], query_ref, sems.at[2 + chunks + groups]))
    for copy in copies:
        copy.start()

    copies[0].wait()
    count = order_ref.shape[0]
    here = lax.axis_index("rep")
    index, wanted, wanted_beside = 0, 0, 0
    for i in range(count):
        wanted = jnp.where(order_ref[i] == here, i, wanted)
        wanted_beside = jnp.where(order_ref[i] == (here ^ 1), i, wanted_beside)
        smaller = 0
        for j in range(i + 1, count):
            smaller = smaller + (order_ref[j] < order_ref[i]).astype(jnp.int32)
        index = index + smaller * math.factorial(count - 1 - i)
    index_ref[0] = index
    pick_ref[0] = (wanted_beside == (here ^ 2)).astype(jnp.int32)
    pick_ref[1] = jnp.where(wanted == here, 0, jnp.where(wanted == (here ^ 2), 1, 2))

    lanes = wide.shape[2]
    for i in range(chunks):
        copies[1 + i].wait()
        at = slice(i * chunk * groups, (i + 1) * chunk * groups)
        for part in range(wide.shape[0]):
            values = rows_ref[i * chunk : (i + 1) * chunk, :, part * lanes : (part + 1) * lanes]
            wide[part, at] = values.astype(F32).reshape(chunk * groups, lanes)
        for group in range(groups):
            for part in range(wide.shape[0]):
                start = group * width + part * lanes
                picked = wide[part, pl.ds(at.start + group, chunk, stride=groups), :]
                packed[i * chunk : (i + 1) * chunk, start : start + lanes] = picked.astype(BF16)
    for group in range(groups):
        copies[1 + chunks + group].wait()
    copies[1 + chunks + groups].wait()
    gain = gain_ref[...].astype(F32)[None]
    projected = dot(packed[...], weight_ref[...])
    scale = lax.rsqrt(jnp.mean(projected * projected, axis=-1, keepdims=True) + 1e-06)
    latent_ref[...] = (projected * scale * gain).astype(BF16)

    copies[2 + chunks + groups].wait()
    new_count, heads, head_size = query_ref.shape
    query = query_ref[...].astype(F32)
    upper = lax.axis_index("seq") == 1
    query = jnp.where(upper, query[:, heads // 2 :], query[:, : heads // 2])
    half_ref[...] = query.reshape(half_ref.shape).astype(BF16)


def score_kernel(parts, *refs):
    latent_refs, (lift_ref, query_ref), (score_ref, value_ref, top_ref) = (
        refs[:parts],
        refs[parts : parts + 2],
        refs[parts + 2 :],
    )
    head_size = query_ref.shape[-1]
    lift = lift_ref[lax.axis_index("seq")]
    query = query_ref[...]
    top = None
    for part, latent_ref in enumerate(latent_refs):
        tokens = latent_ref.shape[0]
        at = slice(part * tokens, (part + 1) * tokens)
        lifted = dot(latent_ref[...], lift).astype(BF16)
        score = lax.dot_general(
            lifted[:, :head_size], query, (((1,), (1,)), ((), ())), preferred_element_type=F32
        )
        score_ref[at] = score
        value_ref[at] = lifted[:, head_size:]
        part_top = jnp.max(score, axis=0, keepdims=True)
        top = part_top if top is None else jnp.maximum(top, part_top)
    top_ref[...] = jnp.broadcast_to(top, top_ref.shape)


def fetch_kernel(weight_ref, own_ref, sent_ref, kept_ref, sems):
    core = lax.axis_index("tensor") % 2
    depth, columns = sent_ref.shape
    rows = depth // COPIES
    group = lax.axis_index("seq")
    copies = []
    for part, (held_ref, half, first) in enumerate(
        ((own_ref, group, 0), (sent_ref, 1 - group, 1 - core), (kept_ref, 1 - group, core))
    ):
        first = pl.multiple_of(first * columns, columns)
        for i in range(COPIES):
            start = pl.multiple_of(half * depth + i * rows, rows)
            source = weight_ref.at[pl.ds(start, rows), pl.ds(first, held_ref.shape[1])]
            target = held_ref.at[pl.ds(i * rows, rows)]
            copies.append(pltpu.make_async_copy(source, target, sems.at[part, i]))
    for copy in copies:
        copy.start()
    for copy in copies:
        copy.wait()


def fetch(weight):
    depth, columns = weight.shape[0] // 2, weight.shape[1]
    return call(
        fetch_kernel,
        "fetch",
        [pltpu.VMEM((depth, width), weight.dtype) for width in (columns, columns // 2, columns // 2)],
        [weight],
        4,
        scratch=[pltpu.SemaphoreType.DMA((3, COPIES))],
        hbm_in=1,
        cost=cost(0, 0),
    )


def choose(pick, refs, out_ref):
    for i, ref in enumerate(refs):

        @pl.when(pick == i)
        def _():
            out_ref[...] = ref[...]


def pass_kernel(pick_ref, own_ref, second_ref, out_ref):
    choose(pick_ref[0], (own_ref, second_ref), out_ref)


def halve_kernel(near_ref, far_ref, upper_ref, lower_ref):
    half = upper_ref.shape[0]
    upper_ref[...] = near_ref[:half]
    lower_ref[...] = far_ref[half:]


def choose_and_score_kernel(parts, pick_ref, *refs):
    *refs, score_ref, value_ref, top_ref, query_ref = refs
    choose(pick_ref[1], refs[parts + 1 :], query_ref)
    score_kernel(parts, *refs[: parts + 1], query_ref, score_ref, value_ref, top_ref)


def score_call(name, latents, lift, query, pick=None):
    queries = [query] if pick is None else query
    tokens = sum(latent.shape[0] for latent in latents)
    rows, head_size = queries[0].shape
    outs = [shape((tokens, rows), F32), shape((tokens, head_size), BF16), shape((8, rows), F32)]
    operands = [*latents, lift, *queries]
    estimate = cost(0, 0)
    if pick is None:
        body = lambda *refs: score_kernel(len(latents), *refs)
        return call(body, name, outs, operands, 16, cost=estimate)
    body = lambda *refs: choose_and_score_kernel(len(latents), *refs)
    outs.append(shape((rows, head_size), BF16))
    return call(body, name, outs, [pick, *operands], 16, smem_in=1, cost=estimate)


def attend_kernel(block, *refs):
    (*score_refs, out_ref, turned) = refs
    new_count = out_ref.shape[0]
    triples = [score_refs[i : i + 3] for i in range(0, len(score_refs), 3)]
    head_size = triples[0][1].shape[-1]
    coef = head_size ** (-0.5) * math.log2(math.e)
    top = triples[0][2][:1]
    for triple in triples[1:]:
        top = jnp.maximum(top, triple[2][:1])
    total = jnp.zeros_like(top)
    summed = jnp.zeros((head_size, top.shape[1]), F32)
    for score_ref, value_ref, _ in triples:
        for start in range(0, score_ref.shape[0], block):
            at = slice(start, start + block)
            expo = jnp.exp2((score_ref[at] - top) * coef)
            total += jnp.sum(expo, axis=0, keepdims=True)
            summed += lax.dot_general(
                value_ref[at], expo.astype(BF16), (((0,), (0,)), ((), ())), preferred_element_type=F32
            )
    turned[...] = (summed / total).T
    heads = turned.shape[0] // new_count
    for head in range(heads):
        out_ref[:, head * head_size : (head + 1) * head_size] = turned[
            pl.ds(head, new_count, stride=heads), :
        ].astype(BF16)


def project_kernel(tile, rows_ref, weight_ref, out_ref):
    rows = rows_ref[...]
    width = out_ref.shape[2]
    for part in range(out_ref.shape[0]):
        for column in range(0, width, tile):
            at = part * width + column
            out_ref[part, :, column : column + tile] = dot(
                rows, weight_ref[:, at : at + tile]
            )


def project_more_kernel(tile, own, kept, rows_ref, weight_ref, before_ref, out_ref):
    here = lax.axis_index("tensor")
    core, chip = here % 2, here // 2
    half = core if own else 1 - core
    width = out_ref.shape[1]
    start = (chip if kept else 1 - chip) * width
    rows = rows_ref[...]
    for column in range(0, width, tile):
        at = pl.ds(pl.multiple_of(start + column, tile), tile)
        out_ref[:, column : column + tile] = before_ref[half, :, at] + dot(rows, weight_ref[:, at])


def add_kernel(one_ref, other_ref, out_ref):
    out_ref[...] = one_ref[...] + other_ref[...]


def sum_kernel(own_ref, beside_ref, across_ref, out_ref):
    out_ref[...] = (own_ref[...] + beside_ref[...] + across_ref[...]).astype(out_ref.dtype)


def join_kernel(places, *refs):
    pieces = refs[: len(places)]
    out_ref, sems = refs[-2:]
    here = lax.axis_index("tensor")
    core, chip = here % 2, here // 2
    width = pieces[0].shape[1]
    copies = []
    for i, place in enumerate(places):
        at = 2 * (1 - core if place // 2 else core) + (1 - chip if place % 2 else chip)
        at = pl.ds(pl.multiple_of(at * width, width), width)
        copies.append(pltpu.make_async_copy(pieces[i], out_ref.at[0, :, at], sems.at[i]))
    for copy in copies:
        copy.start()
    for copy in copies:
        copy.wait()


def join(places, pieces, before):
    new_count, width = pieces[0].shape
    return pl.pallas_call(
        lambda *refs: join_kernel(places, *refs),
        out_shape=shape((1, new_count, 4 * width), BF16),
        in_specs=[IN_VMEM] * len(places) + ([] if before is None else [IN_HBM]),
        out_specs=IN_HBM,
        scratch_shapes=[pltpu.SemaphoreType.DMA((len(places),))],
        input_output_aliases={} if before is None else {len(places): 0},
        compiler_params=pltpu.CompilerParams(vmem_limit_bytes=4 * MIB),
        name="join",
    )(*pieces, *([] if before is None else [before]))


def square_shards(key_value_rows, queries, w_comp, latent_gain, w_up, w_out, replica_order):
    orders = list(itertools.permutations(range(lax.axis_size("rep"))))
    _, new_count, heads, head_size = queries.shape
    _, tokens, all_groups, width = key_value_rows.shape
    latent_width = w_comp.shape[1]
    rows = heads // 2 * new_count

    chunks = 3 if tokens % 48 == 0 else 1
    latent, query, index, pick = call(
        lambda *refs: compress_kernel(chunks, *refs),
        "compress",
        [shape((tokens, latent_width), BF16), shape((rows, head_size), BF16), *[shape((n,), jnp.int32) for n in (1, 2)]],
        [replica_order, key_value_rows, w_comp, latent_gain, queries],
        16,
        scratch=[
            pltpu.SMEM(replica_order.shape, jnp.int32),
            pltpu.VMEM(key_value_rows.shape[1:], BF16),
            pltpu.VMEM(w_comp.shape, BF16),
            pltpu.VMEM(latent_gain.shape, BF16),
            pltpu.VMEM(queries.shape[1:], BF16),
            pltpu.VMEM((width // 128, tokens * all_groups, 128), F32),
            pltpu.VMEM((tokens, all_groups * width), BF16),
            pltpu.SemaphoreType.DMA((3 + chunks + all_groups,)),
        ],
        hbm_in=5,
        smem_out=2,
        cost=cost(0, 0),
    )

    near = swap(latent, "seq", 1)
    far = swap(latent, "tensor", 2)
    second_query = swap(query, "rep", 2)
    held, held_sent, held_kept = fetch(w_out)
    second_query, held = lax.optimization_barrier((second_query, held))
    (passed,) = call(
        pass_kernel,
        "pass",
        [shape(query.shape, query.dtype)],
        [pick, query, second_query],
        4,
        smem_in=1,
        cost=cost(0, 0),
    )
    near, far, _ = lax.optimization_barrier((near, far, passed))
    upper, lower = call(
        halve_kernel,
        "halve",
        [shape((tokens // 2, latent_width), BF16)] * 2,
        [near, far],
        4,
        cost=cost(0, 0),
    )
    corner = [swap(upper, "tensor", 2), swap(lower, "seq", 1)]
    passed = swap(passed, "rep", 1)
    given, near, far, _ = lax.optimization_barrier((latent, near, far, upper))
    besides = [swap(piece, "tensor", 1) for piece in (given, near, far)]
    choices = [query, second_query, passed]
    *first, query = score_call("score_here", [given, near, far], w_up, choices, pick)
    corner, first[2] = lax.optimization_barrier((corner, first[2]))
    corner += [swap(piece, "tensor", 1) for piece in corner]
    second = list(score_call("score_beside", besides, w_up, query))
    corner[2], second[2] = lax.optimization_barrier((corner[2], second[2]))
    third = score_call("score_corner", corner, w_up, query)
    depth = rows // new_count * head_size
    (attended,) = call(
        lambda *refs: attend_kernel(tokens, *refs),
        "attend",
        [shape((new_count, depth), BF16)],
        [*first, *second, *third],
        16,
        scratch=[pltpu.VMEM((rows, head_size), F32)],
        cost=cost(0, 0),
    )
    attended_other = swap(attended, "seq", 1)
    columns = w_out.shape[1]
    tile = min(512, columns // 2)
    (partial,) = call(
        lambda *refs: project_kernel(tile, *refs),
        "project",
        [shape((2, new_count, columns // 2), F32)],
        [attended, held],
        12,
        cost=cost(0, 0),
    )

    quarter = (new_count, columns // 4)

    def project_more(other, own, kept):
        return call(
            lambda *refs: project_more_kernel(tile, own, kept, *refs),
            "project_own" if own else "project_sent",
            [shape(quarter, F32)],
            [other, held_kept if own else held_sent, partial],
            12,
            cost=cost(0, 0),
        )[0]

    given = swap(project_more(attended_other, False, False), "tensor", 1)
    operands = [project_more(attended_other, True, False), given]
    operands[0], other = lax.optimization_barrier((operands[0], attended_other))
    kept = project_more(other, False, True)
    (given,) = call(add_kernel, "add", [shape(quarter, F32)], operands, 8, cost=cost(0, 0))
    other, given, kept = lax.optimization_barrier((attended_other, given, kept))
    given = swap(given, "tensor", 2)
    kept = swap(kept, "tensor", 1)
    operands = [project_more(other, True, True), kept, given]
    (own,) = call(sum_kernel, "sum", [shape(quarter, BF16)], operands, 8, cost=cost(0, 0))

    def reply(order):
        pairs = [(p * 4 + t, r * 4 + t) for r, p in enumerate(order) for t in range(4)]
        crossed = [(source, target ^ 2) for source, target in pairs]
        axes = ("rep", "tensor")

        def run(value):
            across = lax.ppermute(value, axes, crossed)
            if order == tuple(range(len(order))):
                return value, across
            return lax.ppermute(value, axes, pairs), across

        return run

    own, across = lax.switch(index[0], [reply(order) for order in orders], own)
    beside, last = swap(own, "tensor", 1), swap(across, "tensor", 1)
    joined = join((0, 1), [own, across], None)
    return join((2, 3), [beside, last], joined)


def shards(key_value_rows, queries, w_comp, latent_gain, w_up, w_out, replica_order):
    orders = list(itertools.permutations(range(lax.axis_size("rep"))))
    index = order_index(replica_order, orders)
    query = route(queries[0], index, orders, False)
    rows = key_value_rows[0]
    latent = compress(rows.reshape(rows.shape[0], -1), w_comp, latent_gain)
    latent = lax.all_gather(latent, "tensor", axis=0, tiled=True)
    groups = w_up.shape[0]
    lifted = jnp.einsum("tf,gfy->tgy", latent, w_up, preferred_element_type=F32).astype(BF16)
    head_size = query.shape[-1]
    new_count = query.shape[0]
    keys = lifted[..., :head_size]
    values = lifted[..., head_size:]
    grouped_heads = query.reshape(new_count, groups, -1, head_size)
    scores = jnp.einsum(
        "nghd,tgd->nght", grouped_heads, keys, preferred_element_type=F32
    ) * head_size ** (-0.5)
    top = lax.pmax(jnp.max(scores, axis=-1), "seq")
    expo = jnp.exp(scores - top[..., None])
    total = jnp.sum(expo, axis=-1)
    summed = jnp.einsum("nght,tgd->nghd", expo.astype(BF16), values, preferred_element_type=F32)
    summed, total = lax.psum((summed, total), "seq")
    attended = (summed / total[..., None]).astype(BF16).reshape(new_count, -1)
    attended = route(attended, index, orders, True)
    return lax.psum(dot(attended, w_out), "tensor").astype(BF16)[None]


def solution(mesh):
    placed = (
        P("rep", ("seq", "tensor"), None, None),
        P("rep", None, "tensor", None),
        P(),
        P(),
        P("tensor", None, None),
        P("tensor", "seq"),
        P(),
    )
    square = all(mesh.shape[axis] == size for axis, size in (("seq", 2), ("rep", 4), ("tensor", 4)))
    return jax.shard_map(
        square_shards if square else shards,
        mesh=mesh,
        in_specs=placed,
        out_specs=P("rep", None, "seq"),
        check_vma=False,
    )
```

```python
import itertools
import math

import jax
import jax.numpy as jnp
from jax import lax
from jax.experimental import pallas as pl
from jax.experimental.pallas import tpu as pltpu
from jax.sharding import PartitionSpec as P

BF16, F32 = jnp.bfloat16, jnp.float32
MIB = 1024 * 1024
IN_VMEM = pl.BlockSpec(memory_space=pltpu.VMEM)
IN_SMEM = pl.BlockSpec(memory_space=pltpu.SMEM)
IN_HBM = pl.BlockSpec(memory_space=pltpu.HBM)
COPIES = 8


def shape(dims, dtype):
    return jax.ShapeDtypeStruct(dims, dtype)


def call(body, name, outs, operands, vmem, scratch=(), smem_in=0, smem_out=0, hbm_in=0, cost=None):
    kept = len(operands) - hbm_in
    specs = [IN_SMEM] * smem_in + [IN_VMEM] * (kept - smem_in) + [IN_HBM] * hbm_in
    operands = [
        *operands[:kept],
        *(pltpu.with_memory_space_constraint(operand, pltpu.HBM) for operand in operands[kept:]),
    ]
    out_specs = [IN_VMEM] * (len(outs) - smem_out) + [IN_SMEM] * smem_out
    return pl.pallas_call(
        body,
        out_shape=outs,
        in_specs=specs,
        out_specs=out_specs,
        scratch_shapes=list(scratch),
        compiler_params=pltpu.CompilerParams(vmem_limit_bytes=vmem * MIB),
        cost_estimate=cost,
        name=name,
    )(*operands)


def cost(flops, moved, exps=0):
    return pl.CostEstimate(flops=int(flops), bytes_accessed=int(moved), transcendentals=int(exps))


def dot(a, b):
    return jnp.dot(a, b, preferred_element_type=F32)


def compress(rows, weight, gain):
    projected = dot(rows, weight)
    scale = lax.rsqrt(jnp.mean(projected * projected, axis=-1, keepdims=True) + 1e-06)
    return (projected * scale * gain.astype(F32)[None]).astype(BF16)


def order_index(replica_order, orders):
    table = jnp.array(orders, jnp.int32)
    match = jnp.all(table == replica_order[None], axis=1)
    return jnp.sum(jnp.where(match, lax.iota(jnp.int32, len(orders)), 0))


def route_pairs(order, back):
    return [(p, r) if back else (r, p) for r, p in enumerate(order)]


def route(value, index, orders, back):
    def branch(order):
        return lambda v: lax.ppermute(v, "rep", route_pairs(order, back))

    return lax.switch(index, [branch(o) for o in orders], value)


def shift(value, axis, hops):
    size = lax.axis_size(axis)
    return lax.ppermute(value, axis, [(i, (i + hops) % size) for i in range(size)])


def swap(value, axis, bit):
    pairs = [(i, i ^ bit) for i in range(lax.axis_size(axis))]
    return lax.ppermute(value, axis, pairs)


def compress_kernel(chunks, *refs):
    (order_hbm, rows_hbm, weight_hbm, gain_hbm, query_hbm, latent_ref, half_ref, index_ref, pick_ref) = refs[:9]
    (order_ref, rows_ref, weight_ref, gain_ref, query_ref, wide, packed, sems) = refs[9:]
    tokens, groups, width = rows_ref.shape
    chunk = tokens // chunks
    copies = [pltpu.make_async_copy(order_hbm, order_ref, sems.at[0])]
    for i in range(chunks):
        at = pl.ds(i * chunk, chunk)
        copies.append(pltpu.make_async_copy(rows_hbm.at[0, at], rows_ref.at[at], sems.at[1 + i]))
    for group in range(groups):
        at = pl.ds(group * width, width)
        copies.append(
            pltpu.make_async_copy(weight_hbm.at[at], weight_ref.at[at], sems.at[1 + chunks + group])
        )
    copies.append(pltpu.make_async_copy(gain_hbm, gain_ref, sems.at[1 + chunks + groups]))
    copies.append(pltpu.make_async_copy(query_hbm.at[0], query_ref, sems.at[2 + chunks + groups]))
    for copy in copies:
        copy.start()

    copies[0].wait()
    count = order_ref.shape[0]
    here = lax.axis_index("rep")
    index, wanted, wanted_beside = 0, 0, 0
    for i in range(count):
        wanted = jnp.where(order_ref[i] == here, i, wanted)
        wanted_beside = jnp.where(order_ref[i] == (here ^ 1), i, wanted_beside)
        smaller = 0
        for j in range(i + 1, count):
            smaller = smaller + (order_ref[j] < order_ref[i]).astype(jnp.int32)
        index = index + smaller * math.factorial(count - 1 - i)
    index_ref[0] = index
    pick_ref[0] = (wanted_beside == (here ^ 2)).astype(jnp.int32)
    pick_ref[1] = jnp.where(wanted == here, 0, jnp.where(wanted == (here ^ 2), 1, 2))

    lanes = wide.shape[2]
    for i in range(chunks):
        copies[1 + i].wait()
        at = slice(i * chunk * groups, (i + 1) * chunk * groups)
        for part in range(wide.shape[0]):
            values = rows_ref[i * chunk : (i + 1) * chunk, :, part * lanes : (part + 1) * lanes]
            wide[part, at] = values.astype(F32).reshape(chunk * groups, lanes)
        for group in range(groups):
            for part in range(wide.shape[0]):
                start = group * width + part * lanes
                picked = wide[part, pl.ds(at.start + group, chunk, stride=groups), :]
                packed[i * chunk : (i + 1) * chunk, start : start + lanes] = picked.astype(BF16)
    for group in range(groups):
        copies[1 + chunks + group].wait()
    copies[1 + chunks + groups].wait()
    gain = gain_ref[...].astype(F32)[None]
    projected = dot(packed[...], weight_ref[...])
    scale = lax.rsqrt(jnp.mean(projected * projected, axis=-1, keepdims=True) + 1e-06)
    latent_ref[...] = (projected * scale * gain).astype(BF16)

    copies[2 + chunks + groups].wait()
    new_count, heads, head_size = query_ref.shape
    query = query_ref[...].astype(F32)
    upper = lax.axis_index("seq") == 1
    query = jnp.where(upper, query[:, heads // 2 :], query[:, : heads // 2])
    half_ref[...] = query.reshape(half_ref.shape).astype(BF16)


def score_kernel(parts, *refs):
    latent_refs, (lift_ref, query_ref), (score_ref, value_ref, top_ref) = (
        refs[:parts],
        refs[parts : parts + 2],
        refs[parts + 2 :],
    )
    head_size = query_ref.shape[-1]
    lift = lift_ref[lax.axis_index("seq")]
    query = query_ref[...]
    top = None
    for part, latent_ref in enumerate(latent_refs):
        tokens = latent_ref.shape[0]
        at = slice(part * tokens, (part + 1) * tokens)
        lifted = dot(latent_ref[...], lift).astype(BF16)
        score = lax.dot_general(
            lifted[:, :head_size], query, (((1,), (1,)), ((), ())), preferred_element_type=F32
        )
        score_ref[at] = score
        value_ref[at] = lifted[:, head_size:]
        part_top = jnp.max(score, axis=0, keepdims=True)
        top = part_top if top is None else jnp.maximum(top, part_top)
    top_ref[...] = jnp.broadcast_to(top, top_ref.shape)


def fetch_kernel(weight_ref, own_ref, sent_ref, kept_ref, sems):
    core = lax.axis_index("tensor") % 2
    depth, columns = sent_ref.shape
    rows = depth // COPIES
    group = lax.axis_index("seq")
    copies = []
    for part, (held_ref, half, first) in enumerate(
        ((own_ref, group, 0), (sent_ref, 1 - group, 1 - core), (kept_ref, 1 - group, core))
    ):
        first = pl.multiple_of(first * columns, columns)
        for i in range(COPIES):
            start = pl.multiple_of(half * depth + i * rows, rows)
            source = weight_ref.at[pl.ds(start, rows), pl.ds(first, held_ref.shape[1])]
            target = held_ref.at[pl.ds(i * rows, rows)]
            copies.append(pltpu.make_async_copy(source, target, sems.at[part, i]))
    for copy in copies:
        copy.start()
    for copy in copies:
        copy.wait()


def fetch(weight):
    depth, columns = weight.shape[0] // 2, weight.shape[1]
    return call(
        fetch_kernel,
        "fetch",
        [pltpu.VMEM((depth, width), weight.dtype) for width in (columns, columns // 2, columns // 2)],
        [weight],
        4,
        scratch=[pltpu.SemaphoreType.DMA((3, COPIES))],
        hbm_in=1,
        cost=cost(0, 0),
    )


def choose(pick, refs, out_ref):
    for i, ref in enumerate(refs):

        @pl.when(pick == i)
        def _():
            out_ref[...] = ref[...]


def pass_kernel(pick_ref, own_ref, second_ref, out_ref):
    choose(pick_ref[0], (own_ref, second_ref), out_ref)


def halve_kernel(near_ref, far_ref, upper_ref, lower_ref):
    half = upper_ref.shape[0]
    upper_ref[...] = near_ref[:half]
    lower_ref[...] = far_ref[half:]


def choose_and_score_kernel(parts, pick_ref, *refs):
    *refs, score_ref, value_ref, top_ref, query_ref = refs
    choose(pick_ref[1], refs[parts + 1 :], query_ref)
    score_kernel(parts, *refs[: parts + 1], query_ref, score_ref, value_ref, top_ref)


def score_call(name, latents, lift, query, pick=None):
    queries = [query] if pick is None else query
    tokens = sum(latent.shape[0] for latent in latents)
    rows, head_size = queries[0].shape
    outs = [shape((tokens, rows), F32), shape((tokens, head_size), BF16), shape((8, rows), F32)]
    operands = [*latents, lift, *queries]
    estimate = cost(0, 0)
    if pick is None:
        body = lambda *refs: score_kernel(len(latents), *refs)
        return call(body, name, outs, operands, 16, cost=estimate)
    body = lambda *refs: choose_and_score_kernel(len(latents), *refs)
    outs.append(shape((rows, head_size), BF16))
    return call(body, name, outs, [pick, *operands], 16, smem_in=1, cost=estimate)


def attend_kernel(block, *refs):
    (*score_refs, out_ref, turned) = refs
    new_count = out_ref.shape[0]
    triples = [score_refs[i : i + 3] for i in range(0, len(score_refs), 3)]
    head_size = triples[0][1].shape[-1]
    coef = head_size ** (-0.5) * math.log2(math.e)
    top = triples[0][2][:1]
    for triple in triples[1:]:
        top = jnp.maximum(top, triple[2][:1])
    total = jnp.zeros_like(top)
    summed = jnp.zeros((head_size, top.shape[1]), F32)
    for score_ref, value_ref, _ in triples:
        for start in range(0, score_ref.shape[0], block):
            at = slice(start, start + block)
            expo = jnp.exp2((score_ref[at] - top) * coef)
            total += jnp.sum(expo, axis=0, keepdims=True)
            summed += lax.dot_general(
                value_ref[at], expo.astype(BF16), (((0,), (0,)), ((), ())), preferred_element_type=F32
            )
    rows = top.shape[1]
    turned[:rows] = (summed / total).T
    heads = rows // new_count
    for head in range(heads):
        out_ref[:, head * head_size : (head + 1) * head_size] = turned[
            pl.ds(head, new_count, stride=heads), :
        ].astype(BF16)


def project_kernel(tile, rows_ref, weight_ref, out_ref):
    rows = rows_ref[...]
    width = out_ref.shape[2]
    for part in range(out_ref.shape[0]):
        for column in range(0, width, tile):
            at = part * width + column
            out_ref[part, :, column : column + tile] = dot(
                rows, weight_ref[:, at : at + tile]
            )


def project_more_kernel(tile, own, kept, rows_ref, weight_ref, before_ref, out_ref):
    here = lax.axis_index("tensor")
    core, chip = here % 2, here // 2
    half = core if own else 1 - core
    width = out_ref.shape[1]
    start = (chip if kept else 1 - chip) * width
    rows = rows_ref[...]
    for column in range(0, width, tile):
        at = pl.ds(pl.multiple_of(start + column, tile), tile)
        out_ref[:, column : column + tile] = before_ref[half, :, at] + dot(rows, weight_ref[:, at])


def add_kernel(one_ref, other_ref, out_ref):
    out_ref[...] = one_ref[...] + other_ref[...]


def sum_kernel(own_ref, beside_ref, across_ref, out_ref):
    out_ref[...] = (own_ref[...] + beside_ref[...] + across_ref[...]).astype(out_ref.dtype)


def join_kernel(places, *refs):
    pieces = refs[: len(places)]
    out_ref, sems = refs[-2:]
    here = lax.axis_index("tensor")
    core, chip = here % 2, here // 2
    width = pieces[0].shape[1]
    copies = []
    for i, place in enumerate(places):
        at = 2 * (1 - core if place // 2 else core) + (1 - chip if place % 2 else chip)
        at = pl.ds(pl.multiple_of(at * width, width), width)
        copies.append(pltpu.make_async_copy(pieces[i], out_ref.at[0, :, at], sems.at[i]))
    for copy in copies:
        copy.start()
    for copy in copies:
        copy.wait()


def join(places, pieces, before):
    new_count, width = pieces[0].shape
    return pl.pallas_call(
        lambda *refs: join_kernel(places, *refs),
        out_shape=shape((1, new_count, 4 * width), BF16),
        in_specs=[IN_VMEM] * len(places) + ([] if before is None else [IN_HBM]),
        out_specs=IN_HBM,
        scratch_shapes=[pltpu.SemaphoreType.DMA((len(places),))],
        input_output_aliases={} if before is None else {len(places): 0},
        compiler_params=pltpu.CompilerParams(vmem_limit_bytes=4 * MIB),
        name="join",
    )(*pieces, *([] if before is None else [before]))


def square_shards(key_value_rows, queries, w_comp, latent_gain, w_up, w_out, replica_order):
    orders = list(itertools.permutations(range(lax.axis_size("rep"))))
    _, new_count, heads, head_size = queries.shape
    _, tokens, all_groups, width = key_value_rows.shape
    latent_width = w_comp.shape[1]
    rows = heads // 2 * new_count

    chunks = 3 if tokens % 48 == 0 else 1
    latent, query, index, pick = call(
        lambda *refs: compress_kernel(chunks, *refs),
        "compress",
        [shape((tokens, latent_width), BF16), shape((rows, head_size), BF16), *[shape((n,), jnp.int32) for n in (1, 2)]],
        [replica_order, key_value_rows, w_comp, latent_gain, queries],
        16,
        scratch=[
            pltpu.SMEM(replica_order.shape, jnp.int32),
            pltpu.VMEM(key_value_rows.shape[1:], BF16),
            pltpu.VMEM(w_comp.shape, BF16),
            pltpu.VMEM(latent_gain.shape, BF16),
            pltpu.VMEM(queries.shape[1:], BF16),
            pltpu.VMEM((width // 128, (tokens + 1) * all_groups, 128), F32),
            pltpu.VMEM((tokens, all_groups * width), BF16),
            pltpu.SemaphoreType.DMA((3 + chunks + all_groups,)),
        ],
        hbm_in=5,
        smem_out=2,
        cost=cost(0, 0),
    )

    near = swap(latent, "seq", 1)
    far = swap(latent, "tensor", 2)
    second_query = swap(query, "rep", 2)
    held, held_sent, held_kept = fetch(w_out)
    second_query, held = lax.optimization_barrier((second_query, held))
    (passed,) = call(
        pass_kernel,
        "pass",
        [shape(query.shape, query.dtype)],
        [pick, query, second_query],
        4,
        smem_in=1,
        cost=cost(0, 0),
    )
    near, far, _ = lax.optimization_barrier((near, far, passed))
    upper, lower = call(
        halve_kernel,
        "halve",
        [shape((tokens // 2, latent_width), BF16)] * 2,
        [near, far],
        4,
        cost=cost(0, 0),
    )
    corner = [swap(upper, "tensor", 2), swap(lower, "seq", 1)]
    passed = swap(passed, "rep", 1)
    given, near, far, _ = lax.optimization_barrier((latent, near, far, upper))
    besides = [swap(piece, "tensor", 1) for piece in (given, near, far)]
    choices = [query, second_query, passed]
    *first, query = score_call("score_here", [given, near, far], w_up, choices, pick)
    corner, first[2] = lax.optimization_barrier((corner, first[2]))
    corner += [swap(piece, "tensor", 1) for piece in corner]
    second = list(score_call("score_beside", besides, w_up, query))
    corner[2], second[2] = lax.optimization_barrier((corner[2], second[2]))
    third = score_call("score_corner", corner, w_up, query)
    depth = rows // new_count * head_size
    (attended,) = call(
        lambda *refs: attend_kernel(tokens, *refs),
        "attend",
        [shape((new_count, depth), BF16)],
        [*first, *second, *third],
        16,
        scratch=[pltpu.VMEM((rows + rows // new_count, head_size), F32)],
        cost=cost(0, 0),
    )
    attended_other = swap(attended, "seq", 1)
    columns = w_out.shape[1]
    tile = min(512, columns // 2)
    (partial,) = call(
        lambda *refs: project_kernel(tile, *refs),
        "project",
        [shape((2, new_count, columns // 2), F32)],
        [attended, held],
        12,
        cost=cost(0, 0),
    )

    quarter = (new_count, columns // 4)

    def project_more(other, own, kept):
        return call(
            lambda *refs: project_more_kernel(tile, own, kept, *refs),
            "project_own" if own else "project_sent",
            [shape(quarter, F32)],
            [other, held_kept if own else held_sent, partial],
            12,
            cost=cost(0, 0),
        )[0]

    given = swap(project_more(attended_other, False, False), "tensor", 1)
    operands = [project_more(attended_other, True, False), given]
    operands[0], other = lax.optimization_barrier((operands[0], attended_other))
    kept = project_more(other, False, True)
    (given,) = call(add_kernel, "add", [shape(quarter, F32)], operands, 8, cost=cost(0, 0))
    other, given, kept = lax.optimization_barrier((attended_other, given, kept))
    given = swap(given, "tensor", 2)
    kept = swap(kept, "tensor", 1)
    operands = [project_more(other, True, True), kept, given]
    (own,) = call(sum_kernel, "sum", [shape(quarter, BF16)], operands, 8, cost=cost(0, 0))

    def reply(order):
        pairs = [(p * 4 + t, r * 4 + t) for r, p in enumerate(order) for t in range(4)]
        crossed = [(source, target ^ 2) for source, target in pairs]
        axes = ("rep", "tensor")

        def run(value):
            if max(abs(p - r) for r, p in enumerate(order)) > 2:
                own = lax.ppermute(value, axes, pairs)
                return own, swap(own, "tensor", 2)
            across = lax.ppermute(value, axes, crossed)
            if order == tuple(range(len(order))):
                return value, across
            return lax.ppermute(value, axes, pairs), across

        return run

    own, across = lax.switch(index[0], [reply(order) for order in orders], own)
    beside, last = swap(own, "tensor", 1), swap(across, "tensor", 1)
    joined = join((0, 1), [own, across], None)
    return join((2, 3), [beside, last], joined)


def shards(key_value_rows, queries, w_comp, latent_gain, w_up, w_out, replica_order):
    orders = list(itertools.permutations(range(lax.axis_size("rep"))))
    index = order_index(replica_order, orders)
    query = route(queries[0], index, orders, False)
    rows = key_value_rows[0]
    latent = compress(rows.reshape(rows.shape[0], -1), w_comp, latent_gain)
    latent = lax.all_gather(latent, "tensor", axis=0, tiled=True)
    groups = w_up.shape[0]
    lifted = jnp.einsum("tf,gfy->tgy", latent, w_up, preferred_element_type=F32).astype(BF16)
    head_size = query.shape[-1]
    new_count = query.shape[0]
    keys = lifted[..., :head_size]
    values = lifted[..., head_size:]
    grouped_heads = query.reshape(new_count, groups, -1, head_size)
    scores = jnp.einsum(
        "nghd,tgd->nght", grouped_heads, keys, preferred_element_type=F32
    ) * head_size ** (-0.5)
    top = lax.pmax(jnp.max(scores, axis=-1), "seq")
    expo = jnp.exp(scores - top[..., None])
    total = jnp.sum(expo, axis=-1)
    summed = jnp.einsum("nght,tgd->nghd", expo.astype(BF16), values, preferred_element_type=F32)
    summed, total = lax.psum((summed, total), "seq")
    attended = (summed / total[..., None]).astype(BF16).reshape(new_count, -1)
    attended = route(attended, index, orders, True)
    return lax.psum(dot(attended, w_out), "tensor").astype(BF16)[None]


def solution(mesh):
    placed = (
        P("rep", ("seq", "tensor"), None, None),
        P("rep", None, "tensor", None),
        P(),
        P(),
        P("tensor", None, None),
        P("tensor", "seq"),
        P(),
    )
    square = all(mesh.shape[axis] == size for axis, size in (("seq", 2), ("rep", 4), ("tensor", 4)))
    return jax.shard_map(
        square_shards if square else shards,
        mesh=mesh,
        in_specs=placed,
        out_specs=P("rep", None, "seq"),
        check_vma=False,
    )
```

```python
import itertools
import math

import jax
import jax.numpy as jnp
from jax import lax
from jax.experimental import pallas as pl
from jax.experimental.pallas import tpu as pltpu
from jax.sharding import PartitionSpec as P

BF16, F32 = jnp.bfloat16, jnp.float32
MIB = 1024 * 1024
IN_VMEM = pl.BlockSpec(memory_space=pltpu.VMEM)
IN_SMEM = pl.BlockSpec(memory_space=pltpu.SMEM)
IN_HBM = pl.BlockSpec(memory_space=pltpu.HBM)
COPIES = 8


def shape(dims, dtype):
    return jax.ShapeDtypeStruct(dims, dtype)


def call(body, name, outs, operands, vmem, scratch=(), smem_in=0, smem_out=0, hbm_in=0, cost=None):
    kept = len(operands) - hbm_in
    specs = [IN_SMEM] * smem_in + [IN_VMEM] * (kept - smem_in) + [IN_HBM] * hbm_in
    operands = [
        *operands[:kept],
        *(pltpu.with_memory_space_constraint(operand, pltpu.HBM) for operand in operands[kept:]),
    ]
    out_specs = [IN_VMEM] * (len(outs) - smem_out) + [IN_SMEM] * smem_out
    return pl.pallas_call(
        body,
        out_shape=outs,
        in_specs=specs,
        out_specs=out_specs,
        scratch_shapes=list(scratch),
        compiler_params=pltpu.CompilerParams(vmem_limit_bytes=vmem * MIB),
        cost_estimate=cost,
        name=name,
    )(*operands)


def cost(flops, moved, exps=0):
    return pl.CostEstimate(flops=int(flops), bytes_accessed=int(moved), transcendentals=int(exps))


def dot(a, b):
    return jnp.dot(a, b, preferred_element_type=F32)


def compress(rows, weight, gain):
    projected = dot(rows, weight)
    scale = lax.rsqrt(jnp.mean(projected * projected, axis=-1, keepdims=True) + 1e-06)
    return (projected * scale * gain.astype(F32)[None]).astype(BF16)


def order_index(replica_order, orders):
    table = jnp.array(orders, jnp.int32)
    match = jnp.all(table == replica_order[None], axis=1)
    return jnp.sum(jnp.where(match, lax.iota(jnp.int32, len(orders)), 0))


def route_pairs(order, back):
    return [(p, r) if back else (r, p) for r, p in enumerate(order)]


def route(value, index, orders, back):
    def branch(order):
        return lambda v: lax.ppermute(v, "rep", route_pairs(order, back))

    return lax.switch(index, [branch(o) for o in orders], value)


def shift(value, axis, hops):
    size = lax.axis_size(axis)
    return lax.ppermute(value, axis, [(i, (i + hops) % size) for i in range(size)])


def swap(value, axis, bit):
    pairs = [(i, i ^ bit) for i in range(lax.axis_size(axis))]
    return lax.ppermute(value, axis, pairs)


def compress_kernel(chunks, *refs):
    (order_hbm, rows_hbm, weight_hbm, gain_hbm, query_hbm, latent_ref, half_ref, index_ref, pick_ref) = refs[:9]
    (order_ref, rows_ref, weight_ref, gain_ref, query_ref, wide, packed, sems) = refs[9:]
    tokens, groups, width = rows_ref.shape
    chunk = tokens // chunks
    copies = [pltpu.make_async_copy(order_hbm, order_ref, sems.at[0])]
    for i in range(chunks):
        at = pl.ds(i * chunk, chunk)
        copies.append(pltpu.make_async_copy(rows_hbm.at[0, at], rows_ref.at[at], sems.at[1 + i]))
    for group in range(groups):
        at = pl.ds(group * width, width)
        copies.append(
            pltpu.make_async_copy(weight_hbm.at[at], weight_ref.at[at], sems.at[1 + chunks + group])
        )
    copies.append(pltpu.make_async_copy(gain_hbm, gain_ref, sems.at[1 + chunks + groups]))
    copies.append(pltpu.make_async_copy(query_hbm.at[0], query_ref, sems.at[2 + chunks + groups]))
    for copy in copies:
        copy.start()

    copies[0].wait()
    count = order_ref.shape[0]
    here = lax.axis_index("rep")
    index, wanted, wanted_beside = 0, 0, 0
    for i in range(count):
        wanted = jnp.where(order_ref[i] == here, i, wanted)
        wanted_beside = jnp.where(order_ref[i] == (here ^ 1), i, wanted_beside)
        smaller = 0
        for j in range(i + 1, count):
            smaller = smaller + (order_ref[j] < order_ref[i]).astype(jnp.int32)
        index = index + smaller * math.factorial(count - 1 - i)
    index_ref[0] = index
    pick_ref[0] = (wanted_beside == (here ^ 2)).astype(jnp.int32)
    pick_ref[1] = jnp.where(wanted == here, 0, jnp.where(wanted == (here ^ 2), 1, 2))

    lanes = wide.shape[2]
    for i in range(chunks):
        copies[1 + i].wait()
        at = slice(i * chunk * groups, (i + 1) * chunk * groups)
        for part in range(wide.shape[0]):
            values = rows_ref[i * chunk : (i + 1) * chunk, :, part * lanes : (part + 1) * lanes]
            wide[part, at] = values.astype(F32).reshape(chunk * groups, lanes)
        for group in range(groups):
            for part in range(wide.shape[0]):
                start = group * width + part * lanes
                picked = wide[part, pl.ds(at.start + group, chunk, stride=groups), :]
                packed[i * chunk : (i + 1) * chunk, start : start + lanes] = picked.astype(BF16)
    copies[2 + chunks + groups].wait()
    new_count, heads, head_size = query_ref.shape
    query = query_ref[...].astype(F32)
    upper = lax.axis_index("seq") == 1
    query = jnp.where(upper, query[:, heads // 2 :], query[:, : heads // 2])
    half_ref[...] = query.reshape(half_ref.shape).astype(BF16)

    for group in range(groups):
        copies[1 + chunks + group].wait()
    copies[1 + chunks + groups].wait()
    gain = gain_ref[...].astype(F32)[None]
    projected = dot(packed[...], weight_ref[...])
    scale = lax.rsqrt(jnp.mean(projected * projected, axis=-1, keepdims=True) + 1e-06)
    latent_ref[...] = (projected * scale * gain).astype(BF16)


def score_kernel(parts, *refs):
    latent_refs, (lift_ref, query_ref), (score_ref, value_ref, top_ref) = (
        refs[:parts],
        refs[parts : parts + 2],
        refs[parts + 2 :],
    )
    head_size = query_ref.shape[-1]
    lift = lift_ref[lax.axis_index("seq")]
    query = query_ref[...]
    top = None
    for part, latent_ref in enumerate(latent_refs):
        tokens = latent_ref.shape[0]
        at = slice(part * tokens, (part + 1) * tokens)
        lifted = dot(latent_ref[...], lift).astype(BF16)
        score = lax.dot_general(
            lifted[:, :head_size], query, (((1,), (1,)), ((), ())), preferred_element_type=F32
        )
        score_ref[at] = score
        value_ref[at] = lifted[:, head_size:]
        part_top = jnp.max(score, axis=0, keepdims=True)
        top = part_top if top is None else jnp.maximum(top, part_top)
    top_ref[...] = jnp.broadcast_to(top, top_ref.shape)


def fetch_kernel(weight_ref, own_ref, sent_ref, kept_ref, sems):
    core = lax.axis_index("tensor") % 2
    depth, columns = sent_ref.shape
    rows = depth // COPIES
    group = lax.axis_index("seq")
    copies = []
    for part, (held_ref, half, first) in enumerate(
        ((own_ref, group, 0), (sent_ref, 1 - group, 1 - core), (kept_ref, 1 - group, core))
    ):
        first = pl.multiple_of(first * columns, columns)
        for i in range(COPIES):
            start = pl.multiple_of(half * depth + i * rows, rows)
            source = weight_ref.at[pl.ds(start, rows), pl.ds(first, held_ref.shape[1])]
            target = held_ref.at[pl.ds(i * rows, rows)]
            copies.append(pltpu.make_async_copy(source, target, sems.at[part, i]))
    for copy in copies:
        copy.start()
    for copy in copies:
        copy.wait()


def fetch(weight):
    depth, columns = weight.shape[0] // 2, weight.shape[1]
    return call(
        fetch_kernel,
        "fetch",
        [pltpu.VMEM((depth, width), weight.dtype) for width in (columns, columns // 2, columns // 2)],
        [weight],
        4,
        scratch=[pltpu.SemaphoreType.DMA((3, COPIES))],
        hbm_in=1,
        cost=cost(0, 0),
    )


def choose(pick, refs, out_ref):
    for i, ref in enumerate(refs):

        @pl.when(pick == i)
        def _():
            out_ref[...] = ref[...]


def pass_kernel(pick_ref, own_ref, second_ref, out_ref):
    choose(pick_ref[0], (own_ref, second_ref), out_ref)


def halve_kernel(near_ref, far_ref, upper_ref, lower_ref):
    half = upper_ref.shape[0]
    upper_ref[...] = near_ref[:half]
    lower_ref[...] = far_ref[half:]


def choose_and_score_kernel(parts, pick_ref, *refs):
    *refs, score_ref, value_ref, top_ref, query_ref = refs
    choose(pick_ref[1], refs[parts + 1 :], query_ref)
    score_kernel(parts, *refs[: parts + 1], query_ref, score_ref, value_ref, top_ref)


def score_call(name, latents, lift, query, pick=None):
    queries = [query] if pick is None else query
    tokens = sum(latent.shape[0] for latent in latents)
    rows, head_size = queries[0].shape
    outs = [shape((tokens, rows), F32), shape((tokens, head_size), BF16), shape((8, rows), F32)]
    operands = [*latents, lift, *queries]
    estimate = cost(0, 0)
    if pick is None:
        body = lambda *refs: score_kernel(len(latents), *refs)
        return call(body, name, outs, operands, 16, cost=estimate)
    body = lambda *refs: choose_and_score_kernel(len(latents), *refs)
    outs.append(shape((rows, head_size), BF16))
    return call(body, name, outs, [pick, *operands], 16, smem_in=1, cost=estimate)


def attend_kernel(block, *refs):
    (*score_refs, out_ref, turned) = refs
    new_count = out_ref.shape[0]
    triples = [score_refs[i : i + 3] for i in range(0, len(score_refs), 3)]
    head_size = triples[0][1].shape[-1]
    coef = head_size ** (-0.5) * math.log2(math.e)
    top = triples[0][2][:1]
    for triple in triples[1:]:
        top = jnp.maximum(top, triple[2][:1])
    total = jnp.zeros_like(top)
    summed = jnp.zeros((head_size, top.shape[1]), F32)
    for score_ref, value_ref, _ in triples:
        for start in range(0, score_ref.shape[0], block):
            at = slice(start, start + block)
            expo = jnp.exp2((score_ref[at] - top) * coef)
            total += jnp.sum(expo, axis=0, keepdims=True)
            summed += lax.dot_general(
                value_ref[at], expo.astype(BF16), (((0,), (0,)), ((), ())), preferred_element_type=F32
            )
    rows = top.shape[1]
    turned[:rows] = (summed / total).T
    heads = rows // new_count
    for head in range(heads):
        out_ref[:, head * head_size : (head + 1) * head_size] = turned[
            pl.ds(head, new_count, stride=heads), :
        ].astype(BF16)


def project_kernel(tile, rows_ref, weight_ref, out_ref):
    rows = rows_ref[...]
    width = out_ref.shape[2]
    for part in range(out_ref.shape[0]):
        for column in range(0, width, tile):
            at = part * width + column
            out_ref[part, :, column : column + tile] = dot(
                rows, weight_ref[:, at : at + tile]
            )


def project_more_kernel(tile, own, kept, rows_ref, weight_ref, before_ref, out_ref):
    here = lax.axis_index("tensor")
    core, chip = here % 2, here // 2
    half = core if own else 1 - core
    width = out_ref.shape[1]
    start = (chip if kept else 1 - chip) * width
    rows = rows_ref[...]
    for column in range(0, width, tile):
        at = pl.ds(pl.multiple_of(start + column, tile), tile)
        out_ref[:, column : column + tile] = before_ref[half, :, at] + dot(rows, weight_ref[:, at])


def add_kernel(one_ref, other_ref, out_ref):
    out_ref[...] = one_ref[...] + other_ref[...]


def sum_kernel(own_ref, beside_ref, across_ref, out_ref):
    out_ref[...] = (own_ref[...] + beside_ref[...] + across_ref[...]).astype(out_ref.dtype)


def join_kernel(places, *refs):
    pieces = refs[: len(places)]
    out_ref, sems = refs[-2:]
    here = lax.axis_index("tensor")
    core, chip = here % 2, here // 2
    width = pieces[0].shape[1]
    copies = []
    for i, place in enumerate(places):
        at = 2 * (1 - core if place // 2 else core) + (1 - chip if place % 2 else chip)
        at = pl.ds(pl.multiple_of(at * width, width), width)
        copies.append(pltpu.make_async_copy(pieces[i], out_ref.at[0, :, at], sems.at[i]))
    for copy in copies:
        copy.start()
    for copy in copies:
        copy.wait()


def blank(dims):
    return pl.pallas_call(
        lambda out_ref: None, out_shape=shape(dims, BF16), out_specs=IN_HBM, name="blank"
    )()


def join(places, pieces, before):
    new_count, width = pieces[0].shape
    return pl.pallas_call(
        lambda *refs: join_kernel(places, *refs),
        out_shape=shape((1, new_count, 4 * width), BF16),
        in_specs=[IN_VMEM] * len(places) + [IN_HBM],
        out_specs=IN_HBM,
        scratch_shapes=[pltpu.SemaphoreType.DMA((len(places),))],
        input_output_aliases={len(places): 0},
        compiler_params=pltpu.CompilerParams(vmem_limit_bytes=4 * MIB),
        name="join",
    )(*pieces, before)


def square_shards(key_value_rows, queries, w_comp, latent_gain, w_up, w_out, replica_order):
    orders = list(itertools.permutations(range(lax.axis_size("rep"))))
    _, new_count, heads, head_size = queries.shape
    _, tokens, all_groups, width = key_value_rows.shape
    latent_width = w_comp.shape[1]
    rows = heads // 2 * new_count

    chunks = 6 if tokens % 96 == 0 else 1
    latent, query, index, pick = call(
        lambda *refs: compress_kernel(chunks, *refs),
        "compress",
        [shape((tokens, latent_width), BF16), shape((rows, head_size), BF16), *[shape((n,), jnp.int32) for n in (1, 2)]],
        [replica_order, key_value_rows, w_comp, latent_gain, queries],
        16,
        scratch=[
            pltpu.SMEM(replica_order.shape, jnp.int32),
            pltpu.VMEM(key_value_rows.shape[1:], BF16),
            pltpu.VMEM(w_comp.shape, BF16),
            pltpu.VMEM(latent_gain.shape, BF16),
            pltpu.VMEM(queries.shape[1:], BF16),
            pltpu.VMEM((width // 128, (tokens + 1) * all_groups, 128), F32),
            pltpu.VMEM((tokens, all_groups * width), BF16),
            pltpu.SemaphoreType.DMA((3 + chunks + all_groups,)),
        ],
        hbm_in=5,
        smem_out=2,
        cost=cost(0, 0),
    )

    near = swap(latent, "seq", 1)
    far = swap(latent, "tensor", 2)
    second_query = swap(query, "rep", 2)
    held, held_sent, held_kept = fetch(w_out)
    second_query, held = lax.optimization_barrier((second_query, held))
    (passed,) = call(
        pass_kernel,
        "pass",
        [shape(query.shape, query.dtype)],
        [pick, query, second_query],
        4,
        smem_in=1,
        cost=cost(0, 0),
    )
    near, far, _ = lax.optimization_barrier((near, far, passed))
    upper, lower = call(
        halve_kernel,
        "halve",
        [shape((tokens // 2, latent_width), BF16)] * 2,
        [near, far],
        4,
        cost=cost(0, 0),
    )
    corner = [swap(upper, "tensor", 2), swap(lower, "seq", 1)]
    passed = swap(passed, "rep", 1)
    given, near, far, _ = lax.optimization_barrier((latent, near, far, upper))
    besides = [swap(piece, "tensor", 1) for piece in (given, near, far)]
    choices = [query, second_query, passed]
    *first, query = score_call("score_here", [given, near, far], w_up, choices, pick)
    corner, first[2] = lax.optimization_barrier((corner, first[2]))
    corner += [swap(piece, "tensor", 1) for piece in corner]
    second = list(score_call("score_beside", besides, w_up, query))
    corner[2], second[2] = lax.optimization_barrier((corner[2], second[2]))
    third = score_call("score_corner", corner, w_up, query)
    depth = rows // new_count * head_size
    (attended,) = call(
        lambda *refs: attend_kernel(tokens, *refs),
        "attend",
        [shape((new_count, depth), BF16)],
        [*first, *second, *third],
        16,
        scratch=[pltpu.VMEM((rows + rows // new_count, head_size), F32)],
        cost=cost(0, 0),
    )
    attended_other = swap(attended, "seq", 1)
    columns = w_out.shape[1]
    tile = min(512, columns // 2)
    (partial,) = call(
        lambda *refs: project_kernel(tile, *refs),
        "project",
        [shape((2, new_count, columns // 2), F32)],
        [attended, held],
        12,
        cost=cost(0, 0),
    )

    quarter = (new_count, columns // 4)

    def project_more(other, own, kept):
        return call(
            lambda *refs: project_more_kernel(tile, own, kept, *refs),
            "project_own" if own else "project_sent",
            [shape(quarter, F32)],
            [other, held_kept if own else held_sent, partial],
            12,
            cost=cost(0, 0),
        )[0]

    given = swap(project_more(attended_other, False, False), "tensor", 1)
    operands = [project_more(attended_other, True, False), given]
    operands[0], other = lax.optimization_barrier((operands[0], attended_other))
    kept = project_more(other, False, True)
    (given,) = call(add_kernel, "add", [shape(quarter, F32)], operands, 8, cost=cost(0, 0))
    other, given, kept = lax.optimization_barrier((attended_other, given, kept))
    given = swap(given, "tensor", 2)
    kept = swap(kept, "tensor", 1)
    other, joined = lax.optimization_barrier((other, blank((1, new_count, columns))))
    operands = [project_more(other, True, True), kept, given]
    (own,) = call(sum_kernel, "sum", [shape(quarter, BF16)], operands, 8, cost=cost(0, 0))

    def reply(order):
        pairs = [(p * 4 + t, r * 4 + t) for r, p in enumerate(order) for t in range(4)]
        crossed = [(source, target ^ 2) for source, target in pairs]
        axes = ("rep", "tensor")

        def run(value):
            if max(abs(p - r) for r, p in enumerate(order)) > 2:
                own = lax.ppermute(value, axes, pairs)
                return own, swap(own, "tensor", 2)
            across = lax.ppermute(value, axes, crossed)
            if order == tuple(range(len(order))):
                return value, across
            return lax.ppermute(value, axes, pairs), across

        return run

    own, across = lax.switch(index[0], [reply(order) for order in orders], own)
    beside, last = swap(own, "tensor", 1), swap(across, "tensor", 1)
    joined = join((0, 1), [own, across], joined)
    return join((2, 3), [beside, last], joined)


def shards(key_value_rows, queries, w_comp, latent_gain, w_up, w_out, replica_order):
    orders = list(itertools.permutations(range(lax.axis_size("rep"))))
    index = order_index(replica_order, orders)
    query = route(queries[0], index, orders, False)
    rows = key_value_rows[0]
    latent = compress(rows.reshape(rows.shape[0], -1), w_comp, latent_gain)
    latent = lax.all_gather(latent, "tensor", axis=0, tiled=True)
    groups = w_up.shape[0]
    lifted = jnp.einsum("tf,gfy->tgy", latent, w_up, preferred_element_type=F32).astype(BF16)
    head_size = query.shape[-1]
    new_count = query.shape[0]
    keys = lifted[..., :head_size]
    values = lifted[..., head_size:]
    grouped_heads = query.reshape(new_count, groups, -1, head_size)
    scores = jnp.einsum(
        "nghd,tgd->nght", grouped_heads, keys, preferred_element_type=F32
    ) * head_size ** (-0.5)
    top = lax.pmax(jnp.max(scores, axis=-1), "seq")
    expo = jnp.exp(scores - top[..., None])
    total = jnp.sum(expo, axis=-1)
    summed = jnp.einsum("nght,tgd->nghd", expo.astype(BF16), values, preferred_element_type=F32)
    summed, total = lax.psum((summed, total), "seq")
    attended = (summed / total[..., None]).astype(BF16).reshape(new_count, -1)
    attended = route(attended, index, orders, True)
    return lax.psum(dot(attended, w_out), "tensor").astype(BF16)[None]


def solution(mesh):
    placed = (
        P("rep", ("seq", "tensor"), None, None),
        P("rep", None, "tensor", None),
        P(),
        P(),
        P("tensor", None, None),
        P("tensor", "seq"),
        P(),
    )
    square = all(mesh.shape[axis] == size for axis, size in (("seq", 2), ("rep", 4), ("tensor", 4)))
    return jax.shard_map(
        square_shards if square else shards,
        mesh=mesh,
        in_specs=placed,
        out_specs=P("rep", None, "seq"),
        check_vma=False,
    )
```

```python
import itertools
import math

import jax
import jax.numpy as jnp
from jax import lax
from jax.experimental import pallas as pl
from jax.experimental.pallas import tpu as pltpu
from jax.sharding import PartitionSpec as P

BF16, F32 = jnp.bfloat16, jnp.float32
MIB = 1024 * 1024
IN_VMEM = pl.BlockSpec(memory_space=pltpu.VMEM)
IN_SMEM = pl.BlockSpec(memory_space=pltpu.SMEM)
IN_HBM = pl.BlockSpec(memory_space=pltpu.HBM)
COPIES = 8


def shape(dims, dtype):
    return jax.ShapeDtypeStruct(dims, dtype)


def call(body, name, outs, operands, vmem, scratch=(), smem_in=0, smem_out=0, hbm_in=0, cost=None):
    kept = len(operands) - hbm_in
    specs = [IN_SMEM] * smem_in + [IN_VMEM] * (kept - smem_in) + [IN_HBM] * hbm_in
    operands = [
        *operands[:kept],
        *(pltpu.with_memory_space_constraint(operand, pltpu.HBM) for operand in operands[kept:]),
    ]
    out_specs = [IN_VMEM] * (len(outs) - smem_out) + [IN_SMEM] * smem_out
    return pl.pallas_call(
        body,
        out_shape=outs,
        in_specs=specs,
        out_specs=out_specs,
        scratch_shapes=list(scratch),
        compiler_params=pltpu.CompilerParams(vmem_limit_bytes=vmem * MIB),
        cost_estimate=cost,
        name=name,
    )(*operands)


def cost(flops, moved, exps=0):
    return pl.CostEstimate(flops=int(flops), bytes_accessed=int(moved), transcendentals=int(exps))


def dot(a, b):
    return jnp.dot(a, b, preferred_element_type=F32)


def compress(rows, weight, gain):
    projected = dot(rows, weight)
    scale = lax.rsqrt(jnp.mean(projected * projected, axis=-1, keepdims=True) + 1e-06)
    return (projected * scale * gain.astype(F32)[None]).astype(BF16)


def order_index(replica_order, orders):
    table = jnp.array(orders, jnp.int32)
    match = jnp.all(table == replica_order[None], axis=1)
    return jnp.sum(jnp.where(match, lax.iota(jnp.int32, len(orders)), 0))


def route_pairs(order, back):
    return [(p, r) if back else (r, p) for r, p in enumerate(order)]


def route(value, index, orders, back):
    def branch(order):
        return lambda v: lax.ppermute(v, "rep", route_pairs(order, back))

    return lax.switch(index, [branch(o) for o in orders], value)


def shift(value, axis, hops):
    size = lax.axis_size(axis)
    return lax.ppermute(value, axis, [(i, (i + hops) % size) for i in range(size)])


def swap(value, axis, bit):
    pairs = [(i, i ^ bit) for i in range(lax.axis_size(axis))]
    return lax.ppermute(value, axis, pairs)


def compress_kernel(chunks, *refs):
    (order_hbm, rows_hbm, weight_hbm, gain_hbm, query_hbm, latent_ref, half_ref, index_ref, pick_ref) = refs[:9]
    (order_ref, rows_ref, weight_ref, gain_ref, query_ref, wide, packed, sems) = refs[9:]
    tokens, groups, width = rows_ref.shape
    chunk = tokens // chunks
    copies = [pltpu.make_async_copy(order_hbm, order_ref, sems.at[0])]
    for i in range(chunks):
        at = pl.ds(i * chunk, chunk)
        copies.append(pltpu.make_async_copy(rows_hbm.at[0, at], rows_ref.at[at], sems.at[1 + i]))
    for group in range(groups):
        at = pl.ds(group * width, width)
        copies.append(
            pltpu.make_async_copy(weight_hbm.at[at], weight_ref.at[at], sems.at[1 + chunks + group])
        )
    copies.append(pltpu.make_async_copy(gain_hbm, gain_ref, sems.at[1 + chunks + groups]))
    copies.append(pltpu.make_async_copy(query_hbm.at[0], query_ref, sems.at[2 + chunks + groups]))
    for copy in copies:
        copy.start()

    copies[0].wait()
    count = order_ref.shape[0]
    here = lax.axis_index("rep")
    index, wanted, wanted_beside = 0, 0, 0
    for i in range(count):
        wanted = jnp.where(order_ref[i] == here, i, wanted)
        wanted_beside = jnp.where(order_ref[i] == (here ^ 1), i, wanted_beside)
        smaller = 0
        for j in range(i + 1, count):
            smaller = smaller + (order_ref[j] < order_ref[i]).astype(jnp.int32)
        index = index + smaller * math.factorial(count - 1 - i)
    index_ref[0] = index
    pick_ref[0] = (wanted_beside == (here ^ 2)).astype(jnp.int32)
    pick_ref[1] = jnp.where(wanted == here, 0, jnp.where(wanted == (here ^ 2), 1, 2))

    lanes = wide.shape[2]
    for i in range(chunks):
        copies[1 + i].wait()
        at = slice(i * chunk * groups, (i + 1) * chunk * groups)
        for part in range(wide.shape[0]):
            values = rows_ref[i * chunk : (i + 1) * chunk, :, part * lanes : (part + 1) * lanes]
            wide[part, at] = values.astype(F32).reshape(chunk * groups, lanes)
        for group in range(groups):
            for part in range(wide.shape[0]):
                start = group * width + part * lanes
                picked = wide[part, pl.ds(at.start + group, chunk, stride=groups), :]
                packed[i * chunk : (i + 1) * chunk, start : start + lanes] = picked.astype(BF16)
    copies[2 + chunks + groups].wait()
    new_count, heads, head_size = query_ref.shape
    query = query_ref[...].astype(F32)
    upper = lax.axis_index("seq") == 1
    query = jnp.where(upper, query[:, heads // 2 :], query[:, : heads // 2])
    half_ref[...] = query.reshape(half_ref.shape).astype(BF16)

    for group in range(groups):
        copies[1 + chunks + group].wait()
    copies[1 + chunks + groups].wait()
    gain = gain_ref[...].astype(F32)[None]
    projected = dot(packed[...], weight_ref[...])
    scale = lax.rsqrt(jnp.mean(projected * projected, axis=-1, keepdims=True) + 1e-06)
    latent_ref[...] = (projected * scale * gain).astype(BF16)


def score_kernel(parts, *refs):
    latent_refs, (lift_ref, query_ref), (score_ref, value_ref, top_ref) = (
        refs[:parts],
        refs[parts : parts + 2],
        refs[parts + 2 :],
    )
    head_size = query_ref.shape[-1]
    lift = lift_ref[lax.axis_index("seq")]
    query = query_ref[...]
    top = None
    for part, latent_ref in enumerate(latent_refs):
        tokens = latent_ref.shape[0]
        at = slice(part * tokens, (part + 1) * tokens)
        lifted = dot(latent_ref[...], lift).astype(BF16)
        score = lax.dot_general(
            lifted[:, :head_size], query, (((1,), (1,)), ((), ())), preferred_element_type=F32
        )
        score_ref[at] = score
        value_ref[at] = lifted[:, head_size:]
        part_top = jnp.max(score, axis=0, keepdims=True)
        top = part_top if top is None else jnp.maximum(top, part_top)
    top_ref[...] = jnp.broadcast_to(top, top_ref.shape)


def fetch_kernel(weight_ref, own_ref, sent_ref, kept_ref, sems):
    core = lax.axis_index("tensor") % 2
    depth, columns = sent_ref.shape
    rows = depth // COPIES
    group = lax.axis_index("seq")
    copies = []
    for part, (held_ref, half, first) in enumerate(
        ((own_ref, group, 0), (sent_ref, 1 - group, 1 - core), (kept_ref, 1 - group, core))
    ):
        first = pl.multiple_of(first * columns, columns)
        for i in range(COPIES):
            start = pl.multiple_of(half * depth + i * rows, rows)
            source = weight_ref.at[pl.ds(start, rows), pl.ds(first, held_ref.shape[1])]
            target = held_ref.at[pl.ds(i * rows, rows)]
            copies.append(pltpu.make_async_copy(source, target, sems.at[part, i]))
    for copy in copies:
        copy.start()
    for copy in copies:
        copy.wait()


def fetch(weight):
    depth, columns = weight.shape[0] // 2, weight.shape[1]
    return call(
        fetch_kernel,
        "fetch",
        [pltpu.VMEM((depth, width), weight.dtype) for width in (columns, columns // 2, columns // 2)],
        [weight],
        4,
        scratch=[pltpu.SemaphoreType.DMA((3, COPIES))],
        hbm_in=1,
        cost=cost(0, 0),
    )


def choose(pick, refs, out_ref):
    for i, ref in enumerate(refs):

        @pl.when(pick == i)
        def _():
            out_ref[...] = ref[...]


def pass_kernel(pick_ref, own_ref, second_ref, out_ref):
    choose(pick_ref[0], (own_ref, second_ref), out_ref)


def halve_kernel(near_ref, far_ref, upper_ref, lower_ref):
    half = upper_ref.shape[0]
    upper_ref[...] = near_ref[:half]
    lower_ref[...] = far_ref[half:]


def choose_and_score_kernel(parts, pick_ref, *refs):
    *refs, score_ref, value_ref, top_ref, query_ref = refs
    choose(pick_ref[1], refs[parts + 1 :], query_ref)
    score_kernel(parts, *refs[: parts + 1], query_ref, score_ref, value_ref, top_ref)


def score_call(name, latents, lift, query, pick=None):
    queries = [query] if pick is None else query
    tokens = sum(latent.shape[0] for latent in latents)
    rows, head_size = queries[0].shape
    outs = [shape((tokens, rows), F32), shape((tokens, head_size), BF16), shape((8, rows), F32)]
    operands = [*latents, lift, *queries]
    estimate = cost(0, 0)
    if pick is None:
        body = lambda *refs: score_kernel(len(latents), *refs)
        return call(body, name, outs, operands, 16, cost=estimate)
    body = lambda *refs: choose_and_score_kernel(len(latents), *refs)
    outs.append(shape((rows, head_size), BF16))
    return call(body, name, outs, [pick, *operands], 16, smem_in=1, cost=estimate)


def attend_kernel(block, *refs):
    (*score_refs, out_ref, turned) = refs
    new_count = out_ref.shape[0]
    triples = [score_refs[i : i + 3] for i in range(0, len(score_refs), 3)]
    head_size = triples[0][1].shape[-1]
    coef = head_size ** (-0.5) * math.log2(math.e)
    top = triples[0][2][:1]
    for triple in triples[1:]:
        top = jnp.maximum(top, triple[2][:1])
    total = jnp.zeros_like(top)
    summed = jnp.zeros((head_size, top.shape[1]), F32)
    for score_ref, value_ref, _ in triples:
        for start in range(0, score_ref.shape[0], block):
            at = slice(start, start + block)
            expo = jnp.exp2((score_ref[at] - top) * coef)
            total += jnp.sum(expo, axis=0, keepdims=True)
            summed += lax.dot_general(
                value_ref[at], expo.astype(BF16), (((0,), (0,)), ((), ())), preferred_element_type=F32
            )
    rows = top.shape[1]
    turned[:rows] = (summed / total).T
    heads = rows // new_count
    for head in range(heads):
        out_ref[:, head * head_size : (head + 1) * head_size] = turned[
            pl.ds(head, new_count, stride=heads), :
        ].astype(BF16)


def project_kernel(tile, rows_ref, weight_ref, out_ref):
    rows = rows_ref[...]
    width = out_ref.shape[2]
    for part in range(out_ref.shape[0]):
        for column in range(0, width, tile):
            at = part * width + column
            out_ref[part, :, column : column + tile] = dot(
                rows, weight_ref[:, at : at + tile]
            )


def project_more_kernel(tile, own, kept, rows_ref, weight_ref, before_ref, out_ref):
    here = lax.axis_index("tensor")
    core, chip = here % 2, here // 2
    half = core if own else 1 - core
    width = out_ref.shape[1]
    start = (chip if kept else 1 - chip) * width
    rows = rows_ref[...]
    for column in range(0, width, tile):
        at = pl.ds(pl.multiple_of(start + column, tile), tile)
        out_ref[:, column : column + tile] = before_ref[half, :, at] + dot(rows, weight_ref[:, at])


def add_kernel(one_ref, other_ref, out_ref):
    out_ref[...] = one_ref[...] + other_ref[...]


def sum_kernel(own_ref, beside_ref, across_ref, out_ref):
    out_ref[...] = (own_ref[...] + beside_ref[...] + across_ref[...]).astype(out_ref.dtype)


def join_kernel(places, *refs):
    pieces = refs[: len(places)]
    out_ref, sems = refs[-2:]
    here = lax.axis_index("tensor")
    core, chip = here % 2, here // 2
    width = pieces[0].shape[1]
    copies = []
    for i, place in enumerate(places):
        at = 2 * (1 - core if place // 2 else core) + (1 - chip if place % 2 else chip)
        at = pl.ds(pl.multiple_of(at * width, width), width)
        copies.append(pltpu.make_async_copy(pieces[i], out_ref.at[0, :, at], sems.at[i]))
    for copy in copies:
        copy.start()
    for copy in copies:
        copy.wait()


def join(places, pieces, before, held=IN_VMEM):
    new_count, width = pieces[0].shape
    if held is IN_HBM:
        pieces = [pltpu.with_memory_space_constraint(piece, pltpu.HBM) for piece in pieces]
    return pl.pallas_call(
        lambda *refs: join_kernel(places, *refs),
        out_shape=shape((1, new_count, 4 * width), BF16),
        in_specs=[held] * len(places) + ([] if before is None else [IN_HBM]),
        out_specs=IN_HBM,
        scratch_shapes=[pltpu.SemaphoreType.DMA((len(places),))],
        input_output_aliases={} if before is None else {len(places): 0},
        compiler_params=pltpu.CompilerParams(vmem_limit_bytes=4 * MIB),
        name="join",
    )(*pieces, *([] if before is None else [before]))


def square_shards(key_value_rows, queries, w_comp, latent_gain, w_up, w_out, replica_order):
    orders = list(itertools.permutations(range(lax.axis_size("rep"))))
    _, new_count, heads, head_size = queries.shape
    _, tokens, all_groups, width = key_value_rows.shape
    latent_width = w_comp.shape[1]
    rows = heads // 2 * new_count

    chunks = 6 if tokens % 96 == 0 else 1
    latent, query, index, pick = call(
        lambda *refs: compress_kernel(chunks, *refs),
        "compress",
        [shape((tokens, latent_width), BF16), shape((rows, head_size), BF16), *[shape((n,), jnp.int32) for n in (1, 2)]],
        [replica_order, key_value_rows, w_comp, latent_gain, queries],
        16,
        scratch=[
            pltpu.SMEM(replica_order.shape, jnp.int32),
            pltpu.VMEM(key_value_rows.shape[1:], BF16),
            pltpu.VMEM(w_comp.shape, BF16),
            pltpu.VMEM(latent_gain.shape, BF16),
            pltpu.VMEM(queries.shape[1:], BF16),
            pltpu.VMEM((width // 128, (tokens + 1) * all_groups, 128), F32),
            pltpu.VMEM((tokens, all_groups * width), BF16),
            pltpu.SemaphoreType.DMA((3 + chunks + all_groups,)),
        ],
        hbm_in=5,
        smem_out=2,
        cost=cost(0, 0),
    )

    near = swap(latent, "seq", 1)
    far = swap(latent, "tensor", 2)
    second_query = swap(query, "rep", 2)
    held, held_sent, held_kept = fetch(w_out)
    second_query, held = lax.optimization_barrier((second_query, held))
    (passed,) = call(
        pass_kernel,
        "pass",
        [shape(query.shape, query.dtype)],
        [pick, query, second_query],
        4,
        smem_in=1,
        cost=cost(0, 0),
    )
    near, far, _ = lax.optimization_barrier((near, far, passed))
    upper, lower = call(
        halve_kernel,
        "halve",
        [shape((tokens // 2, latent_width), BF16)] * 2,
        [near, far],
        4,
        cost=cost(0, 0),
    )
    corner = [swap(upper, "tensor", 2), swap(lower, "seq", 1)]
    passed = swap(passed, "rep", 1)
    given, near, far, _ = lax.optimization_barrier((latent, near, far, upper))
    besides = [swap(piece, "tensor", 1) for piece in (given, near, far)]
    choices = [query, second_query, passed]
    *first, query = score_call("score_here", [given, near, far], w_up, choices, pick)
    corner, first[2] = lax.optimization_barrier((corner, first[2]))
    corner += [swap(piece, "tensor", 1) for piece in corner]
    second = list(score_call("score_beside", besides, w_up, query))
    corner[2], second[2] = lax.optimization_barrier((corner[2], second[2]))
    third = score_call("score_corner", corner, w_up, query)
    depth = rows // new_count * head_size
    (attended,) = call(
        lambda *refs: attend_kernel(tokens, *refs),
        "attend",
        [shape((new_count, depth), BF16)],
        [*first, *second, *third],
        16,
        scratch=[pltpu.VMEM((rows + rows // new_count, head_size), F32)],
        cost=cost(0, 0),
    )
    attended_other = swap(attended, "seq", 1)
    columns = w_out.shape[1]
    tile = min(512, columns // 2)
    (partial,) = call(
        lambda *refs: project_kernel(tile, *refs),
        "project",
        [shape((2, new_count, columns // 2), F32)],
        [attended, held],
        12,
        cost=cost(0, 0),
    )

    quarter = (new_count, columns // 4)

    def project_more(other, own, kept):
        return call(
            lambda *refs: project_more_kernel(tile, own, kept, *refs),
            "project_own" if own else "project_sent",
            [shape(quarter, F32)],
            [other, held_kept if own else held_sent, partial],
            12,
            cost=cost(0, 0),
        )[0]

    given = swap(project_more(attended_other, False, False), "tensor", 1)
    operands = [project_more(attended_other, True, False), given]
    operands[0], other = lax.optimization_barrier((operands[0], attended_other))
    kept = project_more(other, False, True)
    (given,) = call(add_kernel, "add", [shape(quarter, F32)], operands, 8, cost=cost(0, 0))
    other, given, kept = lax.optimization_barrier((attended_other, given, kept))
    given = swap(given, "tensor", 2)
    kept = swap(kept, "tensor", 1)
    operands = [project_more(other, True, True), kept, given]
    (own,) = call(sum_kernel, "sum", [shape(quarter, BF16)], operands, 8, cost=cost(0, 0))

    def reply(order):
        pairs = [(p * 4 + t, r * 4 + t) for r, p in enumerate(order) for t in range(4)]
        crossed = [(source, target ^ 2) for source, target in pairs]
        axes = ("rep", "tensor")

        def run(value):
            if max(abs(p - r) for r, p in enumerate(order)) > 2:
                own = lax.ppermute(value, axes, pairs)
                return own, swap(own, "tensor", 2)
            across = lax.ppermute(value, axes, crossed)
            if order == tuple(range(len(order))):
                return value, across
            return lax.ppermute(value, axes, pairs), across

        return run

    own, across = lax.switch(index[0], [reply(order) for order in orders], own)
    beside, last = swap(own, "tensor", 1), swap(across, "tensor", 1)
    joined = join((0, 1), [own, across], None, IN_HBM)
    return join((2, 3), [beside, last], joined)


def shards(key_value_rows, queries, w_comp, latent_gain, w_up, w_out, replica_order):
    orders = list(itertools.permutations(range(lax.axis_size("rep"))))
    index = order_index(replica_order, orders)
    query = route(queries[0], index, orders, False)
    rows = key_value_rows[0]
    latent = compress(rows.reshape(rows.shape[0], -1), w_comp, latent_gain)
    latent = lax.all_gather(latent, "tensor", axis=0, tiled=True)
    groups = w_up.shape[0]
    lifted = jnp.einsum("tf,gfy->tgy", latent, w_up, preferred_element_type=F32).astype(BF16)
    head_size = query.shape[-1]
    new_count = query.shape[0]
    keys = lifted[..., :head_size]
    values = lifted[..., head_size:]
    grouped_heads = query.reshape(new_count, groups, -1, head_size)
    scores = jnp.einsum(
        "nghd,tgd->nght", grouped_heads, keys, preferred_element_type=F32
    ) * head_size ** (-0.5)
    top = lax.pmax(jnp.max(scores, axis=-1), "seq")
    expo = jnp.exp(scores - top[..., None])
    total = jnp.sum(expo, axis=-1)
    summed = jnp.einsum("nght,tgd->nghd", expo.astype(BF16), values, preferred_element_type=F32)
    summed, total = lax.psum((summed, total), "seq")
    attended = (summed / total[..., None]).astype(BF16).reshape(new_count, -1)
    attended = route(attended, index, orders, True)
    return lax.psum(dot(attended, w_out), "tensor").astype(BF16)[None]


def solution(mesh):
    placed = (
        P("rep", ("seq", "tensor"), None, None),
        P("rep", None, "tensor", None),
        P(),
        P(),
        P("tensor", None, None),
        P("tensor", "seq"),
        P(),
    )
    square = all(mesh.shape[axis] == size for axis, size in (("seq", 2), ("rep", 4), ("tensor", 4)))
    return jax.shard_map(
        square_shards if square else shards,
        mesh=mesh,
        in_specs=placed,
        out_specs=P("rep", None, "seq"),
        check_vma=False,
    )
```
